32 devices in a mesh: groups: 2 (over y), gx: 4 (over x, core), gy: 4 (over z).
Axes of the slice: x: 2, y: 2, z: 4, core: 2. Of those that a mesh axis runs over, the one named last changes fastest.
Arguments:
- cell_index: int32 [32, 32768], P(('groups', 'gx', 'gy')), parts along dimension 0, may hold values from 0 to 32767, each once within a row
- offset_code: int32 [32, 32768], P(('groups', 'gx', 'gy')), parts along dimension 0, may hold values from 0 to 63
- particle_state: float32 [32, 12, 32768], P(('groups', 'gx', 'gy')), parts along dimension 0, may hold values from -6 to 6
- fluid_flags: int32 [128, 32, 256], P(('groups', 'gx'), 'gy'), parts along dimension 0, may hold values 0 or 1
Outputs:
- pressure: float32 [128, 32, 256], P(('groups', 'gx'), 'gy'), parts along dimension 0
- new_velocity: float32 [32, 3, 32768], P(('groups', 'gx', 'gy')), parts along dimension 0
The draws below stay inside these ranges and needn't reach their ends.
There are 2 independent parts, one for each index of `groups`. The reference program is written for one: setup_inputs(seed, part) draws one part's arguments, and reference() takes and returns one part's arrays. A program takes and returns all parts, laid end to end along the dimension named above; each array names one. Nothing has to cross between parts.
Inputs may be any that keep to these rules, and one draw needn't show every extreme that they name: `cell_index`: each row of a brick lists every cell of the brick exactly once.
All inputs are finite; a program needn't handle non-finite values. No bound on the sum of `fluid_flags` on one device may be relied on, other than what follows from the above.
Results may differ from the reference program's by a relative error of at most 0.0001.
Values sent between devices are 32-bit elements; how exact they have to be, the bound alone decides.
No kernel may reach another device: no remote copies, remote signals or barrier semaphores. Data moves between devices by JAX's collectives and lax.ppermute only.
A program may use at most 128 MiB of HBM per device.

```python
import jax
import jax.numpy as jnp
from jax import lax

CX = 16
CY = 8
NZ = 256
ITERS = 3
CELLS_DEV = 32768
BRICKS = 16
NX = 64
NY = 32
N_GY = 4


def plant(drawn, stream_key, least, top_value):
    extent = drawn.shape
    place = [jax.random.randint(jax.random.fold_in(stream_key, axis), (), 0, extent[axis]) for axis in range(len(extent))]
    drawn = drawn.at[tuple(place)].set(least)
    longest = extent.index(max(extent))
    place[longest] = (place[longest] + 1) % extent[longest]
    return drawn.at[tuple(place)].set(top_value)


def block_scale(key, extent, cuts, smallest, top_value):
    def one(position, parts):
        heights = jax.random.uniform(jax.random.fold_in(jax.random.fold_in(key, 6), position), (parts,), jnp.float32, smallest / len(cuts), top_value / len(cuts))
        return jnp.repeat(jnp.exp(heights), extent[position] // parts).reshape((-1,) + (1,) * (len(extent) - position - 1))

    loudness = one(*cuts[0])
    for cut in cuts[1:]:
        loudness = loudness * one(*cut)
    return loudness


def normal_values(key, dims, scale, limit, cuts=(), kind=jnp.bfloat16):
    entries = jax.random.normal(key, dims, jnp.float32) * scale
    if len(cuts) > 0:
        entries = block_scale(key, dims, cuts, -0.22, 0.18) * entries
    return jnp.clip(entries, min=-limit, max=limit).astype(kind)


def setup_inputs(seed: int = 0, part: int = 0) -> dict:
    keys = jax.random.split(jax.random.key(seed), 5)
    part_keys = jax.random.split(jax.random.fold_in(keys[4], part), 5)
    return {
        "cell_index": jax.vmap(lambda own: jax.random.permutation(own, CELLS_DEV))(jax.random.split(part_keys[0], BRICKS)).reshape((BRICKS, CELLS_DEV)).astype(jnp.int32),
        "offset_code": plant(jax.random.randint(part_keys[1], (BRICKS, CELLS_DEV), 0, 64), jax.random.fold_in(part_keys[1], 1), 0, 63).astype(jnp.int32),
        "particle_state": normal_values(part_keys[2], (BRICKS, 12, CELLS_DEV), 1.0, 6.0, ((0, 16),), jnp.float32),
        "fluid_flags": plant((jax.random.randint(part_keys[3], (NX, NY, NZ), 0, 8) < 7).astype(jnp.int32), jax.random.fold_in(part_keys[3], 1), 0, 1),
    }


CORNERS = [(0, 0, 0), (0, 0, 1), (0, 1, 0), (0, 1, 1), (1, 0, 0), (1, 0, 1), (1, 1, 0), (1, 1, 1)]


def ahead(field, axis):
    widths = [(0, 0)] * field.ndim
    widths[axis] = (0, 1)
    return lax.slice_in_dim(jnp.pad(field, widths), 1, field.shape[axis] + 1, axis=axis)


def behind(field, axis):
    widths = [(0, 0)] * field.ndim
    widths[axis] = (1, 0)
    return lax.slice_in_dim(jnp.pad(field, widths), 0, field.shape[axis], axis=axis)


def fractions(offset_code):
    frac_x = ((offset_code % 4).astype(jnp.float32) + 0.5) * 0.25
    frac_y = (((offset_code // 4) % 4).astype(jnp.float32) + 0.5) * 0.25
    frac_z = ((offset_code // 16).astype(jnp.float32) + 0.5) * 0.25
    return frac_x, frac_y, frac_z


def corner_terms(state, frac_x, frac_y, frac_z, corner):
    step_x, step_y, step_z = corner
    weight_x = frac_x if step_x else 1.0 - frac_x
    weight_y = frac_y if step_y else 1.0 - frac_y
    weight_z = frac_z if step_z else 1.0 - frac_z
    weight = weight_x * weight_y * weight_z
    delta_x = step_x - frac_x
    delta_y = step_y - frac_y
    delta_z = step_z - frac_z
    moments = [weight * (state[comp] + state[3 + 3 * comp] * delta_x + state[4 + 3 * comp] * delta_y + state[5 + 3 * comp] * delta_z) for comp in range(3)]
    return weight, jnp.stack([weight] + moments)


def operate(field, fluid):
    masked = fluid * field
    beside = ahead(masked, 0) + behind(masked, 0) + ahead(masked, 1) + behind(masked, 1) + ahead(masked, 2) + behind(masked, 2)
    return fluid * (6.0 * field - beside) + (1.0 - fluid) * field


def reference(cell_index, offset_code, particle_state, fluid_flags):
    bricks = cell_index.shape[0]
    brick_ids = jnp.arange(bricks, dtype=jnp.int32)
    brick_x = (brick_ids // N_GY)[:, None]
    brick_y = (brick_ids % N_GY)[:, None]
    cell_x = cell_index // (CY * NZ) + brick_x * CX
    cell_y = (cell_index // NZ) % CY + brick_y * CY
    cell_z = cell_index % NZ
    frac_x, frac_y, frac_z = fractions(offset_code)
    state = jnp.moveaxis(particle_state, 1, 0)
    grid = jnp.zeros((4, NX + 1, NY + 1, NZ + 1), jnp.float32)
    for corner in CORNERS:
        weight, terms = corner_terms(state, frac_x, frac_y, frac_z, corner)
        grid = grid.at[:, cell_x + corner[0], cell_y + corner[1], cell_z + corner[2]].add(terms)
    grid = grid[:, :NX, :NY, :NZ]
    velocity = grid[1:] / jnp.maximum(grid[0], 0.5)
    fluid = fluid_flags.astype(jnp.float32)
    divergence = 0.5 * (ahead(velocity[0], 0) - behind(velocity[0], 0)) + 0.5 * (ahead(velocity[1], 1) - behind(velocity[1], 1)) + 0.5 * (ahead(velocity[2], 2) - behind(velocity[2], 2))
    rhs = -fluid * divergence
    inv_diag = 1.0 / (6.0 * fluid + (1.0 - fluid))
    pressure = jnp.zeros_like(rhs)
    residual = rhs
    precond = residual * inv_diag
    direction = precond
    norm_now = jnp.sum(residual * precond)
    for step in range(ITERS):
        image = operate(direction, fluid)
        alpha = norm_now / jnp.sum(direction * image)
        pressure = pressure + alpha * direction
        residual = residual - alpha * image
        if step + 1 < ITERS:
            precond = residual * inv_diag
            norm_next = jnp.sum(residual * precond)
            direction = precond + (norm_next / norm_now) * direction
            norm_now = norm_next
    projected = jnp.stack([fluid * (velocity[comp] - 0.5 * (ahead(pressure, comp) - behind(pressure, comp))) for comp in range(3)])
    padded = jnp.pad(projected, ((0, 0), (0, 1), (0, 1), (0, 1)))
    result = jnp.zeros((3,) + cell_index.shape, jnp.float32)
    for corner in CORNERS:
        weight, terms = corner_terms(state, frac_x, frac_y, frac_z, corner)
        result = result + weight * padded[:, cell_x + corner[0], cell_y + corner[1], cell_z + corner[2]]
    return pressure, jnp.moveaxis(result, 0, 1)
```

```python
import functools

import jax
import jax.numpy as jnp
from jax import lax
from jax.experimental import pallas as pl
from jax.experimental.pallas import tpu as pltpu
from jax.sharding import PartitionSpec as P

F32, I32 = jnp.float32, jnp.int32
CX, CY, CELLS = 16, 8, 32768
TILES = CELLS // 1024
LANE_RUNS, SUB_RUNS, SWAPS = 9, 8, 15 * 16
VMEM = 48 * 2**20


def take(x, index, axis):
    other = tuple(d for d in range(x.ndim) if d != axis)
    dims = lax.GatherDimensionNumbers(
        offset_dims=(),
        collapsed_slice_dims=(axis,),
        start_index_map=(axis,),
        operand_batching_dims=other,
        start_indices_batching_dims=other,
    )
    return lax.gather(
        x, index[..., None], dims, (1,) * x.ndim, mode=lax.GatherScatterMode.PROMISE_IN_BOUNDS
    )


def iota(shape, dim):
    return lax.broadcasted_iota(I32, shape, dim)


def sort_plan(key, lane_ref, sub_ref, swap_ref):
    lanes, subs = iota((64, 128), 1), iota((8, 128), 0)
    zero = jnp.zeros((8, 128), I32)

    def flip(phase, tile):
        if phase < 7:
            return jnp.where(iota((8, 128), 1) & (1 << phase) != 0, 0x7FFF, zero)
        if phase < 10:
            return jnp.where(subs & (1 << (phase - 7)) != 0, 0x7FFF, zero)
        if phase < 15 and tile >> (phase - 10) & 1:
            return zero + 0x7FFF
        return zero

    def lane_steps(groups, top):
        stride = top
        while stride:
            low = lanes & stride == 0
            other = [take(g, lanes ^ stride, 1) for g in groups]
            groups = [
                jnp.where(low, jnp.minimum(g, o), jnp.maximum(g, o)) for g, o in zip(groups, other)
            ]
            stride //= 2
        return groups

    def grouped(tiles):
        return [jnp.concatenate(tiles[8 * i : 8 * i + 8], axis=0) for i in range(4)]

    def lane_run(run, tiles, phases):
        groups = [(g << 7) | lanes for g in grouped(tiles)]
        for phase in phases:
            if len(phases) > 1:
                turn = jnp.concatenate([flip(phase, 0) << 7] * 8, axis=0)
                groups = [g ^ turn for g in groups]
            groups = lane_steps(groups, 1 << min(phase - 1, 6))
            if len(phases) > 1:
                groups = [g ^ turn for g in groups]
        for i, g in enumerate(groups):
            lane_ref[run, 64 * i : 64 * i + 64] = g & 127
        return [groups[i // 8][8 * (i % 8) : 8 * (i % 8) + 8] >> 7 for i in range(TILES)]

    def sub_run(run, tiles, top):
        tiles = [(t << 3) | subs for t in tiles]
        stride = top
        while stride:
            low = subs & stride == 0
            other = [take(t, subs ^ stride, 0) for t in tiles]
            tiles = [jnp.where(low, jnp.minimum(t, o), jnp.maximum(t, o)) for t, o in zip(tiles, other)]
            stride //= 2
        for i, t in enumerate(tiles):
            sub_ref[run, 8 * i : 8 * i + 8] = t & 7
        return [t >> 3 for t in tiles]

    odd = jnp.where(subs & 1 != 0, 0x7FFF, zero)
    tiles = lane_run(0, key, range(1, 7))
    tiles = [t ^ odd for t in tiles]
    first = [lane_ref[0, 8 * i : 8 * i + 8] for i in range(TILES)]
    groups = [(g << 7) | f for g, f in zip(grouped(tiles), grouped(first))]
    groups = lane_steps(groups, 64)
    for i, g in enumerate(groups):
        lane_ref[0, 64 * i : 64 * i + 64] = g & 127
    tiles = [(groups[i // 8][8 * (i % 8) : 8 * (i % 8) + 8] >> 7) ^ odd for i in range(TILES)]

    swap = 0
    for phase in range(8, 16):
        turns = [flip(phase, i) for i in range(TILES)]
        tiles = [t ^ f for t, f in zip(tiles, turns)]
        stride = 1 << (phase - 1)
        while stride >= 1024:
            hop = stride // 1024
            for i in range(TILES):
                if i & hop == 0:
                    a, b = tiles[i], tiles[i + hop]
                    swap_ref[8 * swap : 8 * swap + 8] = jnp.where(a > b, 1, zero)
                    swap += 1
                    tiles[i], tiles[i + hop] = jnp.minimum(a, b), jnp.maximum(a, b)
            stride //= 2
        tiles = sub_run(phase - 8, tiles, min(stride, 512) // 128)
        tiles = lane_run(phase - 7, tiles, [phase])
        tiles = [t ^ f for t, f in zip(tiles, turns)]
    return tiles


def follow_plan(tiles, lane_ref, sub_ref, swap_ref):
    tiles = [take(t, lane_ref[0, 8 * i : 8 * i + 8], 1) for i, t in enumerate(tiles)]
    swap = 0
    for phase in range(8, 16):
        stride = 1 << (phase - 1)
        while stride >= 1024:
            hop = stride // 1024
            for i in range(TILES):
                if i & hop == 0:
                    a, b = tiles[i], tiles[i + hop]
                    crossed = swap_ref[8 * swap : 8 * swap + 8] != 0
                    swap += 1
                    tiles[i], tiles[i + hop] = jnp.where(crossed, b, a), jnp.where(crossed, a, b)
            stride //= 2
        tiles = [take(t, sub_ref[phase - 8, 8 * i : 8 * i + 8], 0) for i, t in enumerate(tiles)]
        tiles = [take(t, lane_ref[phase - 7, 8 * i : 8 * i + 8], 1) for i, t in enumerate(tiles)]
    return tiles


def plan_scratch():
    return [
        pltpu.VMEM((LANE_RUNS, CELLS // 128, 128), I32),
        pltpu.VMEM((SUB_RUNS, CELLS // 128, 128), I32),
        pltpu.VMEM((8 * SWAPS, 128), I32),
    ]


def split_tiles(array):
    return [array[8 * i : 8 * i + 8] for i in range(TILES)]


def to_cells_kernel(cell_ref, code_ref, state_ref, cells_ref, tag_ref, rows, lane_ref, sub_ref, swap_ref):
    def unpack(t, carry):
        low = pl.multiple_of(t * 128, 128)
        at = pl.multiple_of(t * 8, 8)
        rows[0, pl.ds(at, 8), :] = state_ref[0, 0:8, pl.ds(low, 128)]
        rows[1, pl.ds(at, 4), :] = state_ref[0, 8:12, pl.ds(low, 128)]
        return carry

    lax.fori_loop(0, CELLS // 128, unpack, 0, unroll=8)
    cell = cell_ref[...]
    key = (cell & ~0x780) | ((cell & 0x80) << 3) | ((cell & 0x700) >> 1)
    sort_plan(split_tiles(key), lane_ref, sub_ref, swap_ref)
    tag = (code_ref[...] << 15) | (iota((256, 128), 0) * 128 + iota((256, 128), 1))
    for i, t in enumerate(follow_plan(split_tiles(tag), lane_ref, sub_ref, swap_ref)):
        tag_ref[8 * i : 8 * i + 8] = t

    def move(c, carry):
        half, place = c >> 3, c & 7
        tiles = [rows[half, pl.ds(place + 64 * i, 8, stride=8), :] for i in range(TILES)]
        for i, t in enumerate(follow_plan(tiles, lane_ref, sub_ref, swap_ref)):
            cells_ref[c, 8 * i : 8 * i + 8] = t
        return carry

    lax.fori_loop(0, 12, move, 0)


def to_cells(cell, code, state):
    return pl.pallas_call(
        to_cells_kernel,
        out_shape=(
            jax.ShapeDtypeStruct((12, 256, 128), F32),
            jax.ShapeDtypeStruct((256, 128), I32),
        ),
        scratch_shapes=[pltpu.VMEM((2, 2048, 128), F32)] + plan_scratch(),
        compiler_params=pltpu.CompilerParams(vmem_limit_bytes=VMEM),
        name="to_cells",
    )(cell, code, state)


def to_particles_kernel(tag_ref, value_ref, out_ref, rows, lane_ref, sub_ref, swap_ref):
    sort_plan(split_tiles(tag_ref[...] & 0x7FFF), lane_ref, sub_ref, swap_ref)

    def move(c, carry):
        tiles = [value_ref[c, 8 * i : 8 * i + 8] for i in range(TILES)]
        for i, t in enumerate(follow_plan(tiles, lane_ref, sub_ref, swap_ref)):
            rows[pl.ds(c + 64 * i, 8, stride=8), :] = t
        return carry

    lax.fori_loop(0, 3, move, 0)

    def pack(t, carry):
        low = pl.multiple_of(t * 128, 128)
        at = pl.multiple_of(t * 8, 8)
        out_ref[0, :, pl.ds(low, 128)] = rows[pl.ds(at, 3), :]
        return carry

    lax.fori_loop(0, CELLS // 128, pack, 0, unroll=8)


def to_particles(tag, values):
    return pl.pallas_call(
        to_particles_kernel,
        out_shape=jax.ShapeDtypeStruct((1, 3, CELLS), F32),
        scratch_shapes=[pltpu.VMEM((2048, 128), F32)] + plan_scratch(),
        compiler_params=pltpu.CompilerParams(vmem_limit_bytes=VMEM),
        name="to_particles",
    )(tag, values)


ITERS = 3


CORNERS = [(0, 0, 0), (0, 0, 1), (0, 1, 0), (0, 1, 1), (1, 0, 0), (1, 0, 1), (1, 1, 0), (1, 1, 1)]


def padded_2(block, sides, width):
    for axis, dim in sides:
        count = lax.axis_size(axis)
        forward = [(i, i + 1) for i in range(count - 1)]
        backward = [(target, source) for source, target in forward]
        low = lax.ppermute(
            lax.slice_in_dim(block, block.shape[dim] - width, None, axis=dim), axis, forward
        )
        high = lax.ppermute(lax.slice_in_dim(block, 0, width, axis=dim), axis, backward)
        block = jnp.concatenate([low, block, high], axis=dim)
    return block


def shifted(value, axis, steps):
    count = lax.axis_size(axis)
    leading, last = (max(0, -steps), min(count, count - steps))
    return lax.ppermute(value, axis, [(source, source + steps) for source in range(leading, last)])


def ahead(field, axis):
    widths = [(0, 0)] * field.ndim
    widths[axis] = (0, 1)
    return lax.slice_in_dim(jnp.pad(field, widths), 1, field.shape[axis] + 1, axis=axis)


def behind(field, axis):
    widths = [(0, 0)] * field.ndim
    widths[axis] = (1, 0)
    return lax.slice_in_dim(jnp.pad(field, widths), 0, field.shape[axis], axis=axis)


def fractions(offset_code):
    frac_x = ((offset_code % 4).astype(jnp.float32) + 0.5) * 0.25
    frac_y = ((offset_code // 4 % 4).astype(jnp.float32) + 0.5) * 0.25
    frac_z = ((offset_code // 16).astype(jnp.float32) + 0.5) * 0.25
    return (frac_x, frac_y, frac_z)


def corner_terms(state, frac_x, frac_y, frac_z, corner):
    step_x, step_y, step_z = corner
    weight_x = frac_x if step_x else 1.0 - frac_x
    weight_y = frac_y if step_y else 1.0 - frac_y
    weight_z = frac_z if step_z else 1.0 - frac_z
    weight = weight_x * weight_y * weight_z
    delta_x = step_x - frac_x
    delta_y = step_y - frac_y
    delta_z = step_z - frac_z
    moments = [
        weight
        * (
            state[comp]
            + state[3 + 3 * comp] * delta_x
            + state[4 + 3 * comp] * delta_y
            + state[5 + 3 * comp] * delta_z
        )
        for comp in range(3)
    ]
    return (weight, jnp.stack([weight] + moments))


def operate(field, fluid):
    masked = fluid * field
    padded = padded_2(masked, (("gx", 0), ("gy", 1)), 1)
    beside = (
        padded[2:, 1:-1]
        + padded[:-2, 1:-1]
        + padded[1:-1, 2:]
        + padded[1:-1, :-2]
        + ahead(masked, 2)
        + behind(masked, 2)
    )
    return fluid * (6.0 * field - beside) + (1.0 - fluid) * field


def precond_total(residual, precond):
    return lax.psum(jnp.sum(residual * precond), ("gx", "gy"))


def local(cell_index, offset_code, particle_state, fluid_flags):
    width_x, width_y, depth = fluid_flags.shape
    shape_cells = (width_x, width_y, depth)
    moved, tag = to_cells(
        cell_index.reshape(256, 128), offset_code.reshape(256, 128), particle_state
    )

    def unfold(tiles):
        return jnp.moveaxis(tiles.reshape(tiles.shape[:-2] + (CX, 2, CY, 128)), -3, -2).reshape(
            tiles.shape[:-2] + shape_cells
        )

    state_cells = unfold(moved)
    code_cells = unfold(tag) >> 15
    frac_x, frac_y, frac_z = fractions(code_cells)
    grid = jnp.zeros((4, width_x + 1, width_y + 1, depth + 1), jnp.float32)
    weights = []
    for corner in CORNERS:
        weight, terms = corner_terms(state_cells, frac_x, frac_y, frac_z, corner)
        weights.append(weight)
        grid = grid + jnp.pad(
            terms,
            (
                (0, 0),
                (corner[0], 1 - corner[0]),
                (corner[1], 1 - corner[1]),
                (corner[2], 1 - corner[2]),
            ),
        )
    arrived_x = shifted(grid[:, width_x], "gx", 1)
    grid = grid[:, :width_x].at[:, 0].add(arrived_x)
    arrived_y = shifted(grid[:, :, width_y], "gy", 1)
    grid = grid[:, :, :width_y].at[:, :, 0].add(arrived_y)
    grid = grid[..., :depth]
    velocity = grid[1:] / jnp.maximum(grid[0], 0.5)
    fluid = fluid_flags.astype(jnp.float32)
    framed = padded_2(velocity, (("gx", 1), ("gy", 2)), 1)
    divergence = (
        0.5 * (framed[0, 2:, 1:-1] - framed[0, :-2, 1:-1])
        + 0.5 * (framed[1, 1:-1, 2:] - framed[1, 1:-1, :-2])
        + 0.5 * (ahead(velocity[2], 2) - behind(velocity[2], 2))
    )
    rhs = -fluid * divergence
    inv_diag = 1.0 / (6.0 * fluid + (1.0 - fluid))
    pressure = jnp.zeros_like(rhs)
    residual = rhs
    precond = residual * inv_diag
    direction = precond
    norm_now = precond_total(residual, precond)
    for step in range(ITERS):
        image = operate(direction, fluid)
        alpha = norm_now / lax.psum(jnp.sum(direction * image), ("gx", "gy"))
        pressure = pressure + alpha * direction
        residual = residual - alpha * image
        if step + 1 < ITERS:
            precond = residual * inv_diag
            norm_next = precond_total(residual, precond)
            direction = precond + norm_next / norm_now * direction
            norm_now = norm_next
    framed_p = padded_2(pressure, (("gx", 0), ("gy", 1)), 1)
    slope_x = framed_p[2:, 1:-1] - framed_p[:-2, 1:-1]
    slope_y = framed_p[1:-1, 2:] - framed_p[1:-1, :-2]
    slope_z = ahead(pressure, 2) - behind(pressure, 2)
    projected = jnp.stack(
        [
            fluid * (velocity[0] - 0.5 * slope_x),
            fluid * (velocity[1] - 0.5 * slope_y),
            fluid * (velocity[2] - 0.5 * slope_z),
        ]
    )
    upper_x = shifted(projected[:, 0:1], "gx", -1)
    extended = jnp.concatenate([projected, upper_x], axis=1)
    upper_y = shifted(extended[:, :, 0:1], "gy", -1)
    extended = jnp.concatenate([extended, upper_y], axis=2)
    extended = jnp.concatenate(
        [extended, jnp.zeros(extended.shape[:3] + (1,), jnp.float32)], axis=3
    )
    result_cells = jnp.zeros((3,) + shape_cells, jnp.float32)
    for corner, weight in zip(CORNERS, weights):
        window = extended[
            :,
            corner[0] : corner[0] + width_x,
            corner[1] : corner[1] + width_y,
            corner[2] : corner[2] + depth,
        ]
        result_cells = result_cells + weight * window
    folded = jnp.moveaxis(result_cells.reshape(3, CX, CY, 2, 128), 3, 2).reshape(3, 256, 128)
    return (pressure, to_particles(tag, folded))


def solution(mesh):
    return jax.shard_map(
        local,
        mesh=mesh,
        in_specs=(
            P(("groups", "gx", "gy"), None),
            P(("groups", "gx", "gy"), None),
            P(("groups", "gx", "gy"), None, None),
            P(("groups", "gx"), "gy", None),
        ),
        out_specs=(P(("groups", "gx"), "gy", None), P(("groups", "gx", "gy"), None, None)),
        check_vma=False,
    )
```

```python
import functools

import jax
import jax.numpy as jnp
from jax import lax
from jax.experimental import pallas as pl
from jax.experimental.pallas import tpu as pltpu
from jax.sharding import PartitionSpec as P

F32, I32 = jnp.float32, jnp.int32
CX, CY, CELLS = 16, 8, 32768
TILES = CELLS // 1024
LANE_RUNS, SUB_RUNS, SWAPS = 9, 3, 30 * 16
VMEM = 48 * 2**20


def take(x, index, axis):
    other = tuple(d for d in range(x.ndim) if d != axis)
    dims = lax.GatherDimensionNumbers(
        offset_dims=(),
        collapsed_slice_dims=(axis,),
        start_index_map=(axis,),
        operand_batching_dims=other,
        start_indices_batching_dims=other,
    )
    return lax.gather(
        x, index[..., None], dims, (1,) * x.ndim, mode=lax.GatherScatterMode.PROMISE_IN_BOUNDS
    )


def iota(shape, dim):
    return lax.broadcasted_iota(I32, shape, dim)


def sort_plan(tiles, lane_ref, sub_ref, swap_ref):
    lanes, subs = iota((64, 128), 1), iota((8, 128), 0)
    top = 0x7FFF

    def grouped(tiles):
        return [jnp.concatenate(tiles[8 * i : 8 * i + 8], axis=0) for i in range(4)]

    def lane_steps(groups, stride):
        while stride:
            low = lanes & stride == 0
            other = [take(g, lanes ^ stride, 1) for g in groups]
            groups = [
                jnp.where(low, jnp.minimum(g, o), jnp.maximum(g, o)) for g, o in zip(groups, other)
            ]
            stride //= 2
        return groups

    def record(run, groups):
        for i, g in enumerate(groups):
            lane_ref[run, 64 * i : 64 * i + 64] = g & 127
        return [groups[i // 8][8 * (i % 8) : 8 * (i % 8) + 8] >> 7 for i in range(TILES)]

    groups = [(g << 7) | lanes for g in grouped(tiles)]
    for phase in range(1, 7):
        turn = jnp.where(lanes & (1 << phase) != 0, top << 7, 0)
        groups = [g ^ turn for g in groups]
        groups = lane_steps(groups, 1 << (phase - 1))
        groups = [g ^ turn for g in groups]
    turn = jnp.where(iota((64, 128), 0) & 8 != 0, top << 7, 0)
    groups = lane_steps([g ^ turn for g in groups], 64)
    tiles = record(0, groups)
    tiles = [t ^ top if i & 1 else t for i, t in enumerate(tiles)]

    swap = 0
    for phase in range(8, 16):
        if phase < 12:
            turns = [top if i >> (phase - 7) & 1 else 0 for i in range(TILES)]
        elif phase < 15:
            turns = [jnp.where(subs & (1 << (phase - 12)) != 0, top, 0)] * TILES
        else:
            turns = [0] * TILES
        tiles = [t ^ f for t, f in zip(tiles, turns)]
        if phase > 12:
            tiles = [(t << 3) | subs for t in tiles]
            stride = 1 << (phase - 13)
            while stride:
                low = subs & stride == 0
                other = [take(t, subs ^ stride, 0) for t in tiles]
                tiles = [
                    jnp.where(low, jnp.minimum(t, o), jnp.maximum(t, o)) for t, o in zip(tiles, other)
                ]
                stride //= 2
            for i, t in enumerate(tiles):
                sub_ref[phase - 13, 8 * i : 8 * i + 8] = t & 7
            tiles = [t >> 3 for t in tiles]
        hop = 1 << (min(phase, 12) - 8)
        while hop:
            for i in range(TILES):
                if i & hop == 0:
                    a, b = tiles[i], tiles[i + hop]
                    swap_ref[8 * swap : 8 * swap + 8] = jnp.where(a > b, 1, 0)
                    swap += 1
                    tiles[i], tiles[i + hop] = jnp.minimum(a, b), jnp.maximum(a, b)
            hop //= 2
        groups = [(g << 7) | lanes for g in grouped(tiles)]
        tiles = record(phase - 7, lane_steps(groups, 64))
        tiles = [t ^ f for t, f in zip(tiles, turns)]
    return tiles


def follow_plan(tiles, lane_ref, sub_ref, swap_ref):
    tiles = [take(t, lane_ref[0, 8 * i : 8 * i + 8], 1) for i, t in enumerate(tiles)]
    swap = 0
    for phase in range(8, 16):
        if phase > 12:
            tiles = [take(t, sub_ref[phase - 13, 8 * i : 8 * i + 8], 0) for i, t in enumerate(tiles)]
        hop = 1 << (min(phase, 12) - 8)
        while hop:
            for i in range(TILES):
                if i & hop == 0:
                    a, b = tiles[i], tiles[i + hop]
                    crossed = swap_ref[8 * swap : 8 * swap + 8] != 0
                    swap += 1
                    tiles[i], tiles[i + hop] = jnp.where(crossed, b, a), jnp.where(crossed, a, b)
            hop //= 2
        tiles = [take(t, lane_ref[phase - 7, 8 * i : 8 * i + 8], 1) for i, t in enumerate(tiles)]
    return tiles


def plan_shapes():
    return [(LANE_RUNS, 256, 128), (SUB_RUNS, 256, 128), (8 * SWAPS, 128)]


def plan_scratch():
    return [pltpu.VMEM(shape, I32) for shape in plan_shapes()]


def split_tiles(array):
    return [array[8 * i : 8 * i + 8] for i in range(TILES)]


def z_behind(a):
    r = pltpu.roll(a, 1, 2)
    fill = jnp.concatenate([jnp.zeros_like(r[:1]), r[:1]], axis=0)
    return jnp.where(iota(a.shape, 2) == 0, fill, r)


def z_ahead(a):
    r = pltpu.roll(a, 127, 2)
    fill = jnp.concatenate([r[1:], jnp.zeros_like(r[:1])], axis=0)
    return jnp.where(iota(a.shape, 2) == 127, fill, r)


def y_shift(a, steps):
    return jnp.stack([pltpu.roll(a[h], steps % a.shape[1], 0) for h in range(2)])


def fractions(code):
    return [((code >> shift & 3).astype(F32) + 0.5) * 0.25 for shift in (0, 2, 4)]


Y_UP = ((0, 4, 5), (1, 5, 4), (2, 4, 5), (3, 5, 4), (4, 5, 3))
Y_DOWN = ((0, 0, 5), (1, 0, 4), (2, 0, 5), (3, 0, 4), (4, 0, 4))
X_UP = ((0, 12, 5), (1, 12, 5), (2, 13, 4), (3, 13, 4), (4, 13, 3))
X_DOWN = ((0, 0, 5), (1, 0, 5), (2, 0, 4), (3, 0, 4), (4, 0, 4))
UP_ROWS, DOWN_ROWS = 720, 752


def y_pieces(table):
    at, out = 0, []
    for x in range(CX + 1):
        for field, first, count in table:
            if field == 4 and x == CX:
                continue
            for half in range(2):
                out.append((field, x, half, first, count, at))
                at += count
    return out


def x_pieces(table):
    at, out = 0, []
    for field, first, count in table:
        for plane in range(first, first + count):
            for half in range(2):
                out.append((field, plane, half, at))
                at += 17
    return out


def deposit_kernel(
    cell_ref, code_ref, state_ref, flag_ref, grid_ref, up_ref, down_ref, tag_ref, cells, lane_ref, sub_ref, swap_ref
):
    cell = cell_ref[...]
    key = ((cell & 0x700) << 4) | ((cell & 0x7800) >> 3) | (cell & 0xFF)
    sort_plan(split_tiles(key), lane_ref, sub_ref, swap_ref)
    tag = (code_ref[...] << 15) | (iota((256, 128), 0) * 128 + iota((256, 128), 1))
    for i, t in enumerate(follow_plan(split_tiles(tag), lane_ref, sub_ref, swap_ref)):
        tag_ref[8 * i : 8 * i + 8] = t

    def move(c, carry):
        tiles = [state_ref[c, 8 * i : 8 * i + 8] for i in range(TILES)]
        for i, t in enumerate(follow_plan(tiles, lane_ref, sub_ref, swap_ref)):
            cells[c, i] = t
        return carry

    lax.fori_loop(0, 12, move, 0)

    up_at = {(f, x, h): (first, count, at) for f, x, h, first, count, at in y_pieces(Y_UP)}
    down_at = {(f, x, h): (first, count, at) for f, x, h, first, count, at in y_pieces(Y_DOWN)}
    first_row = iota((2, 8, 128), 1) == 0
    before = None
    for x in range(CX + 1):
        here = []
        if x < CX:
            code = jnp.stack([tag_ref[16 * x + 8 * h : 16 * x + 8 * h + 8] >> 15 for h in range(2)])
            fx, fy, fz = fractions(code)
            wx, wy, wz = (1.0 - fx, fx), (1.0 - fy, fy), (1.0 - fz, fz)
            w = {(i, j, k): wx[i] * wy[j] * wz[k] for i in (0, 1) for j in (0, 1) for k in (0, 1)}
            here.append(w)
            for comp in range(3):
                v = cells[comp, 2 * x : 2 * x + 2]
                c0, c1, c2 = [cells[3 + 3 * comp + e, 2 * x : 2 * x + 2] for e in range(3)]
                base = v - c0 * fx - c1 * fy - c2 * fz
                terms = {}
                for i in (0, 1):
                    a = base + c0 if i else base
                    for j in (0, 1):
                        b = a + c1 if j else a
                        for k in (0, 1):
                            terms[i, j, k] = w[i, j, k] * (b + c2 if k else b)
                here.append(terms)
        for f in range(4):
            s = {}
            for j in (0, 1):
                for k in (0, 1):
                    parts = []
                    if x < CX:
                        parts.append(here[f][0, j, k])
                    if x > 0:
                        parts.append(before[f][1, j, k])
                    s[j, k] = sum(parts[1:], parts[0])
            near, far = [s[j, 0] + z_behind(s[j, 1]) for j in (0, 1)]
            turned = y_shift(far, 1)
            main = near + jnp.where(first_row, 0.0, turned)
            grid_ref[f, x] = main
            for h in range(2):
                first, count, at = up_at[f, x, h]
                up_ref[at : at + 8 - first] = main[h, first:8]
                up_ref[at + 8 - first : at + 9 - first] = turned[h, 0:1]
                first, count, at = down_at[f, x, h]
                down_ref[at : at + count] = main[h, :count]
        if x < CX:
            for h in range(2):
                flags = flag_ref[x, :, 128 * h : 128 * h + 128].astype(F32)
                for table, ref in ((up_at, up_ref), (down_at, down_ref)):
                    first, count, at = table[4, x, h]
                    ref[at : at + count] = flags[first : first + count]
        before = here


def kernel_call(body, name, outs, scratch, in_specs=None):
    return pl.pallas_call(
        body,
        out_shape=outs,
        **({} if in_specs is None else dict(in_specs=in_specs)),
        scratch_shapes=scratch,
        compiler_params=pltpu.CompilerParams(vmem_limit_bytes=VMEM),
        name=name,
    )


def of(shape, kind=F32):
    return jax.ShapeDtypeStruct(shape, kind)


def deposit(cell, code, state, flags):
    return kernel_call(
        deposit_kernel,
        "deposit",
        (of((4, CX + 1, 2, 8, 128)), of((UP_ROWS, 128)), of((DOWN_ROWS, 128)), of((256, 128), I32)),
        [pltpu.VMEM((12, TILES, 8, 128), F32)] + plan_scratch(),
    )(cell, code, state, flags)


def widen_kernel(keep_ref, grid_ref, own_ref, low_ref, high_ref, flag_ref, wide_ref, up_ref, down_ref):
    keep = keep_ref[1]
    zero = jnp.zeros((2, 8, 128), F32)
    for f in range(5):
        for x in range(CX + 1):
            wide_ref[f, x, :, 0:8] = zero
            wide_ref[f, x, :, 16:24] = zero
            if f < 4:
                wide_ref[f, x, :, 8:16] = grid_ref[f, x]
            elif x < CX:
                for h in range(2):
                    wide_ref[f, x, h, 8:16] = flag_ref[x, :, 128 * h : 128 * h + 128].astype(F32)
            else:
                wide_ref[f, x, :, 8:16] = zero
    for f, x, h, first, count, at in y_pieces(Y_DOWN):
        wide_ref[f, x, h, 16 : 16 + count] = high_ref[at : at + count]
    for f, x, h, first, count, at in y_pieces(Y_UP):
        below = 8 - first
        wide_ref[f, x, h, first:8] = low_ref[at : at + below]
        if f < 4:
            rim = at + below
            wide_ref[f, x, h, 8:9] = wide_ref[f, x, h, 8:9] + low_ref[rim : rim + 1]
            wide_ref[f, x, h, 16:17] = wide_ref[f, x, h, 16:17] + keep * own_ref[rim : rim + 1]
    for table, ref in ((X_UP, up_ref), (X_DOWN, down_ref)):
        for f, plane, h, at in x_pieces(table):
            ref[at : at + 17] = wide_ref[f, plane, h, 4:21]


def smem():
    return pl.BlockSpec(memory_space=pltpu.SMEM)


def vmem():
    return pl.BlockSpec(memory_space=pltpu.VMEM)


def widen(keep, grid, own, low, high, flags):
    return kernel_call(
        widen_kernel,
        "widen",
        (of((5, CX + 1, 2, 24, 128)), of((UP_ROWS, 128)), of((DOWN_ROWS, 128))),
        [],
        [smem()] + [vmem()] * 5,
    )(keep, grid, own, low, high, flags)


def krylov_kernel(keep_ref, wide_ref, low_ref, high_ref, vel_ref, fluid_ref, k0_ref, k1_ref, k2_ref, sums_ref, ext):
    keep = keep_ref[0]
    zero = jnp.zeros((2, 24, 128), F32)
    for f in range(5):
        for plane in (0, 1, 2, 3, 21, 22, 23, 24):
            ext[f, plane] = zero
        for x in range(CX):
            ext[f, x + 4] = wide_ref[f, x]
        ext[f, 20] = keep * wide_ref[f, CX]
    for f, plane, h, at in x_pieces(X_UP):
        rows = low_ref[at : at + 17]
        if plane == CX:
            ext[f, 4, h, 4:21] = ext[f, 4, h, 4:21] + rows
        else:
            ext[f, plane - 12, h, 4:21] = rows
    for f, plane, h, at in x_pieces(X_DOWN):
        rows = high_ref[at : at + 17]
        if plane == 0 and f < 4:
            ext[f, 20, h, 4:21] = ext[f, 20, h, 4:21] + rows
        else:
            ext[f, plane + 20, h, 4:21] = rows
    for plane in range(25):
        mass = jnp.maximum(ext[0, plane], 0.5)
        for d in range(3):
            vel_ref[d, plane] = ext[1 + d, plane] / mass
        fluid_ref[plane] = ext[4, plane]
    for plane in range(1, 24):
        vy, vz = vel_ref[1, plane], vel_ref[2, plane]
        divergence = (
            0.5 * (vel_ref[0, plane + 1] - vel_ref[0, plane - 1])
            + 0.5 * (y_shift(vy, -1) - y_shift(vy, 1))
            + 0.5 * (z_ahead(vz) - z_behind(vz))
        )
        k0_ref[plane] = -fluid_ref[plane] * divergence

    def applied(ref, plane):
        a = ref[plane]
        beside = (
            ref[plane + 1] + ref[plane - 1] + y_shift(a, 1) + y_shift(a, -1) + z_ahead(a) + z_behind(a)
        )
        return fluid_ref[plane] * (a - beside * (1.0 / 6.0))

    for plane in range(2, 23):
        k1_ref[plane] = applied(k0_ref, plane)
    for plane in range(3, 22):
        k2_ref[plane] = applied(k1_ref, plane)
    totals = [jnp.zeros((2, 8, 128), F32)] * 14
    for plane in range(4, 20):
        k0, k1, k2 = [ref[plane, :, 8:16] for ref in (k0_ref, k1_ref, k2_ref)]
        k3 = applied(k2_ref, plane)[:, 8:16]
        u1, w1 = k0 - k1, k1 - k2
        u2 = u1 - w1
        w2 = w1 - (k2 - k3)
        pairs = (
            (k0, k0), (k0, k1), (k1, k1), (k1, k2), (k2, k2), (k2, k3),
            (k0, u1), (u1, u1), (u1, u2), (u2, u2), (k0, w1), (u1, w1), (u1, w2), (u2, w2),
        )
        totals = [t + a * b for t, (a, b) in zip(totals, pairs)]
    for i, t in enumerate(totals):
        sums_ref[i : i + 1] = jnp.sum(t[0] + t[1], axis=0, keepdims=True)
    sums_ref[14:16] = jnp.zeros((2, 128), F32)


def krylov(keep, wide, low, high):
    return kernel_call(
        krylov_kernel,
        "krylov",
        (of((3, 25, 2, 24, 128)),) + (of((25, 2, 24, 128)),) * 4 + (of((16, 128)),),
        [pltpu.VMEM((5, 25, 2, 24, 128), F32)],
        [smem()] + [vmem()] * 3,
    )(keep, wide, low, high)


def steps_from(gram, energy, apply_once):
    def form(a, table):
        total = None
        for i, p in enumerate(a):
            for j, q in enumerate(a):
                if p is not None and q is not None:
                    term = p * q * table[i + j]
                    total = term if total is None else total + term
        return total

    def ratio(a, b):
        return jnp.where(b > 0.0, a / jnp.where(b > 0.0, b, 1.0), 0.0)

    one, zero = jnp.ones_like(gram[0]), jnp.zeros_like(gram[0])
    residual, direction, answer = [one], [one], [zero] * 3
    norm = gram[0]
    for step in range(3):
        alpha = ratio(norm, form(direction, energy))
        for i, p in enumerate(direction):
            answer[i] = answer[i] + alpha * p
        if step == 2:
            return answer
        image = apply_once(direction, zero)
        residual = [a - alpha * b for a, b in zip(residual + [zero], image)]
        norm_next = form(residual, gram)
        direction = [a + ratio(norm_next, norm) * b for a, b in zip(residual, direction + [zero])]
        norm = norm_next


def coefficients(m):
    power = steps_from(m[0:5], m[1:6], lambda a, zero: [zero] + a)
    shifted = steps_from(
        [m[0]] + m[6:10],
        [m[1]] + m[10:14],
        lambda a, zero: [p - q for p, q in zip(a + [zero], [zero] + a)],
    )
    turned = [shifted[0] + shifted[1] + shifted[2], -shifted[1] - 2.0 * shifted[2], shifted[2]]
    smooth = m[1] < 0.3 * m[0]
    return [jnp.where(smooth, a, b) * (1.0 / 6.0) for a, b in zip(power, turned)]


def plan_kernel(tag_ref, lane_ref, sub_ref, swap_ref):
    place = tag_ref[...] & 0x7FFF
    key = ((place & 0x380) << 5) | ((place & 0x7C00) >> 3) | (place & 0x7F)
    sort_plan(split_tiles(key), lane_ref, sub_ref, swap_ref)


def return_plan(tag):
    return kernel_call(plan_kernel, "return_plan", [of(shape, I32) for shape in plan_shapes()], [])(tag)


def project_kernel(
    sums_ref, vel_ref, fluid_ref, k0_ref, k1_ref, k2_ref, tag_ref, lane_ref, sub_ref, swap_ref,
    pressure_ref, out_ref, press, proj, value,
):
    total = jnp.sum(sums_ref[...].reshape(-1, 16, 128), axis=0)
    total = jnp.sum(total, axis=1, keepdims=True)
    c = coefficients([jnp.broadcast_to(total[i : i + 1], (8, 128)) for i in range(14)])
    c = [jnp.concatenate([a, a, a], axis=0)[None] for a in c]
    for plane in range(3, 22):
        press[plane] = c[0] * k0_ref[plane] + c[1] * k1_ref[plane] + c[2] * k2_ref[plane]
    for x in range(CX):
        for h in range(2):
            pressure_ref[x, :, 128 * h : 128 * h + 128] = press[x + 4, h, 8:16]
    for x in range(CX + 1):
        p = press[x + 4]
        slopes = (
            press[x + 5] - press[x + 3],
            y_shift(p, -1) - y_shift(p, 1),
            z_ahead(p) - z_behind(p),
        )
        for d in range(3):
            field = fluid_ref[x + 4] * (vel_ref[d, x + 4] - 0.5 * slopes[d])
            proj[x, d, 0] = field
            proj[x, d, 1] = z_ahead(field)
    for x in range(CX):
        code = jnp.stack([tag_ref[16 * x + 8 * h : 16 * x + 8 * h + 8] >> 15 for h in range(2)])
        fx, fy, fz = fractions(code)
        wx, wy, wz = (1.0 - fx, fx), (1.0 - fy, fy), (1.0 - fz, fz)
        w = {(i, j, k): wx[i] * wy[j] * wz[k] for i in (0, 1) for j in (0, 1) for k in (0, 1)}
        for d in range(3):
            result = None
            for (i, j, k), weight in w.items():
                term = weight * proj[x + i, d, k, :, 8 + j : 16 + j]
                result = term if result is None else result + term
            value[d, 2 * x : 2 * x + 2] = result

    def move(d, carry):
        tiles = [value[d, i] for i in range(TILES)]
        for i, t in enumerate(follow_plan(tiles, lane_ref, sub_ref, swap_ref)):
            out_ref[d, 8 * i : 8 * i + 8] = t
        return carry

    lax.fori_loop(0, 3, move, 0)


def project(*args):
    return kernel_call(
        project_kernel,
        "project",
        (of((CX, CY, 256)), of((3, 256, 128))),
        [
            pltpu.VMEM((25, 2, 24, 128), F32),
            pltpu.VMEM((CX + 1, 3, 2, 2, 24, 128), F32),
            pltpu.VMEM((3, TILES, 8, 128), F32),
        ],
    )(*args)


def neighbours(up, down, axis):
    pairs = [(i, i + 1) for i in range(lax.axis_size(axis) - 1)]
    return lax.ppermute(up, axis, pairs), lax.ppermute(down, axis, [(b, a) for a, b in pairs])


def everywhere(sums):
    for axis in ("gx", "gy"):
        count = lax.axis_size(axis)
        parts = [sums]
        for shift in range(1, count):
            parts.append(lax.ppermute(sums, axis, [(i, (i + shift) % count) for i in range(count)]))
        sums = functools.reduce(jnp.add, parts)
    return sums


def local(cell_index, offset_code, particle_state, fluid_flags):
    places = [(axis, lax.axis_index(axis), lax.axis_size(axis)) for axis in ("gx", "gy")]
    keep = jnp.stack([(at + 1 < size).astype(F32) for _, at, size in places])
    grid, up, down, tag = deposit(
        cell_index.reshape(256, 128),
        offset_code.reshape(256, 128),
        particle_state.reshape(12, 256, 128),
        fluid_flags,
    )
    low, high = neighbours(up, down, "gy")
    plan = return_plan(tag)
    wide, up_x, down_x = widen(keep, grid, up, low, high, fluid_flags)
    low, high = neighbours(up_x, down_x, "gx")
    vel, fluid, k0, k1, k2, sums = krylov(keep, wide, low, high)
    sums = everywhere(sums)
    pressure, result = project(sums, vel, fluid, k0, k1, k2, tag, *plan)
    return pressure, result.reshape(1, 3, CELLS)


def solution(mesh):
    return jax.shard_map(
        local,
        mesh=mesh,
        in_specs=(
            P(("groups", "gx", "gy"), None),
            P(("groups", "gx", "gy"), None),
            P(("groups", "gx", "gy"), None, None),
            P(("groups", "gx"), "gy", None),
        ),
        out_specs=(P(("groups", "gx"), "gy", None), P(("groups", "gx", "gy"), None, None)),
        check_vma=False,
    )
```

```python
import functools
import math

import jax
import jax.numpy as jnp
from jax import lax
from jax.experimental import pallas as pl
from jax.experimental.pallas import tpu as pltpu
from jax.sharding import PartitionSpec as P

F32, I32 = jnp.float32, jnp.int32
CX, CY, CELLS = 16, 8, 32768
TILES = CELLS // 1024
LANE_RUNS, SUB_RUNS, SWAPS = 9, 3, 30 * 16


def take(x, index, axis):
    other = tuple(d for d in range(x.ndim) if d != axis)
    dims = lax.GatherDimensionNumbers(
        offset_dims=(),
        collapsed_slice_dims=(axis,),
        start_index_map=(axis,),
        operand_batching_dims=other,
        start_indices_batching_dims=other,
    )
    return lax.gather(
        x, index[..., None], dims, (1,) * x.ndim, mode=lax.GatherScatterMode.PROMISE_IN_BOUNDS
    )


def iota(shape, dim):
    return lax.broadcasted_iota(I32, shape, dim)


def sort_plan(tiles, lane_ref, sub_ref, swap_ref):
    lanes, subs = iota((64, 128), 1), iota((8, 128), 0)
    top = 0x7FFF

    def grouped(tiles):
        return [jnp.concatenate(tiles[8 * i : 8 * i + 8], axis=0) for i in range(4)]

    def lane_steps(groups, stride):
        while stride:
            low = lanes & stride == 0
            other = [take(g, lanes ^ stride, 1) for g in groups]
            groups = [
                jnp.where(low, jnp.minimum(g, o), jnp.maximum(g, o)) for g, o in zip(groups, other)
            ]
            stride //= 2
        return groups

    def record(run, groups):
        for i, g in enumerate(groups):
            lane_ref[run, 64 * i : 64 * i + 64] = g & 127
        return [groups[i // 8][8 * (i % 8) : 8 * (i % 8) + 8] >> 7 for i in range(TILES)]

    groups = [(g << 7) | lanes for g in grouped(tiles)]
    for phase in range(1, 7):
        turn = jnp.where(lanes & (1 << phase) != 0, top << 7, 0)
        groups = [g ^ turn for g in groups]
        groups = lane_steps(groups, 1 << (phase - 1))
        groups = [g ^ turn for g in groups]
    turn = jnp.where(iota((64, 128), 0) & 8 != 0, top << 7, 0)
    groups = lane_steps([g ^ turn for g in groups], 64)
    tiles = record(0, groups)
    tiles = [t ^ top if i & 1 else t for i, t in enumerate(tiles)]

    swap = 0
    for phase in range(8, 16):
        if phase < 12:
            turns = [top if i >> (phase - 7) & 1 else 0 for i in range(TILES)]
        elif phase < 15:
            turns = [jnp.where(subs & (1 << (phase - 12)) != 0, top, 0)] * TILES
        else:
            turns = [0] * TILES
        tiles = [t ^ f for t, f in zip(tiles, turns)]
        if phase > 12:
            tiles = [(t << 3) | subs for t in tiles]
            stride = 1 << (phase - 13)
            while stride:
                low = subs & stride == 0
                other = [take(t, subs ^ stride, 0) for t in tiles]
                tiles = [
                    jnp.where(low, jnp.minimum(t, o), jnp.maximum(t, o)) for t, o in zip(tiles, other)
                ]
                stride //= 2
            for i, t in enumerate(tiles):
                sub_ref[phase - 13, 8 * i : 8 * i + 8] = t & 7
            tiles = [t >> 3 for t in tiles]
        hop = 1 << (min(phase, 12) - 8)
        while hop:
            for i in range(TILES):
                if i & hop == 0:
                    a, b = tiles[i], tiles[i + hop]
                    swap_ref[8 * swap : 8 * swap + 8] = jnp.where(a > b, 1, 0)
                    swap += 1
                    tiles[i], tiles[i + hop] = jnp.minimum(a, b), jnp.maximum(a, b)
            hop //= 2
        groups = [(g << 7) | lanes for g in grouped(tiles)]
        tiles = record(phase - 7, lane_steps(groups, 64))
        tiles = [t ^ f for t, f in zip(tiles, turns)]
    return tiles


def follow_plan(channels, lane_ref, sub_ref, swap_ref):
    def gathered(ref, run, axis):
        for i in range(TILES):
            index = ref[run, 8 * i : 8 * i + 8]
            for tiles in channels:
                tiles[i] = take(tiles[i], index, axis)

    gathered(lane_ref, 0, 1)
    swap = 0
    for phase in range(8, 16):
        if phase > 12:
            gathered(sub_ref, phase - 13, 0)
        hop = 1 << (min(phase, 12) - 8)
        while hop:
            for i in range(TILES):
                if i & hop == 0:
                    crossed = swap_ref[8 * swap : 8 * swap + 8] != 0
                    swap += 1
                    for tiles in channels:
                        a, b = tiles[i], tiles[i + hop]
                        tiles[i], tiles[i + hop] = jnp.where(crossed, b, a), jnp.where(crossed, a, b)
            hop //= 2
        gathered(lane_ref, phase - 7, 1)
    return channels


def plan_shapes():
    return [(LANE_RUNS, 256, 128), (SUB_RUNS, 256, 128), (8 * SWAPS, 128)]


def plan_scratch():
    return [pltpu.VMEM(shape, I32) for shape in plan_shapes()]


def split_tiles(array):
    return [array[8 * i : 8 * i + 8] for i in range(TILES)]


def z_behind(a):
    r = pltpu.roll(a, 1, 2)
    fill = jnp.concatenate([jnp.zeros_like(r[:1]), r[:1]], axis=0)
    return jnp.where(iota(a.shape, 2) == 0, fill, r)


def z_ahead(a):
    r = pltpu.roll(a, 127, 2)
    fill = jnp.concatenate([r[1:], jnp.zeros_like(r[:1])], axis=0)
    return jnp.where(iota(a.shape, 2) == 127, fill, r)


def y_shift(a, steps):
    return jnp.stack([pltpu.roll(a[h], steps % a.shape[1], 0) for h in range(2)])


def fractions(code):
    return [((code >> shift & 3).astype(F32) + 0.5) * 0.25 for shift in (0, 2, 4)]


Y_UP = ((0, 4, 5), (1, 5, 4), (2, 4, 5), (3, 5, 4), (4, 5, 3))
Y_DOWN = ((0, 0, 5), (1, 0, 4), (2, 0, 5), (3, 0, 4), (4, 0, 4))
X_UP = ((0, 12, 5), (1, 12, 5), (2, 13, 4), (3, 13, 4), (4, 13, 3))
X_DOWN = ((0, 0, 5), (1, 0, 5), (2, 0, 4), (3, 0, 4), (4, 0, 4))
UP_ROWS, DOWN_ROWS = 720, 752


def y_pieces(table):
    at, out = 0, []
    for x in range(CX + 1):
        for field, first, count in table:
            if field == 4 and x == CX:
                continue
            for half in range(2):
                out.append((field, x, half, first, count, at))
                at += count
    return out


def x_pieces(table):
    at, out = 0, []
    for field, first, count in table:
        for plane in range(first, first + count):
            for half in range(2):
                out.append((field, plane, half, at))
                at += 17
    return out


def plan_kernel(source, key_ref, lane_ref, sub_ref, swap_ref):
    k = key_ref[...]
    if source:
        key = ((k & 0x700) << 4) | ((k & 0x7800) >> 3) | (k & 0xFF)
    else:
        key = ((k & 0x380) << 5) | ((k & 0x7C00) >> 3) | (k & 0x7F)
    sort_plan(split_tiles(key), lane_ref, sub_ref, swap_ref)


def make_plan(key, source):
    return kernel_call(
        functools.partial(plan_kernel, source),
        "cell_plan" if source else "particle_plan",
        [of(shape, I32) for shape in plan_shapes()],
        [],
        (key,),
        flops=10**7,
    )


def move_kernel(value_ref, lane_ref, sub_ref, swap_ref, out_ref):
    def move(pair, carry):
        at = (2 * pair, 2 * pair + 1)
        channels = [[value_ref[c, 8 * i : 8 * i + 8] for i in range(TILES)] for c in at]
        follow_plan(channels, lane_ref, sub_ref, swap_ref)
        for c, tiles in zip(at, channels):
            for i, t in enumerate(tiles):
                out_ref[c, 8 * i : 8 * i + 8] = t
        return carry

    lax.fori_loop(0, value_ref.shape[0] // 2, move, 0)


def move_tag_kernel(code_ref, state_ref, lane_ref, sub_ref, swap_ref, out_ref, tag_ref):
    tag = (code_ref[...] << 15) | (iota((256, 128), 0) * 128 + iota((256, 128), 1))
    for i, t in enumerate(follow_plan([split_tiles(tag)], lane_ref, sub_ref, swap_ref)[0]):
        tag_ref[8 * i : 8 * i + 8] = t
    move_kernel(state_ref, lane_ref, sub_ref, swap_ref, out_ref)


def move_to_cells(code, state, plan):
    return kernel_call(
        move_tag_kernel, "to_cells", (of(state.shape), of(code.shape, I32)), [], (code, state, *plan), flops=10**7
    )


def move_to_particles(values, plan):
    return kernel_call(move_kernel, "to_particles", (of(values.shape),), [], (values, *plan), flops=10**7)[0]


def deposit_kernel(cells_ref, tag_ref, flag_ref, grid_ref, up_ref, down_ref):
    up_at = {(f, x, h): (first, count, at) for f, x, h, first, count, at in y_pieces(Y_UP)}
    down_at = {(f, x, h): (first, count, at) for f, x, h, first, count, at in y_pieces(Y_DOWN)}
    first_row = iota((2, 8, 128), 1) == 0
    before = None
    for x in range(CX + 1):
        here = []
        if x < CX:
            code = tag_ref[16 * x : 16 * x + 16].reshape(2, 8, 128) >> 15
            fx, fy, fz = fractions(code)
            wx, wy, wz = (1.0 - fx, fx), (1.0 - fy, fy), (1.0 - fz, fz)
            w = {(i, j, k): wx[i] * wy[j] * wz[k] for i in (0, 1) for j in (0, 1) for k in (0, 1)}
            here.append(w)
            for comp in range(3):
                v, c0, c1, c2 = [
                    cells_ref[c, 16 * x : 16 * x + 16].reshape(2, 8, 128)
                    for c in (comp, 3 + 3 * comp, 4 + 3 * comp, 5 + 3 * comp)
                ]
                base = v - c0 * fx - c1 * fy - c2 * fz
                terms = {}
                for i in (0, 1):
                    a = base + c0 if i else base
                    for j in (0, 1):
                        b = a + c1 if j else a
                        for k in (0, 1):
                            terms[i, j, k] = w[i, j, k] * (b + c2 if k else b)
                here.append(terms)
        for f in range(4):
            s = {}
            for j in (0, 1):
                for k in (0, 1):
                    parts = []
                    if x < CX:
                        parts.append(here[f][0, j, k])
                    if x > 0:
                        parts.append(before[f][1, j, k])
                    s[j, k] = sum(parts[1:], parts[0])
            near, far = [s[j, 0] + z_behind(s[j, 1]) for j in (0, 1)]
            turned = y_shift(far, 1)
            main = near + jnp.where(first_row, 0.0, turned)
            grid_ref[f, x] = main
            for h in range(2):
                first, count, at = up_at[f, x, h]
                up_ref[at : at + 8 - first] = main[h, first:8]
                up_ref[at + 8 - first : at + 9 - first] = turned[h, 0:1]
                first, count, at = down_at[f, x, h]
                down_ref[at : at + count] = main[h, :count]
        if x < CX:
            for h in range(2):
                flags = flag_ref[x, :, 128 * h : 128 * h + 128].astype(F32)
                for table, ref in ((up_at, up_ref), (down_at, down_ref)):
                    first, count, at = table[4, x, h]
                    ref[at : at + count] = flags[first : first + count]
        before = here


def tiled_bytes(shape):
    *outer, rows, columns = shape
    return 4 * math.prod(outer) * (-(-rows // 8) * 8) * (-(-columns // 128) * 128)


def kernel_call(body, name, outs, scratch, args, in_specs=None, flops=0):
    held = [x.shape for x in (*args, *outs) if len(x.shape) > 1] + list(scratch)
    size = sum(tiled_bytes(shape) for shape in held)
    return pl.pallas_call(
        body,
        out_shape=outs,
        **({} if in_specs is None else dict(in_specs=in_specs)),
        scratch_shapes=[pltpu.VMEM(shape, F32) for shape in scratch],
        compiler_params=pltpu.CompilerParams(vmem_limit_bytes=size + 4 * 2**20),
        cost_estimate=pl.CostEstimate(flops=flops, bytes_accessed=size, transcendentals=0),
        name=name,
    )(*args)


def of(shape, kind=F32):
    return jax.ShapeDtypeStruct(shape, kind)


def deposit(cells, tag, flags):
    return kernel_call(
        deposit_kernel,
        "deposit",
        (of((4, CX + 1, 2, 8, 128)), of((UP_ROWS, 128)), of((DOWN_ROWS, 128))),
        [],
        (cells, tag, flags),
    )


def widen_kernel(keep_ref, grid_ref, own_ref, low_ref, high_ref, flag_ref, after_ref, wide_ref, up_ref, down_ref):
    keep = keep_ref[1]
    zero = jnp.zeros((2, 8, 128), F32)
    for f in range(5):
        for x in range(CX + 1):
            wide_ref[f, x, :, 0:8] = zero
            wide_ref[f, x, :, 16:24] = zero
            if f < 4:
                wide_ref[f, x, :, 8:16] = grid_ref[f, x]
            elif x < CX:
                for h in range(2):
                    wide_ref[f, x, h, 8:16] = flag_ref[x, :, 128 * h : 128 * h + 128].astype(F32)
            else:
                wide_ref[f, x, :, 8:16] = zero
    for f, x, h, first, count, at in y_pieces(Y_DOWN):
        wide_ref[f, x, h, 16 : 16 + count] = high_ref[at : at + count]
    for f, x, h, first, count, at in y_pieces(Y_UP):
        below = 8 - first
        wide_ref[f, x, h, first:8] = low_ref[at : at + below]
        if f < 4:
            rim = at + below
            wide_ref[f, x, h, 8:9] = wide_ref[f, x, h, 8:9] + low_ref[rim : rim + 1]
            wide_ref[f, x, h, 16:17] = wide_ref[f, x, h, 16:17] + keep * own_ref[rim : rim + 1]
    for table, ref in ((X_UP, up_ref), (X_DOWN, down_ref)):
        for f, plane, h, at in x_pieces(table):
            ref[at : at + 17] = wide_ref[f, plane, h, 4:21]


def smem():
    return pl.BlockSpec(memory_space=pltpu.SMEM)


def vmem():
    return pl.BlockSpec(memory_space=pltpu.VMEM)


def widen(keep, grid, own, low, high, flags, after):
    return kernel_call(
        widen_kernel,
        "widen",
        (of((5, CX + 1, 2, 24, 128)), of((UP_ROWS, 128)), of((DOWN_ROWS, 128))),
        [],
        (keep, grid, own, low, high, flags, after),
        [smem()] + [vmem()] * 5 + [pl.BlockSpec(memory_space=pl.ANY)],
    )


def krylov_kernel(keep_ref, wide_ref, low_ref, high_ref, vel_ref, fluid_ref, k0_ref, k1_ref, k2_ref, sums_ref, ext):
    keep = keep_ref[0]
    zero = jnp.zeros((2, 24, 128), F32)
    for f in range(5):
        for plane in (0, 1, 2, 3, 21, 22, 23, 24):
            ext[f, plane] = zero
        for x in range(CX):
            ext[f, x + 4] = wide_ref[f, x]
        ext[f, 20] = keep * wide_ref[f, CX]
    for f, plane, h, at in x_pieces(X_UP):
        rows = low_ref[at : at + 17]
        if plane == CX:
            ext[f, 4, h, 4:21] = ext[f, 4, h, 4:21] + rows
        else:
            ext[f, plane - 12, h, 4:21] = rows
    for f, plane, h, at in x_pieces(X_DOWN):
        rows = high_ref[at : at + 17]
        if plane == 0 and f < 4:
            ext[f, 20, h, 4:21] = ext[f, 20, h, 4:21] + rows
        else:
            ext[f, plane + 20, h, 4:21] = rows
    for plane in range(25):
        inverse = 1.0 / jnp.maximum(ext[0, plane], 0.5)
        for d in range(3):
            vel_ref[d, plane] = ext[1 + d, plane] * inverse
        fluid_ref[plane] = ext[4, plane]
    for plane in range(1, 24):
        vy, vz = vel_ref[1, plane], vel_ref[2, plane]
        divergence = (
            0.5 * (vel_ref[0, plane + 1] - vel_ref[0, plane - 1])
            + 0.5 * (y_shift(vy, -1) - y_shift(vy, 1))
            + 0.5 * (z_ahead(vz) - z_behind(vz))
        )
        k0_ref[plane] = -fluid_ref[plane] * divergence

    def applied(ref, plane):
        a = ref[plane]
        beside = (
            ref[plane + 1] + ref[plane - 1] + y_shift(a, 1) + y_shift(a, -1) + z_ahead(a) + z_behind(a)
        )
        return fluid_ref[plane] * (a - beside * (1.0 / 6.0))

    for plane in range(2, 23):
        k1_ref[plane] = applied(k0_ref, plane)
    for plane in range(3, 22):
        k2_ref[plane] = applied(k1_ref, plane)
    totals = [jnp.zeros((2, 8, 128), F32)] * 14
    for plane in range(4, 20):
        k0, k1, k2 = [ref[plane, :, 8:16] for ref in (k0_ref, k1_ref, k2_ref)]
        k3 = applied(k2_ref, plane)[:, 8:16]
        u1, w1 = k0 - k1, k1 - k2
        u2 = u1 - w1
        w2 = w1 - (k2 - k3)
        pairs = (
            (k0, k0), (k0, k1), (k1, k1), (k1, k2), (k2, k2), (k2, k3),
            (k0, u1), (u1, u1), (u1, u2), (u2, u2), (k0, w1), (u1, w1), (u1, w2), (u2, w2),
        )
        totals = [t + a * b for t, (a, b) in zip(totals, pairs)]
    for i, t in enumerate(totals):
        sums_ref[i : i + 1] = jnp.sum(t[0] + t[1], axis=0, keepdims=True)
    sums_ref[14:16] = jnp.zeros((2, 128), F32)


def krylov(keep, wide, low, high):
    return kernel_call(
        krylov_kernel,
        "krylov",
        (of((3, 25, 2, 24, 128)),) + (of((25, 2, 24, 128)),) * 4 + (of((16, 128)),),
        [(5, 25, 2, 24, 128)],
        (keep, wide, low, high),
        [smem()] + [vmem()] * 3,
    )


def steps_from(gram, energy, apply_once):
    def form(a, table):
        total = None
        for i, p in enumerate(a):
            for j, q in enumerate(a):
                if p is not None and q is not None:
                    term = p * q * table[i + j]
                    total = term if total is None else total + term
        return total

    def ratio(a, b):
        return jnp.where(b > 0.0, a / jnp.where(b > 0.0, b, 1.0), 0.0)

    one, zero = jnp.ones_like(gram[0]), jnp.zeros_like(gram[0])
    residual, direction, answer = [one], [one], [zero] * 3
    norm = gram[0]
    for step in range(3):
        alpha = ratio(norm, form(direction, energy))
        for i, p in enumerate(direction):
            answer[i] = answer[i] + alpha * p
        if step == 2:
            return answer
        image = apply_once(direction, zero)
        residual = [a - alpha * b for a, b in zip(residual + [zero], image)]
        norm_next = form(residual, gram)
        direction = [a + ratio(norm_next, norm) * b for a, b in zip(residual, direction + [zero])]
        norm = norm_next


def coefficients(m):
    power = steps_from(m[0:5], m[1:6], lambda a, zero: [zero] + a)
    shifted = steps_from(
        [m[0]] + m[6:10],
        [m[1]] + m[10:14],
        lambda a, zero: [p - q for p, q in zip(a + [zero], [zero] + a)],
    )
    turned = [shifted[0] + shifted[1] + shifted[2], -shifted[1] - 2.0 * shifted[2], shifted[2]]
    smooth = m[1] < 0.3 * m[0]
    return [jnp.where(smooth, a, b) * (1.0 / 6.0) for a, b in zip(power, turned)]


def blend_kernel(vel_ref, fluid_ref, k0_ref, k1_ref, k2_ref, tag_ref, out_ref, proj):
    for x in range(CX + 1):
        fluid = fluid_ref[x + 4, :, 8:24]
        for b, ref in enumerate((None, k0_ref, k1_ref, k2_ref)):
            if ref is None:
                fields = [fluid * vel_ref[d, x + 4, :, 8:24] for d in range(3)]
            else:
                p, scale = ref[x + 4], -0.5 * fluid
                inner = p[:, 8:24]
                fields = [
                    scale * (ref[x + 5, :, 8:24] - ref[x + 3, :, 8:24]),
                    scale * (y_shift(p, -1) - y_shift(p, 1))[:, 8:24],
                    scale * (z_ahead(inner) - z_behind(inner)),
                ]
            for d, field in enumerate(fields):
                proj[x, 3 * b + d, 0] = field
                proj[x, 3 * b + d, 1] = z_ahead(field)
    for x in range(CX):
        code = tag_ref[16 * x : 16 * x + 16].reshape(2, 8, 128) >> 15
        fx, fy, fz = fractions(code)
        wx, wy, wz = (1.0 - fx, fx), (1.0 - fy, fy), (1.0 - fz, fz)
        w = {(i, j, k): wx[i] * wy[j] * wz[k] for i in (0, 1) for j in (0, 1) for k in (0, 1)}
        for c in range(12):
            result = None
            for (i, j, k), weight in w.items():
                term = weight * proj[x + i, c, k, :, j : 8 + j]
                result = term if result is None else result + term
            out_ref[c, 16 * x : 16 * x + 16] = result.reshape(16, 128)


def blend(*args):
    return kernel_call(
        blend_kernel, "blend", (of((12, 256, 128)),), [(CX + 1, 12, 2, 2, 16, 128)], args, flops=10**7
    )[0]


def finish_kernel(sums_ref, k0_ref, k1_ref, k2_ref, parts_ref, pressure_ref, out_ref):
    total = jnp.sum(sums_ref[...], axis=1, keepdims=True)
    c = coefficients([jnp.broadcast_to(total[i : i + 1], (8, 128)) for i in range(14)])
    for x in range(CX):
        for h in range(2):
            k0, k1, k2 = [ref[x + 4, h, 8:16] for ref in (k0_ref, k1_ref, k2_ref)]
            pressure_ref[x, :, 128 * h : 128 * h + 128] = c[0] * k0 + c[1] * k1 + c[2] * k2
    for i in range(TILES):
        rows = slice(8 * i, 8 * i + 8)
        for d in range(3):
            out_ref[d, rows] = (
                parts_ref[d, rows]
                + c[0] * parts_ref[3 + d, rows]
                + c[1] * parts_ref[6 + d, rows]
                + c[2] * parts_ref[9 + d, rows]
            )


def finish(*args):
    return kernel_call(finish_kernel, "finish", (of((CX, CY, 256)), of((3, 256, 128))), [], args)


def neighbours(up, down, axis):
    pairs = [(i, i + 1) for i in range(lax.axis_size(axis) - 1)]
    return lax.ppermute(up, axis, pairs), lax.ppermute(down, axis, [(b, a) for a, b in pairs])


def summed(sums, axis):
    count = lax.axis_size(axis)
    parts = [sums]
    for shift in range(1, count):
        parts.append(lax.ppermute(sums, axis, [(i, (i + shift) % count) for i in range(count)]))
    return functools.reduce(jnp.add, parts)


def local(cell_index, offset_code, particle_state, fluid_flags):
    places = [(axis, lax.axis_index(axis), lax.axis_size(axis)) for axis in ("gx", "gy")]
    keep = jnp.stack([(at + 1 < size).astype(F32) for _, at, size in places])
    plan = make_plan(cell_index.reshape(256, 128), True)
    cells, tag = move_to_cells(offset_code.reshape(256, 128), particle_state.reshape(12, 256, 128), plan)
    grid, up, down = deposit(cells, tag, fluid_flags)
    low, high = neighbours(up, down, "gy")
    plan = make_plan(tag & 0x7FFF, False)
    wide, up_x, down_x = widen(keep, grid, up, low, high, fluid_flags, plan[1])
    low, high = neighbours(up_x, down_x, "gx")
    vel, fluid, k0, k1, k2, sums = krylov(keep, wide, low, high)
    parts = blend(vel, fluid, k0, k1, k2, tag)
    sums, parts = lax.optimization_barrier((summed(sums, "gx"), parts))
    parts = move_to_particles(parts, plan)
    sums = summed(sums, "gy")
    pressure, result = finish(sums, k0, k1, k2, parts)
    return pressure, result.reshape(1, 3, CELLS)


def solution(mesh):
    return jax.shard_map(
        local,
        mesh=mesh,
        in_specs=(
            P(("groups", "gx", "gy"), None),
            P(("groups", "gx", "gy"), None),
            P(("groups", "gx", "gy"), None, None),
            P(("groups", "gx"), "gy", None),
        ),
        out_specs=(P(("groups", "gx"), "gy", None), P(("groups", "gx", "gy"), None, None)),
        check_vma=False,
    )
```

```python
import functools
import math

import jax
import jax.numpy as jnp
from jax import lax
from jax.experimental import pallas as pl
from jax.experimental.pallas import tpu as pltpu
from jax.sharding import PartitionSpec as P

F32, I32 = jnp.float32, jnp.int32
CX, CY, CELLS = 16, 8, 32768
TILES = CELLS // 1024
LANE_RUNS, SUB_RUNS, SWAPS = 9, 3, 30 * 16


def take(x, index, axis):
    other = tuple(d for d in range(x.ndim) if d != axis)
    dims = lax.GatherDimensionNumbers(
        offset_dims=(),
        collapsed_slice_dims=(axis,),
        start_index_map=(axis,),
        operand_batching_dims=other,
        start_indices_batching_dims=other,
    )
    return lax.gather(
        x, index[..., None], dims, (1,) * x.ndim, mode=lax.GatherScatterMode.PROMISE_IN_BOUNDS
    )


def iota(shape, dim):
    return lax.broadcasted_iota(I32, shape, dim)


def sort_plan(tiles, lane_ref, sub_ref, swap_ref):
    lanes, subs = iota((64, 128), 1), iota((8, 128), 0)
    top = 0x7FFF

    def grouped(tiles):
        return [jnp.concatenate(tiles[8 * i : 8 * i + 8], axis=0) for i in range(4)]

    def lane_steps(groups, stride):
        def ordered(low, a, b):
            return jnp.where(low, jnp.minimum(a, b), jnp.maximum(a, b))

        while stride:
            half = stride // 2
            low, low_half = lanes & stride == 0, lanes & half == 0
            across = [take(g, lanes ^ stride, 1) for g in groups]
            if half:
                beside = [take(g, lanes ^ half, 1) for g in groups]
                both = [take(g, lanes ^ (stride | half), 1) for g in groups]
                groups = [
                    ordered(low_half, ordered(low, g, a), ordered(low, b, c))
                    for g, a, b, c in zip(groups, across, beside, both)
                ]
            else:
                groups = [ordered(low, g, a) for g, a in zip(groups, across)]
            stride //= 4
        return groups

    def record(run, groups):
        for i, g in enumerate(groups):
            lane_ref[run, 64 * i : 64 * i + 64] = g & 127
        return [groups[i // 8][8 * (i % 8) : 8 * (i % 8) + 8] >> 7 for i in range(TILES)]

    groups = [(g << 7) | lanes for g in grouped(tiles)]
    for phase in range(1, 7):
        turn = jnp.where(lanes & (1 << phase) != 0, top << 7, 0)
        groups = [g ^ turn for g in groups]
        groups = lane_steps(groups, 1 << (phase - 1))
        groups = [g ^ turn for g in groups]
    turn = jnp.where(iota((64, 128), 0) & 8 != 0, top << 7, 0)
    groups = lane_steps([g ^ turn for g in groups], 64)
    tiles = record(0, groups)
    tiles = [t ^ top if i & 1 else t for i, t in enumerate(tiles)]

    swap = 0
    for phase in range(8, 16):
        if phase < 12:
            turns = [top if i >> (phase - 7) & 1 else 0 for i in range(TILES)]
        elif phase < 15:
            turns = [jnp.where(subs & (1 << (phase - 12)) != 0, top, 0)] * TILES
        else:
            turns = [0] * TILES
        tiles = [t ^ f for t, f in zip(tiles, turns)]
        if phase > 12:
            tiles = [(t << 3) | subs for t in tiles]
            stride = 1 << (phase - 13)
            while stride:
                low = subs & stride == 0
                other = [take(t, subs ^ stride, 0) for t in tiles]
                tiles = [
                    jnp.where(low, jnp.minimum(t, o), jnp.maximum(t, o)) for t, o in zip(tiles, other)
                ]
                stride //= 2
            for i, t in enumerate(tiles):
                sub_ref[phase - 13, 8 * i : 8 * i + 8] = t & 7
            tiles = [t >> 3 for t in tiles]
        hop = 1 << (min(phase, 12) - 8)
        while hop:
            for i in range(TILES):
                if i & hop == 0:
                    a, b = tiles[i], tiles[i + hop]
                    swap_ref[8 * swap : 8 * swap + 8] = jnp.where(a > b, 1, 0)
                    swap += 1
                    tiles[i], tiles[i + hop] = jnp.minimum(a, b), jnp.maximum(a, b)
            hop //= 2
        groups = [(g << 7) | lanes for g in grouped(tiles)]
        tiles = record(phase - 7, lane_steps(groups, 64))
        tiles = [t ^ f for t, f in zip(tiles, turns)]
    return tiles


def follow_plan(stages, lane_ref, sub_ref, swap_ref):
    def crossings(hops, before):
        out = {}
        for hop in hops:
            for i in range(TILES):
                if i & hop == 0:
                    out[hop, i] = before
                    before += 1
        return out, before

    def pass_over(sets, work):
        for members in sets:
            moved = [{i: ref[c, i] for i in members} for ref, c in stages]
            work(members, moved)
            for (ref, c), tiles in zip(stages, moved):
                for i, t in tiles.items():
                    ref[c, i] = t

    def gathered(ref, run, axis, members, moved):
        for i in members:
            index = ref[run, 8 * i : 8 * i + 8]
            for tiles in moved:
                tiles[i] = take(tiles[i], index, axis)

    def exchanged(hops, number, members, moved):
        for hop in hops:
            for i in members:
                if i & hop == 0:
                    at = 8 * number[hop, i]
                    crossed = swap_ref[at : at + 8] != 0
                    for tiles in moved:
                        a, b = tiles[i], tiles[i + hop]
                        tiles[i], tiles[i + hop] = jnp.where(crossed, b, a), jnp.where(crossed, a, b)

    eights = [range(8 * g, 8 * g + 8) for g in range(4)]
    numbers, before = {}, 0
    for phase in range(8, 16):
        hops = [1 << k for k in reversed(range(min(phase, 12) - 7))]
        numbers[phase], before = crossings(hops, before)

    def first(members, moved):
        gathered(lane_ref, 0, 1, members, moved)
        for phase in (8, 9, 10):
            exchanged([4, 2, 1][10 - phase :], numbers[phase], members, moved)
            gathered(lane_ref, phase - 7, 1, members, moved)

    pass_over(eights, first)
    for phase in range(11, 16):
        wide = [16, 8] if phase > 11 else [8]
        reach = 32 if phase > 11 else 16
        sets = [range(low + k, low + reach, 8) for low in range(0, 32, reach) for k in range(8)]

        def across(members, moved):
            if phase > 12:
                gathered(sub_ref, phase - 13, 0, members, moved)
            exchanged(wide, numbers[phase], members, moved)

        def within(members, moved):
            exchanged([4, 2, 1], numbers[phase], members, moved)
            gathered(lane_ref, phase - 7, 1, members, moved)

        pass_over(sets, across)
        pass_over(eights, within)


def plan_shapes():
    return [(LANE_RUNS, 256, 128), (SUB_RUNS, 256, 128), (8 * SWAPS, 128)]


def plan_scratch():
    return [pltpu.VMEM(shape, I32) for shape in plan_shapes()]


def split_tiles(array):
    return [array[8 * i : 8 * i + 8] for i in range(TILES)]


def z_behind(a):
    r = pltpu.roll(a, 1, 2)
    fill = jnp.concatenate([jnp.zeros_like(r[:1]), r[:1]], axis=0)
    return jnp.where(iota(a.shape, 2) == 0, fill, r)


def z_ahead(a):
    r = pltpu.roll(a, 127, 2)
    fill = jnp.concatenate([r[1:], jnp.zeros_like(r[:1])], axis=0)
    return jnp.where(iota(a.shape, 2) == 127, fill, r)


def y_shift(a, steps):
    return jnp.stack([pltpu.roll(a[h], steps % a.shape[1], 0) for h in range(2)])


def fractions(code):
    return [((code >> shift & 3).astype(F32) + 0.5) * 0.25 for shift in (0, 2, 4)]


Y_UP = ((0, 4, 5), (1, 5, 4), (2, 4, 5), (3, 5, 4), (4, 5, 3))
Y_DOWN = ((0, 0, 5), (1, 0, 4), (2, 0, 5), (3, 0, 4), (4, 0, 4))
X_UP = ((0, 12, 5), (1, 12, 5), (2, 13, 4), (3, 13, 4), (4, 13, 3))
X_DOWN = ((0, 0, 5), (1, 0, 5), (2, 0, 4), (3, 0, 4), (4, 0, 4))
UP_ROWS, DOWN_ROWS = 720, 752


def y_pieces(table):
    at, out = 0, []
    for x in range(CX + 1):
        for field, first, count in table:
            if field == 4 and x == CX:
                continue
            for half in range(2):
                out.append((field, x, half, first, count, at))
                at += count
    return out


def x_pieces(table):
    at, out = 0, []
    for field, first, count in table:
        for plane in range(first, first + count):
            for half in range(2):
                out.append((field, plane, half, at))
                at += 17
    return out


def particle_plan_kernel(tag_ref, lane_ref, sub_ref, swap_ref):
    k = tag_ref[...] & 0x7FFF
    key = ((k & 0x380) << 5) | ((k & 0x7C00) >> 3) | (k & 0x7F)
    sort_plan(split_tiles(key), lane_ref, sub_ref, swap_ref)


def particle_plan(tag):
    outs = [of(shape, I32) for shape in plan_shapes()]
    return kernel_call(particle_plan_kernel, "particle_plan", outs, [], (tag,), flops=10**7)


def to_cells_kernel(cell_ref, code_ref, state_ref, cells_ref, tag_ref, code, lane_ref, sub_ref, swap_ref, done):
    arrivals = [
        pltpu.make_async_copy(code_ref, code, done.at[0]),
        pltpu.make_async_copy(state_ref, cells_ref, done.at[1]),
    ]
    for arrival in arrivals:
        arrival.start()
    k = cell_ref[...]
    key = ((k & 0x700) << 4) | ((k & 0x7800) >> 3) | (k & 0xFF)
    sort_plan(split_tiles(key), lane_ref, sub_ref, swap_ref)
    for arrival in arrivals:
        arrival.wait()
    tag_ref[0] = (code[...] << 15) | (iota((TILES, 8, 128), 0) * 8 + iota((TILES, 8, 128), 1)) * 128 + iota(
        (TILES, 8, 128), 2
    )
    for quad in range(3):
        stages = [(cells_ref, 4 * quad + c) for c in range(4)]
        follow_plan(stages + [(tag_ref, 0)] * (quad == 0), lane_ref, sub_ref, swap_ref)


def to_cells(cell, code, state):
    anywhere = pl.BlockSpec(memory_space=pltpu.HBM)
    return kernel_call(
        to_cells_kernel,
        "to_cells",
        (of((12, TILES, 8, 128)), of((1, TILES, 8, 128), I32)),
        [pltpu.VMEM(shape, I32) for shape in [(TILES, 8, 128)] + plan_shapes()] + [pltpu.SemaphoreType.DMA((2,))],
        (cell, code.reshape(TILES, 8, 128), state.reshape(12, TILES, 8, 128)),
        [vmem(), anywhere, anywhere],
        flops=10**7,
    )


def deposit_kernel(cells_ref, tag_ref, flag_ref, grid_ref, up_ref, down_ref):
    up_at = {(f, x, h): (first, count, at) for f, x, h, first, count, at in y_pieces(Y_UP)}
    down_at = {(f, x, h): (first, count, at) for f, x, h, first, count, at in y_pieces(Y_DOWN)}
    first_row = iota((2, 8, 128), 1) == 0
    before = None
    for x in range(CX + 1):
        here = []
        if x < CX:
            code = tag_ref[0, 2 * x : 2 * x + 2] >> 15
            fx, fy, fz = fractions(code)
            wx, wy, wz = (1.0 - fx, fx), (1.0 - fy, fy), (1.0 - fz, fz)
            w = {(i, j, k): wx[i] * wy[j] * wz[k] for i in (0, 1) for j in (0, 1) for k in (0, 1)}
            here.append(w)
            for comp in range(3):
                v, c0, c1, c2 = [
                    cells_ref[c, 2 * x : 2 * x + 2]
                    for c in (comp, 3 + 3 * comp, 4 + 3 * comp, 5 + 3 * comp)
                ]
                base = v - c0 * fx - c1 * fy - c2 * fz
                terms = {}
                for i in (0, 1):
                    a = base + c0 if i else base
                    for j in (0, 1):
                        b = a + c1 if j else a
                        for k in (0, 1):
                            terms[i, j, k] = w[i, j, k] * (b + c2 if k else b)
                here.append(terms)
        for f in range(4):
            s = {}
            for j in (0, 1):
                for k in (0, 1):
                    parts = []
                    if x < CX:
                        parts.append(here[f][0, j, k])
                    if x > 0:
                        parts.append(before[f][1, j, k])
                    s[j, k] = sum(parts[1:], parts[0])
            near, far = [s[j, 0] + z_behind(s[j, 1]) for j in (0, 1)]
            turned = y_shift(far, 1)
            main = near + jnp.where(first_row, 0.0, turned)
            grid_ref[f, x] = main
            for h in range(2):
                first, count, at = up_at[f, x, h]
                up_ref[at : at + 8 - first] = main[h, first:8]
                up_ref[at + 8 - first : at + 9 - first] = turned[h, 0:1]
                first, count, at = down_at[f, x, h]
                down_ref[at : at + count] = main[h, :count]
        if x < CX:
            for h in range(2):
                flags = flag_ref[x, :, 128 * h : 128 * h + 128].astype(F32)
                for table, ref in ((up_at, up_ref), (down_at, down_ref)):
                    first, count, at = table[4, x, h]
                    ref[at : at + count] = flags[first : first + count]
        before = here


def tiled_bytes(shape):
    *outer, rows, columns = shape
    return 4 * math.prod(outer) * (-(-rows // 8) * 8) * (-(-columns // 128) * 128)


def kernel_call(body, name, outs, scratch, args, in_specs=None, flops=0):
    scratch = [x if hasattr(x, "dtype") else pltpu.VMEM(x, F32) for x in scratch]
    size = sum(tiled_bytes(x.shape) for x in (*args, *outs, *scratch) if len(x.shape) > 1)
    return pl.pallas_call(
        body,
        out_shape=outs,
        **({} if in_specs is None else dict(in_specs=in_specs)),
        scratch_shapes=scratch,
        compiler_params=pltpu.CompilerParams(vmem_limit_bytes=size + 4 * 2**20),
        cost_estimate=pl.CostEstimate(flops=flops, bytes_accessed=size, transcendentals=0),
        name=name,
    )(*args)


def of(shape, kind=F32):
    return jax.ShapeDtypeStruct(shape, kind)


def deposit(cells, tag, flags):
    return kernel_call(
        deposit_kernel,
        "deposit",
        (of((4, CX + 1, 2, 8, 128)), of((UP_ROWS, 128)), of((DOWN_ROWS, 128))),
        [],
        (cells, tag, flags),
    )


def widen_kernel(keep_ref, grid_ref, own_ref, low_ref, high_ref, flag_ref, after_ref, wide_ref, up_ref, down_ref):
    keep = keep_ref[1]
    zero = jnp.zeros((2, 8, 128), F32)
    for f in range(5):
        for x in range(CX + 1):
            wide_ref[f, x, :, 0:8] = zero
            wide_ref[f, x, :, 16:24] = zero
            if f < 4:
                wide_ref[f, x, :, 8:16] = grid_ref[f, x]
            elif x < CX:
                for h in range(2):
                    wide_ref[f, x, h, 8:16] = flag_ref[x, :, 128 * h : 128 * h + 128].astype(F32)
            else:
                wide_ref[f, x, :, 8:16] = zero
    for f, x, h, first, count, at in y_pieces(Y_DOWN):
        wide_ref[f, x, h, 16 : 16 + count] = high_ref[at : at + count]
    for f, x, h, first, count, at in y_pieces(Y_UP):
        below = 8 - first
        wide_ref[f, x, h, first:8] = low_ref[at : at + below]
        if f < 4:
            rim = at + below
            wide_ref[f, x, h, 8:9] = wide_ref[f, x, h, 8:9] + low_ref[rim : rim + 1]
            wide_ref[f, x, h, 16:17] = wide_ref[f, x, h, 16:17] + keep * own_ref[rim : rim + 1]
    for table, ref in ((X_UP, up_ref), (X_DOWN, down_ref)):
        for f, plane, h, at in x_pieces(table):
            ref[at : at + 17] = wide_ref[f, plane, h, 4:21]


def smem():
    return pl.BlockSpec(memory_space=pltpu.SMEM)


def vmem():
    return pl.BlockSpec(memory_space=pltpu.VMEM)


def widen(keep, grid, own, low, high, flags, after):
    return kernel_call(
        widen_kernel,
        "widen",
        (of((5, CX + 1, 2, 24, 128)), of((UP_ROWS, 128)), of((DOWN_ROWS, 128))),
        [],
        (keep, grid, own, low, high, flags, after),
        [smem()] + [vmem()] * 5 + [pl.BlockSpec(memory_space=pl.ANY)],
    )


def krylov_kernel(keep_ref, wide_ref, low_ref, high_ref, vel_ref, fluid_ref, k0_ref, k1_ref, k2_ref, sums_ref, ext):
    keep = keep_ref[0]
    zero = jnp.zeros((2, 24, 128), F32)
    for f in range(5):
        for plane in (0, 1, 2, 3, 21, 22, 23, 24):
            ext[f, plane] = zero
        for x in range(CX):
            ext[f, x + 4] = wide_ref[f, x]
        ext[f, 20] = keep * wide_ref[f, CX]
    for f, plane, h, at in x_pieces(X_UP):
        rows = low_ref[at : at + 17]
        if plane == CX:
            ext[f, 4, h, 4:21] = ext[f, 4, h, 4:21] + rows
        else:
            ext[f, plane - 12, h, 4:21] = rows
    for f, plane, h, at in x_pieces(X_DOWN):
        rows = high_ref[at : at + 17]
        if plane == 0 and f < 4:
            ext[f, 20, h, 4:21] = ext[f, 20, h, 4:21] + rows
        else:
            ext[f, plane + 20, h, 4:21] = rows
    for plane in range(25):
        inverse = 1.0 / jnp.maximum(ext[0, plane], 0.5)
        for d in range(3):
            vel_ref[d, plane] = ext[1 + d, plane] * inverse
        fluid_ref[plane] = ext[4, plane]
    for plane in range(1, 24):
        vy, vz = vel_ref[1, plane], vel_ref[2, plane]
        divergence = (
            0.5 * (vel_ref[0, plane + 1] - vel_ref[0, plane - 1])
            + 0.5 * (y_shift(vy, -1) - y_shift(vy, 1))
            + 0.5 * (z_ahead(vz) - z_behind(vz))
        )
        k0_ref[plane] = -fluid_ref[plane] * divergence

    def applied(ref, plane):
        a = ref[plane]
        beside = (
            ref[plane + 1] + ref[plane - 1] + y_shift(a, 1) + y_shift(a, -1) + z_ahead(a) + z_behind(a)
        )
        return fluid_ref[plane] * (a - beside * (1.0 / 6.0))

    for plane in range(2, 23):
        k1_ref[plane] = applied(k0_ref, plane)
    for plane in range(3, 22):
        k2_ref[plane] = applied(k1_ref, plane)
    totals = [jnp.zeros((2, 8, 128), F32)] * 14
    for plane in range(4, 20):
        k0, k1, k2 = [ref[plane, :, 8:16] for ref in (k0_ref, k1_ref, k2_ref)]
        k3 = applied(k2_ref, plane)[:, 8:16]
        u1, w1 = k0 - k1, k1 - k2
        u2 = u1 - w1
        w2 = w1 - (k2 - k3)
        pairs = (
            (k0, k0), (k0, k1), (k1, k1), (k1, k2), (k2, k2), (k2, k3),
            (k0, u1), (u1, u1), (u1, u2), (u2, u2), (k0, w1), (u1, w1), (u1, w2), (u2, w2),
        )
        totals = [t + a * b for t, (a, b) in zip(totals, pairs)]
    for i, t in enumerate(totals):
        sums_ref[i : i + 1] = jnp.sum(t[0] + t[1], axis=0, keepdims=True)
    sums_ref[14:16] = jnp.zeros((2, 128), F32)


def krylov(keep, wide, low, high):
    return kernel_call(
        krylov_kernel,
        "krylov",
        (of((3, 25, 2, 24, 128)),) + (of((25, 2, 24, 128)),) * 4 + (of((16, 128)),),
        [(5, 25, 2, 24, 128)],
        (keep, wide, low, high),
        [smem()] + [vmem()] * 3,
    )


def steps_from(gram, energy, apply_once):
    def form(a, table):
        total = None
        for i, p in enumerate(a):
            for j, q in enumerate(a):
                if p is not None and q is not None:
                    term = p * q * table[i + j]
                    total = term if total is None else total + term
        return total

    def ratio(a, b):
        return jnp.where(b > 0.0, a / jnp.where(b > 0.0, b, 1.0), 0.0)

    one, zero = jnp.ones_like(gram[0]), jnp.zeros_like(gram[0])
    residual, direction, answer = [one], [one], [zero] * 3
    norm = gram[0]
    for step in range(3):
        alpha = ratio(norm, form(direction, energy))
        for i, p in enumerate(direction):
            answer[i] = answer[i] + alpha * p
        if step == 2:
            return answer
        image = apply_once(direction, zero)
        residual = [a - alpha * b for a, b in zip(residual + [zero], image)]
        norm_next = form(residual, gram)
        direction = [a + ratio(norm_next, norm) * b for a, b in zip(residual, direction + [zero])]
        norm = norm_next


def coefficients(m):
    power = steps_from(m[0:5], m[1:6], lambda a, zero: [zero] + a)
    shifted = steps_from(
        [m[0]] + m[6:10],
        [m[1]] + m[10:14],
        lambda a, zero: [p - q for p, q in zip(a + [zero], [zero] + a)],
    )
    turned = [shifted[0] + shifted[1] + shifted[2], -shifted[1] - 2.0 * shifted[2], shifted[2]]
    smooth = m[1] < 0.3 * m[0]
    return [jnp.where(smooth, a, b) * (1.0 / 6.0) for a, b in zip(power, turned)]


def project_kernel(
    sums_ref, vel_ref, fluid_ref, k0_ref, k1_ref, k2_ref, tag_ref, lane_ref, sub_ref, swap_ref,
    pressure_ref, out_ref, press, proj,
):
    total = jnp.sum(jnp.sum(sums_ref[...], axis=0), axis=1, keepdims=True)
    c = coefficients([jnp.broadcast_to(total[i : i + 1], (8, 128)) for i in range(14)])
    c = [jnp.concatenate([a, a, a], axis=0)[None] for a in c]
    for plane in range(3, 22):
        press[plane] = c[0] * k0_ref[plane] + c[1] * k1_ref[plane] + c[2] * k2_ref[plane]
    for x in range(CX):
        for h in range(2):
            pressure_ref[x, :, 128 * h : 128 * h + 128] = press[x + 4, h, 8:16]
    for x in range(CX + 1):
        p = press[x + 4]
        inner = p[:, 8:24]
        slopes = (
            press[x + 5, :, 8:24] - press[x + 3, :, 8:24],
            (y_shift(p, -1) - y_shift(p, 1))[:, 8:24],
            z_ahead(inner) - z_behind(inner),
        )
        fluid = fluid_ref[x + 4, :, 8:24]
        for d in range(3):
            field = fluid * (vel_ref[d, x + 4, :, 8:24] - 0.5 * slopes[d])
            for j, rows in enumerate((field[:, 0:8], y_shift(field, -1)[:, 0:8])):
                proj[x, d, j, 0] = rows
                proj[x, d, j, 1] = z_ahead(rows)
    for x in range(CX):
        code = tag_ref[0, 2 * x : 2 * x + 2] >> 15
        fx, fy, fz = fractions(code)
        wx, wy, wz = (1.0 - fx, fx), (1.0 - fy, fy), (1.0 - fz, fz)
        w = {(i, j, k): wx[i] * wy[j] * wz[k] for i in (0, 1) for j in (0, 1) for k in (0, 1)}
        for d in range(3):
            result = None
            for (i, j, k), weight in w.items():
                term = weight * proj[x + i, d, j, k]
                result = term if result is None else result + term
            out_ref[d, 2 * x : 2 * x + 2] = result
    follow_plan([(out_ref, d) for d in range(3)], lane_ref, sub_ref, swap_ref)


def project(*args):
    return kernel_call(
        project_kernel,
        "project",
        (of((CX, CY, 256)), of((3, TILES, 8, 128))),
        [(25, 2, 24, 128), (CX + 1, 3, 2, 2, 2, 8, 128)],
        args,
    )


def neighbours(up, down, axis):
    pairs = [(i, i + 1) for i in range(lax.axis_size(axis) - 1)]
    return lax.ppermute(up, axis, pairs), lax.ppermute(down, axis, [(b, a) for a, b in pairs])


def everywhere(sums):
    count = lax.axis_size("gx") * lax.axis_size("gy")
    spread = jnp.broadcast_to(sums[None], (count,) + sums.shape)
    return lax.all_to_all(spread, ("gx", "gy"), 0, 0)


def local(cell_index, offset_code, particle_state, fluid_flags):
    places = [(axis, lax.axis_index(axis), lax.axis_size(axis)) for axis in ("gx", "gy")]
    keep = jnp.stack([(at + 1 < size).astype(F32) for _, at, size in places])
    cells, tag = to_cells(cell_index.reshape(256, 128), offset_code, particle_state)
    grid, up, down = deposit(cells, tag, fluid_flags)
    low, high = neighbours(up, down, "gy")
    plan = particle_plan(tag.reshape(256, 128))
    wide, up_x, down_x = widen(keep, grid, up, low, high, fluid_flags, plan[1])
    low, high = neighbours(up_x, down_x, "gx")
    vel, fluid, k0, k1, k2, sums = krylov(keep, wide, low, high)
    pressure, result = project(everywhere(sums), vel, fluid, k0, k1, k2, tag, *plan)
    return pressure, result.reshape(1, 3, CELLS)


def solution(mesh):
    return jax.shard_map(
        local,
        mesh=mesh,
        in_specs=(
            P(("groups", "gx", "gy"), None),
            P(("groups", "gx", "gy"), None),
            P(("groups", "gx", "gy"), None, None),
            P(("groups", "gx"), "gy", None),
        ),
        out_specs=(P(("groups", "gx"), "gy", None), P(("groups", "gx", "gy"), None, None)),
        check_vma=False,
    )
```

```python
import functools
import math

import jax
import jax.numpy as jnp
from jax import lax
from jax.experimental import pallas as pl
from jax.experimental.pallas import tpu as pltpu
from jax.sharding import PartitionSpec as P

F32, I32 = jnp.float32, jnp.int32
CX, CY, CELLS = 16, 8, 32768
TILES = CELLS // 1024
LANE_RUNS, SUB_RUNS, SWAPS = 9, 3, 30 * 16


def take(x, index, axis):
    other = tuple(d for d in range(x.ndim) if d != axis)
    dims = lax.GatherDimensionNumbers(
        offset_dims=(),
        collapsed_slice_dims=(axis,),
        start_index_map=(axis,),
        operand_batching_dims=other,
        start_indices_batching_dims=other,
    )
    return lax.gather(
        x, index[..., None], dims, (1,) * x.ndim, mode=lax.GatherScatterMode.PROMISE_IN_BOUNDS
    )


def iota(shape, dim):
    return lax.broadcasted_iota(I32, shape, dim)


def sort_plan(tiles, lane_ref, sub_ref, swap_ref):
    lanes, subs = iota((64, 128), 1), iota((8, 128), 0)
    top = 0x7FFF

    def grouped(tiles):
        return [jnp.concatenate(tiles[8 * i : 8 * i + 8], axis=0) for i in range(4)]

    def partner(x, index, stride, axis):
        if 2 * stride == (128, 8)[axis == 0]:
            return pltpu.roll(x, stride, axis)
        return take(x, index ^ stride, axis)

    def ordered(low, a, b):
        return jnp.where(low, jnp.minimum(a, b), jnp.maximum(a, b))

    def lane_steps(groups, stride):
        while stride:
            low = lanes & stride == 0
            other = [partner(g, lanes, stride, 1) for g in groups]
            groups = [ordered(low, g, o) for g, o in zip(groups, other)]
            stride //= 2
        return groups

    def record(run, groups):
        for i, g in enumerate(groups):
            lane_ref[run, 64 * i : 64 * i + 64] = g & 127
        return [groups[i // 8][8 * (i % 8) : 8 * (i % 8) + 8] >> 7 for i in range(TILES)]

    groups = [(g << 7) | lanes for g in grouped(tiles)]
    for phase in range(1, 7):
        turn = jnp.where(lanes & (1 << phase) != 0, top << 7, 0)
        groups = [g ^ turn for g in groups]
        groups = lane_steps(groups, 1 << (phase - 1))
        groups = [g ^ turn for g in groups]
    turn = jnp.where(iota((64, 128), 0) & 8 != 0, top << 7, 0)
    groups = lane_steps([g ^ turn for g in groups], 64)
    tiles = record(0, groups)
    tiles = [t ^ top if i & 1 else t for i, t in enumerate(tiles)]

    swap = 0
    for phase in range(8, 16):
        if phase < 12:
            turns = [top if i >> (phase - 7) & 1 else 0 for i in range(TILES)]
        elif phase < 15:
            turns = [jnp.where(subs & (1 << (phase - 12)) != 0, top, 0)] * TILES
        else:
            turns = [0] * TILES
        tiles = [t ^ f for t, f in zip(tiles, turns)]
        if phase > 12:
            tiles = [(t << 3) | subs for t in tiles]
            stride = 1 << (phase - 13)
            while stride:
                low = subs & stride == 0
                other = [partner(t, subs, stride, 0) for t in tiles]
                tiles = [ordered(low, t, o) for t, o in zip(tiles, other)]
                stride //= 2
            for i, t in enumerate(tiles):
                sub_ref[phase - 13, 8 * i : 8 * i + 8] = t & 7
            tiles = [t >> 3 for t in tiles]
        hop = 1 << (min(phase, 12) - 8)
        while hop:
            for i in range(TILES):
                if i & hop == 0:
                    a, b = tiles[i], tiles[i + hop]
                    swap_ref[8 * swap : 8 * swap + 8] = jnp.where(a > b, 1, 0)
                    swap += 1
                    tiles[i], tiles[i + hop] = jnp.minimum(a, b), jnp.maximum(a, b)
            hop //= 2
        groups = [(g << 7) | lanes for g in grouped(tiles)]
        tiles = record(phase - 7, lane_steps(groups, 64))
        tiles = [t ^ f for t, f in zip(tiles, turns)]
    return tiles


def follow_plan(stages, lane_ref, sub_ref, swap_ref):
    def crossings(hops, before):
        out = {}
        for hop in hops:
            for i in range(TILES):
                if i & hop == 0:
                    out[hop, i] = before
                    before += 1
        return out, before

    def pass_over(sets, work):
        for members in sets:
            moved = [{i: ref[c, i] for i in members} for ref, c in stages]
            work(members, moved)
            for (ref, c), tiles in zip(stages, moved):
                for i, t in tiles.items():
                    ref[c, i] = t

    def gathered(ref, run, axis, members, moved):
        for i in members:
            index = ref[run, 8 * i : 8 * i + 8]
            for tiles in moved:
                tiles[i] = take(tiles[i], index, axis)

    def exchanged(hops, number, members, moved):
        for hop in hops:
            for i in members:
                if i & hop == 0:
                    at = 8 * number[hop, i]
                    crossed = swap_ref[at : at + 8] != 0
                    for tiles in moved:
                        a, b = tiles[i], tiles[i + hop]
                        tiles[i], tiles[i + hop] = jnp.where(crossed, b, a), jnp.where(crossed, a, b)

    eights = [range(8 * g, 8 * g + 8) for g in range(4)]
    numbers, before = {}, 0
    for phase in range(8, 16):
        hops = [1 << k for k in reversed(range(min(phase, 12) - 7))]
        numbers[phase], before = crossings(hops, before)

    def first(members, moved):
        gathered(lane_ref, 0, 1, members, moved)
        for phase in (8, 9, 10):
            exchanged([4, 2, 1][10 - phase :], numbers[phase], members, moved)
            gathered(lane_ref, phase - 7, 1, members, moved)

    pass_over(eights, first)
    for phase in range(11, 16):
        wide = [16, 8] if phase > 11 else [8]
        reach = 32 if phase > 11 else 16
        sets = [range(low + k, low + reach, 8) for low in range(0, 32, reach) for k in range(8)]

        def across(members, moved):
            if phase > 12:
                gathered(sub_ref, phase - 13, 0, members, moved)
            exchanged(wide, numbers[phase], members, moved)

        def within(members, moved):
            exchanged([4, 2, 1], numbers[phase], members, moved)
            gathered(lane_ref, phase - 7, 1, members, moved)

        pass_over(sets, across)
        pass_over(eights, within)


def plan_shapes():
    return [(LANE_RUNS, 256, 128), (SUB_RUNS, 256, 128), (8 * SWAPS, 128)]


def plan_scratch():
    return [pltpu.VMEM(shape, I32) for shape in plan_shapes()]


def split_tiles(array):
    return [array[8 * i : 8 * i + 8] for i in range(TILES)]


def z_behind(a):
    r = pltpu.roll(a, 1, 2)
    fill = jnp.concatenate([jnp.zeros_like(r[:1]), r[:1]], axis=0)
    return jnp.where(iota(a.shape, 2) == 0, fill, r)


def z_ahead(a):
    r = pltpu.roll(a, 127, 2)
    fill = jnp.concatenate([r[1:], jnp.zeros_like(r[:1])], axis=0)
    return jnp.where(iota(a.shape, 2) == 127, fill, r)


def y_shift(a, steps):
    return jnp.stack([pltpu.roll(a[h], steps % a.shape[1], 0) for h in range(2)])


def fractions(code):
    return [((code >> shift & 3).astype(F32) + 0.5) * 0.25 for shift in (0, 2, 4)]


WAYS = [(dx, dy) for dx in (-1, 0, 1) for dy in (-1, 0, 1) if dx or dy]


def pieces(dx, dy):
    def reach(place, last):
        return max(0, -place, place - last)

    at, out = 0, []
    for plane in {1: range(12, 17), 0: range(17), -1: range(5)}[dx]:
        far_x = reach(plane - dx * CX, CX)
        for field in range(8):
            rows = []
            for row in {1: range(4, 9), 0: range(9), -1: range(5)}[dy]:
                far_y = reach(row - dy * CY, CY)
                read = [
                    max(far_x - 1, 0) + far_y <= 3,
                    far_x + max(far_y - 1, 0) <= 3,
                    far_x + far_y <= 3,
                ]
                shared = plane in (0, CX) or row in (0, CY)
                if field == 7:
                    wanted = read[2] and plane < CX and row < CY
                elif field == 0:
                    wanted = shared and any(read)
                else:
                    wanted = read[(field - 1) % 3] and shared == (field < 4)
                if wanted:
                    rows.append(row)
            while rows:
                count = 1
                while count < len(rows) and rows[count] == rows[0] + count:
                    count += 1
                for half in range(2):
                    out.append((field, plane, half, rows[0], count, at))
                    at += count
                rows = rows[count:]
    return out, -(-at // 8) * 8


def particle_plan_kernel(tag_ref, lane_ref, sub_ref, swap_ref):
    k = tag_ref[...] & 0x7FFF
    key = ((k & 0x380) << 5) | ((k & 0x7C00) >> 3) | (k & 0x7F)
    sort_plan(split_tiles(key), lane_ref, sub_ref, swap_ref)


def particle_plan(tag):
    outs = [of(shape, I32) for shape in plan_shapes()]
    return kernel_call(particle_plan_kernel, "particle_plan", outs, [], (tag,), flops=7 * 10**9)


def to_cells_kernel(cell_ref, code_ref, state_ref, cells_ref, tag_ref, code, lane_ref, sub_ref, swap_ref, done):
    arrivals = [
        pltpu.make_async_copy(code_ref, code, done.at[0]),
        pltpu.make_async_copy(state_ref, cells_ref, done.at[1]),
    ]
    for arrival in arrivals:
        arrival.start()
    k = cell_ref[...]
    key = ((k & 0x700) << 4) | ((k & 0x7800) >> 3) | (k & 0xFF)
    sort_plan(split_tiles(key), lane_ref, sub_ref, swap_ref)
    for arrival in arrivals:
        arrival.wait()
    tag_ref[0] = (code[...] << 15) | (iota((TILES, 8, 128), 0) * 8 + iota((TILES, 8, 128), 1)) * 128 + iota(
        (TILES, 8, 128), 2
    )
    for quad in range(3):
        stages = [(cells_ref, 4 * quad + c) for c in range(4)]
        follow_plan(stages + [(tag_ref, 0)] * (quad == 0), lane_ref, sub_ref, swap_ref)


def to_cells(cell, code, state):
    anywhere = pl.BlockSpec(memory_space=pltpu.HBM)
    return kernel_call(
        to_cells_kernel,
        "to_cells",
        (of((12, TILES, 8, 128)), of((1, TILES, 8, 128), I32)),
        [pltpu.VMEM(shape, I32) for shape in [(TILES, 8, 128)] + plan_shapes()] + [pltpu.SemaphoreType.DMA((2,))],
        (cell, code.reshape(TILES, 8, 128), state.reshape(12, TILES, 8, 128)),
        [vmem(), anywhere, anywhere],
        flops=2 * 10**10,
    )


def deposit_kernel(cells_ref, tag_ref, flag_ref, grid_ref, rim_ref, *out_refs):
    wanted = {}
    for (dx, dy), ref in zip(WAYS, out_refs):
        listed, rows = pieces(dx, dy)
        used = listed[-1][4] + listed[-1][5]
        if used < rows:
            ref[used:rows] = jnp.zeros((rows - used, 128), F32)
        for field, plane, half, first, count, at in listed:
            wanted.setdefault((field, plane), []).append((ref, half, first, count, at))

    def hand_out(field, plane, main, rim):
        for ref, half, first, count, at in wanted.get((field, plane), ()):
            inside = min(count, CY - first)
            if inside > 0:
                ref[at : at + inside] = main[half, first : first + inside]
            if inside < count:
                ref[at + count - 1 : at + count] = rim[half, 0:1]

    first_row = iota((2, 8, 128), 1) == 0
    before = None
    for x in range(CX + 1):
        here = []
        if x < CX:
            code = tag_ref[0, 2 * x : 2 * x + 2] >> 15
            fx, fy, fz = fractions(code)
            wx, wy, wz = (1.0 - fx, fx), (1.0 - fy, fy), (1.0 - fz, fz)
            w = {(i, j, k): wx[i] * wy[j] * wz[k] for i in (0, 1) for j in (0, 1) for k in (0, 1)}
            here.append(w)
            for comp in range(3):
                v, c0, c1, c2 = [
                    cells_ref[c, 2 * x : 2 * x + 2]
                    for c in (comp, 3 + 3 * comp, 4 + 3 * comp, 5 + 3 * comp)
                ]
                base = v - c0 * fx - c1 * fy - c2 * fz
                terms = {}
                for i in (0, 1):
                    a = base + c0 if i else base
                    for j in (0, 1):
                        b = a + c1 if j else a
                        for k in (0, 1):
                            terms[i, j, k] = w[i, j, k] * (b + c2 if k else b)
                here.append(terms)
        for f in range(4):
            s = {}
            for j in (0, 1):
                for k in (0, 1):
                    parts = []
                    if x < CX:
                        parts.append(here[f][0, j, k])
                    if x > 0:
                        parts.append(before[f][1, j, k])
                    s[j, k] = sum(parts[1:], parts[0])
            near, far = [s[j, 0] + z_behind(s[j, 1]) for j in (0, 1)]
            turned = y_shift(far, 1)
            main = near + jnp.where(first_row, 0.0, turned)
            rim = jnp.where(first_row, turned, 0.0)
            grid_ref[f, x], rim_ref[f, x] = main, rim
            hand_out(f, x, main, rim)
            if f == 0:
                inverse = 1.0 / jnp.maximum(main, 0.5)
            else:
                hand_out(3 + f, x, main * inverse, None)
        if x < CX:
            flags = jnp.stack([flag_ref[x, :, 128 * h : 128 * h + 128] for h in range(2)])
            hand_out(7, x, flags.astype(F32), None)
        before = here


def tiled_bytes(shape):
    *outer, rows, columns = shape
    return 4 * math.prod(outer) * (-(-rows // 8) * 8) * (-(-columns // 128) * 128)


def kernel_call(body, name, outs, scratch, args, in_specs=None, flops=0):
    scratch = [x if hasattr(x, "dtype") else pltpu.VMEM(x, F32) for x in scratch]
    size = sum(tiled_bytes(x.shape) for x in (*args, *outs, *scratch) if len(x.shape) > 1)
    return pl.pallas_call(
        body,
        out_shape=outs,
        **({} if in_specs is None else dict(in_specs=in_specs)),
        scratch_shapes=scratch,
        compiler_params=pltpu.CompilerParams(vmem_limit_bytes=size + 4 * 2**20),
        cost_estimate=pl.CostEstimate(flops=flops, bytes_accessed=size, transcendentals=0),
        name=name,
    )(*args)


def of(shape, kind=F32):
    return jax.ShapeDtypeStruct(shape, kind)


def deposit(cells, tag, flags):
    slabs = [of((pieces(dx, dy)[1], 128)) for dx, dy in WAYS]
    grid = of((4, CX + 1, 2, 8, 128))
    return kernel_call(deposit_kernel, "deposit", [grid, grid, *slabs], [], (cells, tag, flags))


def smem():
    return pl.BlockSpec(memory_space=pltpu.SMEM)


def vmem():
    return pl.BlockSpec(memory_space=pltpu.VMEM)


def krylov_kernel(keep_ref, grid_ref, rim_ref, flag_ref, *refs):
    slab_refs, after_ref = refs[: len(WAYS)], refs[len(WAYS)]
    vel_ref, fluid_ref, k0_ref, k1_ref, k2_ref, sums_ref, ext = refs[len(WAYS) + 1 :]
    zero = jnp.zeros((2, 8, 128), F32)
    for plane in range(25):
        own = 4 <= plane <= 20
        for f in range(4):
            ext[f, plane, :, 0:8] = zero
            ext[f, plane, :, 8:16] = grid_ref[f, plane - 4] if own else zero
            ext[f, plane, :, 16:24] = rim_ref[f, plane - 4] if own else zero
        fluid_ref[plane] = jnp.zeros((2, 24, 128), F32)
        if 4 <= plane < 20:
            for h in range(2):
                fluid_ref[plane, h, 8:16] = flag_ref[plane - 4, :, 128 * h : 128 * h + 128].astype(F32)
    arrived = []
    for (dx, dy), ref in zip(WAYS, slab_refs):
        for field, plane, half, first, count, at in pieces(-dx, -dy)[0]:
            arrived.append((field, plane + dx * CX + 4, half, first + dy * CY + 8, count, ref[at : at + count]))
    for field, plane, half, row, count, rows in arrived:
        if field < 4:
            ext[field, plane, half, row : row + count] = ext[field, plane, half, row : row + count] + rows
        elif field == 7:
            fluid_ref[plane, half, row : row + count] = rows
    for f in range(4):
        ext[f, 20] = keep_ref[0] * ext[f, 20]
        for plane in range(25):
            ext[f, plane, :, 16:24] = keep_ref[1] * ext[f, plane, :, 16:24]
    for plane in range(25):
        inverse = 1.0 / jnp.maximum(ext[0, plane], 0.5)
        for d in range(3):
            vel_ref[d, plane] = ext[1 + d, plane] * inverse
    for field, plane, half, row, count, rows in arrived:
        if 4 <= field < 7:
            vel_ref[field - 4, plane, half, row : row + count] = rows
    for plane in range(1, 24):
        vy, vz = vel_ref[1, plane], vel_ref[2, plane]
        divergence = (
            0.5 * (vel_ref[0, plane + 1] - vel_ref[0, plane - 1])
            + 0.5 * (y_shift(vy, -1) - y_shift(vy, 1))
            + 0.5 * (z_ahead(vz) - z_behind(vz))
        )
        k0_ref[plane] = -fluid_ref[plane] * divergence

    def applied(ref, plane):
        a = ref[plane]
        beside = (
            ref[plane + 1] + ref[plane - 1] + y_shift(a, 1) + y_shift(a, -1) + z_ahead(a) + z_behind(a)
        )
        return fluid_ref[plane] * (a - beside * (1.0 / 6.0))

    for plane in range(2, 23):
        k1_ref[plane] = applied(k0_ref, plane)
    for plane in range(3, 22):
        k2_ref[plane] = applied(k1_ref, plane)
    totals = [jnp.zeros((2, 8, 128), F32)] * 14
    for plane in range(4, 20):
        k0, k1, k2 = [ref[plane, :, 8:16] for ref in (k0_ref, k1_ref, k2_ref)]
        k3 = applied(k2_ref, plane)[:, 8:16]
        u1, w1 = k0 - k1, k1 - k2
        u2 = u1 - w1
        w2 = w1 - (k2 - k3)
        pairs = (
            (k0, k0), (k0, k1), (k1, k1), (k1, k2), (k2, k2), (k2, k3),
            (k0, u1), (u1, u1), (u1, u2), (u2, u2), (k0, w1), (u1, w1), (u1, w2), (u2, w2),
        )
        totals = [t + a * b for t, (a, b) in zip(totals, pairs)]
    for i, t in enumerate(totals):
        sums_ref[i : i + 1] = jnp.sum(t[0] + t[1], axis=0, keepdims=True)
    sums_ref[14:16] = jnp.zeros((2, 128), F32)


def krylov(keep, grid, rim, flags, slabs, after):
    return kernel_call(
        krylov_kernel,
        "krylov",
        (of((3, 25, 2, 24, 128)),) + (of((25, 2, 24, 128)),) * 4 + (of((16, 128)),),
        [(4, 25, 2, 24, 128)],
        (keep, grid, rim, flags, *slabs, after),
        [smem()] + [vmem()] * (3 + len(WAYS)) + [pl.BlockSpec(memory_space=pl.ANY)],
    )


def steps_from(gram, energy, apply_once):
    def form(a, table):
        total = None
        for i, p in enumerate(a):
            for j, q in enumerate(a):
                if p is not None and q is not None:
                    term = p * q * table[i + j]
                    total = term if total is None else total + term
        return total

    def ratio(a, b):
        return jnp.where(b > 0.0, a / jnp.where(b > 0.0, b, 1.0), 0.0)

    one, zero = jnp.ones_like(gram[0]), jnp.zeros_like(gram[0])
    residual, direction, answer = [one], [one], [zero] * 3
    norm = gram[0]
    for step in range(3):
        alpha = ratio(norm, form(direction, energy))
        for i, p in enumerate(direction):
            answer[i] = answer[i] + alpha * p
        if step == 2:
            return answer
        image = apply_once(direction, zero)
        residual = [a - alpha * b for a, b in zip(residual + [zero], image)]
        norm_next = form(residual, gram)
        direction = [a + ratio(norm_next, norm) * b for a, b in zip(residual, direction + [zero])]
        norm = norm_next


def coefficients(m):
    power = steps_from(m[0:5], m[1:6], lambda a, zero: [zero] + a)
    shifted = steps_from(
        [m[0]] + m[6:10],
        [m[1]] + m[10:14],
        lambda a, zero: [p - q for p, q in zip(a + [zero], [zero] + a)],
    )
    turned = [shifted[0] + shifted[1] + shifted[2], -shifted[1] - 2.0 * shifted[2], shifted[2]]
    smooth = m[1] < 0.3 * m[0]
    return [jnp.where(smooth, a, b) * (1.0 / 6.0) for a, b in zip(power, turned)]


def project_kernel(
    sums_ref, vel_ref, fluid_ref, k0_ref, k1_ref, k2_ref, tag_ref, lane_ref, sub_ref, swap_ref,
    pressure_ref, out_ref, press, proj,
):
    total = jnp.sum(jnp.sum(sums_ref[...], axis=0), axis=1, keepdims=True)
    c = coefficients([jnp.broadcast_to(total[i : i + 1], (8, 128)) for i in range(14)])
    c = [jnp.concatenate([a, a, a], axis=0)[None] for a in c]
    for plane in range(3, 22):
        press[plane] = c[0] * k0_ref[plane] + c[1] * k1_ref[plane] + c[2] * k2_ref[plane]
    for x in range(CX):
        for h in range(2):
            pressure_ref[x, :, 128 * h : 128 * h + 128] = press[x + 4, h, 8:16]
    for x in range(CX + 1):
        p = press[x + 4]
        inner = p[:, 8:24]
        slopes = (
            press[x + 5, :, 8:24] - press[x + 3, :, 8:24],
            (y_shift(p, -1) - y_shift(p, 1))[:, 8:24],
            z_ahead(inner) - z_behind(inner),
        )
        fluid = fluid_ref[x + 4, :, 8:24]
        for d in range(3):
            field = fluid * (vel_ref[d, x + 4, :, 8:24] - 0.5 * slopes[d])
            for j, rows in enumerate((field[:, 0:8], y_shift(field, -1)[:, 0:8])):
                proj[x, d, j, 0] = rows
                proj[x, d, j, 1] = z_ahead(rows)
    for x in range(CX):
        code = tag_ref[0, 2 * x : 2 * x + 2] >> 15
        fx, fy, fz = fractions(code)
        wx, wy, wz = (1.0 - fx, fx), (1.0 - fy, fy), (1.0 - fz, fz)
        w = {(i, j, k): wx[i] * wy[j] * wz[k] for i in (0, 1) for j in (0, 1) for k in (0, 1)}
        for d in range(3):
            result = None
            for (i, j, k), weight in w.items():
                term = weight * proj[x + i, d, j, k]
                result = term if result is None else result + term
            out_ref[d, 2 * x : 2 * x + 2] = result
    follow_plan([(out_ref, d) for d in range(3)], lane_ref, sub_ref, swap_ref)


def project(*args):
    return kernel_call(
        project_kernel,
        "project",
        (of((CX, CY, 256)), of((3, TILES, 8, 128))),
        [(25, 2, 24, 128), (CX + 1, 3, 2, 2, 2, 8, 128)],
        args,
    )


def to_neighbour(slab, dx, dy):
    wide, high = lax.axis_size("gx"), lax.axis_size("gy")
    pairs = [
        (x * high + y, (x + dx) * high + y + dy)
        for x in range(max(0, -dx), min(wide, wide - dx))
        for y in range(max(0, -dy), min(high, high - dy))
    ]
    return lax.ppermute(slab, ("gx", "gy"), pairs)


def summed(sums, axis):
    count = lax.axis_size(axis)
    parts = [sums]
    for shift in range(1, count):
        parts.append(lax.ppermute(sums, axis, [(i, (i + shift) % count) for i in range(count)]))
    return functools.reduce(jnp.add, parts)


def local(cell_index, offset_code, particle_state, fluid_flags):
    places = [(axis, lax.axis_index(axis), lax.axis_size(axis)) for axis in ("gx", "gy")]
    keep = jnp.stack([(at + 1 < size).astype(F32) for _, at, size in places])
    cells, tag = to_cells(cell_index.reshape(256, 128), offset_code, particle_state)
    grid, rim, *slabs = deposit(cells, tag, fluid_flags)
    order = [WAYS.index(way) for way in ((0, 1), (0, -1), (1, 0), (-1, 0), (1, 1), (-1, -1), (1, -1), (-1, 1))]
    sent = {i: to_neighbour(slabs[i], *WAYS[i]) for i in order}
    arrived = [sent[WAYS.index((-dx, -dy))] for dx, dy in WAYS]
    plan = particle_plan(tag.reshape(256, 128))
    vel, fluid, k0, k1, k2, sums = krylov(keep, grid, rim, fluid_flags, arrived, plan[1])
    sums = summed(summed(sums, "gx"), "gy")[None]
    pressure, result = project(sums, vel, fluid, k0, k1, k2, tag, *plan)
    return pressure, result.reshape(1, 3, CELLS)


def solution(mesh):
    return jax.shard_map(
        local,
        mesh=mesh,
        in_specs=(
            P(("groups", "gx", "gy"), None),
            P(("groups", "gx", "gy"), None),
            P(("groups", "gx", "gy"), None, None),
            P(("groups", "gx"), "gy", None),
        ),
        out_specs=(P(("groups", "gx"), "gy", None), P(("groups", "gx", "gy"), None, None)),
        check_vma=False,
    )
```

```python
import functools
import math

import jax
import jax.numpy as jnp
from jax import lax
from jax.experimental import pallas as pl
from jax.experimental.pallas import tpu as pltpu
from jax.sharding import PartitionSpec as P

F32, I32 = jnp.float32, jnp.int32
CX, CY, CELLS = 16, 8, 32768
TILES = CELLS // 1024
LANE_RUNS, SUB_RUNS, SWAPS = 9, 3, 30 * 16


def take(x, index, axis):
    other = tuple(d for d in range(x.ndim) if d != axis)
    dims = lax.GatherDimensionNumbers(
        offset_dims=(),
        collapsed_slice_dims=(axis,),
        start_index_map=(axis,),
        operand_batching_dims=other,
        start_indices_batching_dims=other,
    )
    return lax.gather(
        x, index[..., None], dims, (1,) * x.ndim, mode=lax.GatherScatterMode.PROMISE_IN_BOUNDS
    )


def iota(shape, dim):
    return lax.broadcasted_iota(I32, shape, dim)


def sort_plan(tiles, lane_ref, sub_ref, swap_ref):
    lanes, subs = iota((64, 128), 1), iota((8, 128), 0)
    top = 0x7FFF

    def grouped(tiles):
        return [jnp.concatenate(tiles[8 * i : 8 * i + 8], axis=0) for i in range(4)]

    def partner(x, index, stride, axis):
        if 2 * stride == (128, 8)[axis == 0]:
            return pltpu.roll(x, stride, axis)
        return take(x, index ^ stride, axis)

    def ordered(low, a, b):
        return jnp.where(low, jnp.minimum(a, b), jnp.maximum(a, b))

    def lane_steps(groups, stride):
        while stride:
            low = lanes & stride == 0
            other = [partner(g, lanes, stride, 1) for g in groups]
            groups = [ordered(low, g, o) for g, o in zip(groups, other)]
            stride //= 2
        return groups

    def record(run, groups):
        for i, g in enumerate(groups):
            lane_ref[run, 64 * i : 64 * i + 64] = g & 127
        return [groups[i // 8][8 * (i % 8) : 8 * (i % 8) + 8] >> 7 for i in range(TILES)]

    groups = [(g << 7) | lanes for g in grouped(tiles)]
    for phase in range(1, 7):
        turn = jnp.where(lanes & (1 << phase) != 0, top << 7, 0)
        groups = [g ^ turn for g in groups]
        groups = lane_steps(groups, 1 << (phase - 1))
        groups = [g ^ turn for g in groups]
    turn = jnp.where(iota((64, 128), 0) & 8 != 0, top << 7, 0)
    groups = lane_steps([g ^ turn for g in groups], 64)
    tiles = record(0, groups)
    tiles = [t ^ top if i & 1 else t for i, t in enumerate(tiles)]

    swap = 0
    for phase in range(8, 16):
        if phase < 12:
            turns = [top if i >> (phase - 7) & 1 else 0 for i in range(TILES)]
        elif phase < 15:
            turns = [jnp.where(subs & (1 << (phase - 12)) != 0, top, 0)] * TILES
        else:
            turns = [0] * TILES
        tiles = [t ^ f for t, f in zip(tiles, turns)]
        if phase > 12:
            tiles = [(t << 3) | subs for t in tiles]
            stride = 1 << (phase - 13)
            while stride:
                low = subs & stride == 0
                other = [partner(t, subs, stride, 0) for t in tiles]
                tiles = [ordered(low, t, o) for t, o in zip(tiles, other)]
                stride //= 2
            for i, t in enumerate(tiles):
                sub_ref[phase - 13, 8 * i : 8 * i + 8] = t & 7
            tiles = [t >> 3 for t in tiles]
        hop = 1 << (min(phase, 12) - 8)
        while hop:
            for i in range(TILES):
                if i & hop == 0:
                    a, b = tiles[i], tiles[i + hop]
                    swap_ref[8 * swap : 8 * swap + 8] = jnp.where(a > b, 1, 0)
                    swap += 1
                    tiles[i], tiles[i + hop] = jnp.minimum(a, b), jnp.maximum(a, b)
            hop //= 2
        groups = [(g << 7) | lanes for g in grouped(tiles)]
        tiles = record(phase - 7, lane_steps(groups, 64))
        tiles = [t ^ f for t, f in zip(tiles, turns)]
    return tiles


def follow_plan(stages, lane_ref, sub_ref, swap_ref):
    def crossings(hops, before):
        out = {}
        for hop in hops:
            for i in range(TILES):
                if i & hop == 0:
                    out[hop, i] = before
                    before += 1
        return out, before

    def pass_over(sets, work):
        for members in sets:
            moved = [{i: ref[c, i] for i in members} for ref, c in stages]
            work(members, moved)
            for (ref, c), tiles in zip(stages, moved):
                for i, t in tiles.items():
                    ref[c, i] = t

    def gathered(ref, run, axis, members, moved):
        for i in members:
            index = ref[run, 8 * i : 8 * i + 8]
            for tiles in moved:
                tiles[i] = take(tiles[i], index, axis)

    def exchanged(hops, number, members, moved):
        for hop in hops:
            for i in members:
                if i & hop == 0:
                    at = 8 * number[hop, i]
                    crossed = swap_ref[at : at + 8] != 0
                    for tiles in moved:
                        a, b = tiles[i], tiles[i + hop]
                        tiles[i], tiles[i + hop] = jnp.where(crossed, b, a), jnp.where(crossed, a, b)

    eights = [range(8 * g, 8 * g + 8) for g in range(4)]
    numbers, before = {}, 0
    for phase in range(8, 16):
        hops = [1 << k for k in reversed(range(min(phase, 12) - 7))]
        numbers[phase], before = crossings(hops, before)

    def first(members, moved):
        gathered(lane_ref, 0, 1, members, moved)
        for phase in (8, 9, 10):
            exchanged([4, 2, 1][10 - phase :], numbers[phase], members, moved)
            gathered(lane_ref, phase - 7, 1, members, moved)

    pass_over(eights, first)
    for phase in range(11, 16):
        wide = [16, 8] if phase > 11 else [8]
        reach = 32 if phase > 11 else 16
        sets = [range(low + k, low + reach, 8) for low in range(0, 32, reach) for k in range(8)]

        def across(members, moved):
            if phase > 12:
                gathered(sub_ref, phase - 13, 0, members, moved)
            exchanged(wide, numbers[phase], members, moved)

        def within(members, moved):
            exchanged([4, 2, 1], numbers[phase], members, moved)
            gathered(lane_ref, phase - 7, 1, members, moved)

        pass_over(sets, across)
        pass_over(eights, within)


def plan_shapes():
    return [(LANE_RUNS, 256, 128), (SUB_RUNS, 256, 128), (8 * SWAPS, 128)]


def plan_scratch():
    return [pltpu.VMEM(shape, I32) for shape in plan_shapes()]


def split_tiles(array):
    return [array[8 * i : 8 * i + 8] for i in range(TILES)]


def z_behind(a):
    r = pltpu.roll(a, 1, 2)
    fill = jnp.concatenate([jnp.zeros_like(r[:1]), r[:1]], axis=0)
    return jnp.where(iota(a.shape, 2) == 0, fill, r)


def z_ahead(a):
    r = pltpu.roll(a, 127, 2)
    fill = jnp.concatenate([r[1:], jnp.zeros_like(r[:1])], axis=0)
    return jnp.where(iota(a.shape, 2) == 127, fill, r)


def y_shift(a, steps):
    return jnp.stack([pltpu.roll(a[h], steps % a.shape[1], 0) for h in range(2)])


def fractions(code):
    return [((code >> shift & 3).astype(F32) + 0.5) * 0.25 for shift in (0, 2, 4)]


PLANES = {1: range(12, 17), 0: range(17), -1: range(5)}
ROWS = {1: range(4, 9), -1: range(5)}


def reach(place, last):
    return max(0, -place, place - last)


def pieces(dx, dy):
    at, out = 0, []
    for plane in PLANES[dx]:
        far_x = reach(plane - dx * CX, CX)
        for field in range(8):
            rows = []
            for row in ROWS[dy] if dy else range(-4, 13):
                far_y = reach(row - dy * CY, CY)
                read = [
                    max(far_x - 1, 0) + far_y <= 3,
                    far_x + max(far_y - 1, 0) <= 3,
                    far_x + far_y <= 3,
                ]
                shared = plane in (0, CX) or (dy != 0 and row in (0, CY))
                if field == 7:
                    wanted = read[2] and plane < CX and (row < CY or not dy)
                elif field == 0:
                    wanted = shared and any(read)
                else:
                    wanted = read[(field - 1) % 3] and shared == (field < 4)
                if wanted:
                    rows.append(row)
            while rows:
                count = 1
                while count < len(rows) and rows[count] == rows[0] + count:
                    count += 1
                for half in range(2):
                    out.append((field, plane, half, rows[0], count, at))
                    at += count
                rows = rows[count:]
    return out, -(-at // 8) * 8


def slab_shape(dx, dy):
    return of((pieces(dx, dy)[1], 128))


def clear_end(ref, listed):
    used = listed[-1][4] + listed[-1][5]
    if used < ref.shape[0]:
        ref[used:] = jnp.zeros((ref.shape[0] - used, 128), F32)


def particle_plan_kernel(tag_ref, lane_ref, sub_ref, swap_ref):
    k = tag_ref[...] & 0x7FFF
    key = ((k & 0x380) << 5) | ((k & 0x7C00) >> 3) | (k & 0x7F)
    sort_plan(split_tiles(key), lane_ref, sub_ref, swap_ref)


def particle_plan(tag):
    outs = [of(shape, I32) for shape in plan_shapes()]
    return kernel_call(particle_plan_kernel, "particle_plan", outs, [], (tag,), flops=10**7)


def to_cells_kernel(cell_ref, code_ref, state_ref, cells_ref, tag_ref, code, lane_ref, sub_ref, swap_ref, done):
    arrivals = [
        pltpu.make_async_copy(code_ref, code, done.at[0]),
        pltpu.make_async_copy(state_ref, cells_ref, done.at[1]),
    ]
    for arrival in arrivals:
        arrival.start()
    k = cell_ref[...]
    key = ((k & 0x700) << 4) | ((k & 0x7800) >> 3) | (k & 0xFF)
    sort_plan(split_tiles(key), lane_ref, sub_ref, swap_ref)
    for arrival in arrivals:
        arrival.wait()
    tag_ref[0] = (code[...] << 15) | (iota((TILES, 8, 128), 0) * 8 + iota((TILES, 8, 128), 1)) * 128 + iota(
        (TILES, 8, 128), 2
    )
    for quad in range(3):
        stages = [(cells_ref, 4 * quad + c) for c in range(4)]
        follow_plan(stages + [(tag_ref, 0)] * (quad == 0), lane_ref, sub_ref, swap_ref)


def to_cells(cell, code, state):
    anywhere = pl.BlockSpec(memory_space=pltpu.HBM)
    return kernel_call(
        to_cells_kernel,
        "to_cells",
        (of((12, TILES, 8, 128)), of((1, TILES, 8, 128), I32)),
        [pltpu.VMEM(shape, I32) for shape in [(TILES, 8, 128)] + plan_shapes()] + [pltpu.SemaphoreType.DMA((2,))],
        (cell, code.reshape(TILES, 8, 128), state.reshape(12, TILES, 8, 128)),
        [vmem(), anywhere, anywhere],
        flops=10**7,
    )


def deposit_kernel(cells_ref, tag_ref, flag_ref, grid_ref, rim_ref, up_ref, down_ref):
    wanted = {}
    for dy, ref in ((1, up_ref), (-1, down_ref)):
        listed = pieces(0, dy)[0]
        clear_end(ref, listed)
        for field, plane, half, first, count, at in listed:
            wanted.setdefault((field, plane), []).append((ref, half, first, count, at))

    def hand_out(field, plane, main, rim):
        for ref, half, first, count, at in wanted.get((field, plane), ()):
            inside = min(count, CY - first)
            if inside > 0:
                ref[at : at + inside] = main[half, first : first + inside]
            if inside < count:
                ref[at + count - 1 : at + count] = rim[half, 0:1]

    first_row = iota((2, 8, 128), 1) == 0
    before = None
    for x in range(CX + 1):
        here = []
        if x < CX:
            code = tag_ref[0, 2 * x : 2 * x + 2] >> 15
            fx, fy, fz = fractions(code)
            wx, wy, wz = (1.0 - fx, fx), (1.0 - fy, fy), (1.0 - fz, fz)
            w = {(i, j, k): wx[i] * wy[j] * wz[k] for i in (0, 1) for j in (0, 1) for k in (0, 1)}
            here.append(w)
            for comp in range(3):
                v, c0, c1, c2 = [
                    cells_ref[c, 2 * x : 2 * x + 2]
                    for c in (comp, 3 + 3 * comp, 4 + 3 * comp, 5 + 3 * comp)
                ]
                base = v - c0 * fx - c1 * fy - c2 * fz
                terms = {}
                for i in (0, 1):
                    a = base + c0 if i else base
                    for j in (0, 1):
                        b = a + c1 if j else a
                        for k in (0, 1):
                            terms[i, j, k] = w[i, j, k] * (b + c2 if k else b)
                here.append(terms)
        for f in range(4):
            s = {}
            for j in (0, 1):
                for k in (0, 1):
                    parts = []
                    if x < CX:
                        parts.append(here[f][0, j, k])
                    if x > 0:
                        parts.append(before[f][1, j, k])
                    s[j, k] = sum(parts[1:], parts[0])
            near, far = [s[j, 0] + z_behind(s[j, 1]) for j in (0, 1)]
            turned = y_shift(far, 1)
            main = near + jnp.where(first_row, 0.0, turned)
            rim = jnp.where(first_row, turned, 0.0)
            grid_ref[f, x], rim_ref[f, x] = main, rim
            hand_out(f, x, main, rim)
            if f == 0:
                inverse = 1.0 / jnp.maximum(main, 0.5)
            else:
                hand_out(3 + f, x, main * inverse, None)
        if x < CX:
            flags = jnp.stack([flag_ref[x, :, 128 * h : 128 * h + 128] for h in range(2)])
            hand_out(7, x, flags.astype(F32), None)
        before = here


def tiled_bytes(shape):
    *outer, rows, columns = shape
    return 4 * math.prod(outer) * (-(-rows // 8) * 8) * (-(-columns // 128) * 128)


def kernel_call(body, name, outs, scratch, args, in_specs=None, flops=0):
    scratch = [x if hasattr(x, "dtype") else pltpu.VMEM(x, F32) for x in scratch]
    size = sum(tiled_bytes(x.shape) for x in (*args, *outs, *scratch) if len(x.shape) > 1)
    return pl.pallas_call(
        body,
        out_shape=outs,
        **({} if in_specs is None else dict(in_specs=in_specs)),
        scratch_shapes=scratch,
        compiler_params=pltpu.CompilerParams(vmem_limit_bytes=size + 4 * 2**20),
        cost_estimate=pl.CostEstimate(flops=flops, bytes_accessed=size, transcendentals=0),
        name=name,
    )(*args)


def of(shape, kind=F32):
    return jax.ShapeDtypeStruct(shape, kind)


def deposit(cells, tag, flags):
    grid = of((4, CX + 1, 2, 8, 128))
    return kernel_call(
        deposit_kernel, "deposit", [grid, grid, slab_shape(0, 1), slab_shape(0, -1)], [], (cells, tag, flags)
    )


def smem():
    return pl.BlockSpec(memory_space=pltpu.SMEM)


def vmem():
    return pl.BlockSpec(memory_space=pltpu.VMEM)


def add_rows(ref, place, row, rows):
    at = (*place, slice(row, row + rows.shape[0]))
    ref[at] = ref[at] + rows


def widen_kernel(
    keep_ref, grid_ref, rim_ref, low_ref, high_ref, flag_ref, after_ref, vel_ref, edge_ref, fluid_ref, up_ref, down_ref, ext
):
    zero = jnp.zeros((2, 8, 128), F32)
    for x in range(CX + 1):
        for f in range(4):
            ext[f, x, :, 0:8] = zero
            ext[f, x, :, 8:16] = grid_ref[f, x]
            ext[f, x, :, 16:24] = rim_ref[f, x]
        if x < CX:
            fluid_ref[x, :, 0:8] = zero
            fluid_ref[x, :, 16:24] = zero
            for h in range(2):
                fluid_ref[x, h, 8:16] = flag_ref[x, :, 128 * h : 128 * h + 128].astype(F32)
    arrived = []
    for dy, ref in ((1, low_ref), (-1, high_ref)):
        for field, x, half, first, count, at in pieces(0, dy)[0]:
            arrived.append((field, x, half, first - dy * CY + 8, ref[at : at + count]))
    for field, x, half, row, rows in arrived:
        if field < 4:
            add_rows(ext, (field, x, half), row, rows)
        elif field == 7:
            fluid_ref[x, half, row : row + rows.shape[0]] = rows
    for f in range(4):
        for x in range(CX + 1):
            ext[f, x, :, 16:24] = keep_ref[1] * ext[f, x, :, 16:24]
        edge_ref[f, 0], edge_ref[f, 1] = ext[f, 0], ext[f, CX]
    for x in range(1, CX):
        inverse = 1.0 / jnp.maximum(ext[0, x], 0.5)
        for d in range(3):
            vel_ref[d, x] = ext[1 + d, x] * inverse
    for field, x, half, row, rows in arrived:
        if 4 <= field < 7:
            vel_ref[field - 4, x, half, row : row + rows.shape[0]] = rows
    for dx, ref in ((1, up_ref), (-1, down_ref)):
        listed = pieces(dx, 0)[0]
        clear_end(ref, listed)
        for field, x, half, first, count, at in listed:
            source = ext.at[field] if field < 4 else fluid_ref if field == 7 else vel_ref.at[field - 4]
            ref[at : at + count] = source[x, half, first + 8 : first + 8 + count]


def widen(keep, *args):
    wide = (CX, 2, 24, 128)
    return kernel_call(
        widen_kernel,
        "widen",
        (of((3, *wide)), of((4, 2, 2, 24, 128)), of(wide), slab_shape(1, 0), slab_shape(-1, 0)),
        [(4, CX + 1, 2, 24, 128)],
        (keep, *args),
        [smem()] + [vmem()] * 5 + [pl.BlockSpec(memory_space=pl.ANY)],
    )


def krylov_kernel(
    keep_ref, near_ref, edge_ref, flag_ref, low_ref, high_ref, vel_ref, fluid_ref, k0_ref, k1_ref, k2_ref, sums_ref, edge
):
    zero = jnp.zeros((2, 24, 128), F32)
    for plane in range(25):
        inner = 4 < plane < 20
        for d in range(3):
            vel_ref[d, plane] = near_ref[d, plane - 4] if inner else zero
        fluid_ref[plane] = flag_ref[plane - 4] if 4 <= plane < 20 else zero
    for f in range(4):
        edge[f, 0], edge[f, 1] = edge_ref[f, 0], edge_ref[f, 1]
    for dx, ref in ((1, low_ref), (-1, high_ref)):
        for field, x, half, first, count, at in pieces(dx, 0)[0]:
            rows, row, plane = ref[at : at + count], first + 8, x - dx * CX + 4
            if field < 4:
                add_rows(edge, (field, (plane - 4) // CX, half), row, rows)
            elif field == 7:
                fluid_ref[plane, half, row : row + count] = rows
            else:
                vel_ref[field - 4, plane, half, row : row + count] = rows
    for side, plane, keep in ((0, 4, 1.0), (1, 20, keep_ref[0])):
        inverse = keep / jnp.maximum(edge[0, side], 0.5)
        for d in range(3):
            vel_ref[d, plane] = edge[1 + d, side] * inverse
    for plane in range(1, 24):
        vy, vz = vel_ref[1, plane], vel_ref[2, plane]
        divergence = (
            0.5 * (vel_ref[0, plane + 1] - vel_ref[0, plane - 1])
            + 0.5 * (y_shift(vy, -1) - y_shift(vy, 1))
            + 0.5 * (z_ahead(vz) - z_behind(vz))
        )
        k0_ref[plane] = -fluid_ref[plane] * divergence

    def applied(ref, plane):
        a = ref[plane]
        beside = (
            ref[plane + 1] + ref[plane - 1] + y_shift(a, 1) + y_shift(a, -1) + z_ahead(a) + z_behind(a)
        )
        return fluid_ref[plane] * (a - beside * (1.0 / 6.0))

    for plane in range(2, 23):
        k1_ref[plane] = applied(k0_ref, plane)
    for plane in range(3, 22):
        k2_ref[plane] = applied(k1_ref, plane)
    totals = [jnp.zeros((2, 8, 128), F32)] * 14
    for plane in range(4, 20):
        k0, k1, k2 = [ref[plane, :, 8:16] for ref in (k0_ref, k1_ref, k2_ref)]
        k3 = applied(k2_ref, plane)[:, 8:16]
        u1, w1 = k0 - k1, k1 - k2
        u2 = u1 - w1
        w2 = w1 - (k2 - k3)
        pairs = (
            (k0, k0), (k0, k1), (k1, k1), (k1, k2), (k2, k2), (k2, k3),
            (k0, u1), (u1, u1), (u1, u2), (u2, u2), (k0, w1), (u1, w1), (u1, w2), (u2, w2),
        )
        totals = [t + a * b for t, (a, b) in zip(totals, pairs)]
    for i, t in enumerate(totals):
        sums_ref[i : i + 1] = jnp.sum(t[0] + t[1], axis=0, keepdims=True)
    sums_ref[14:16] = jnp.zeros((2, 128), F32)


def krylov(keep, *args):
    return kernel_call(
        krylov_kernel,
        "krylov",
        (of((3, 25, 2, 24, 128)),) + (of((25, 2, 24, 128)),) * 4 + (of((16, 128)),),
        [(4, 2, 2, 24, 128)],
        (keep, *args),
        [smem()] + [vmem()] * 5,
    )


def steps_from(gram, energy, apply_once):
    def form(a, table):
        total = None
        for i, p in enumerate(a):
            for j, q in enumerate(a):
                if p is not None and q is not None:
                    term = p * q * table[i + j]
                    total = term if total is None else total + term
        return total

    def ratio(a, b):
        return jnp.where(b > 0.0, a / jnp.where(b > 0.0, b, 1.0), 0.0)

    one, zero = jnp.ones_like(gram[0]), jnp.zeros_like(gram[0])
    residual, direction, answer = [one], [one], [zero] * 3
    norm = gram[0]
    for step in range(3):
        alpha = ratio(norm, form(direction, energy))
        for i, p in enumerate(direction):
            answer[i] = answer[i] + alpha * p
        if step == 2:
            return answer
        image = apply_once(direction, zero)
        residual = [a - alpha * b for a, b in zip(residual + [zero], image)]
        norm_next = form(residual, gram)
        direction = [a + ratio(norm_next, norm) * b for a, b in zip(residual, direction + [zero])]
        norm = norm_next


def coefficients(m):
    power = steps_from(m[0:5], m[1:6], lambda a, zero: [zero] + a)
    shifted = steps_from(
        [m[0]] + m[6:10],
        [m[1]] + m[10:14],
        lambda a, zero: [p - q for p, q in zip(a + [zero], [zero] + a)],
    )
    turned = [shifted[0] + shifted[1] + shifted[2], -shifted[1] - 2.0 * shifted[2], shifted[2]]
    smooth = m[1] < 0.3 * m[0]
    return [jnp.where(smooth, a, b) * (1.0 / 6.0) for a, b in zip(power, turned)]


def project_kernel(
    sums_ref, vel_ref, fluid_ref, k0_ref, k1_ref, k2_ref, tag_ref, lane_ref, sub_ref, swap_ref,
    pressure_ref, out_ref, press, proj,
):
    total = jnp.sum(jnp.sum(sums_ref[...], axis=0), axis=1, keepdims=True)
    c = coefficients([jnp.broadcast_to(total[i : i + 1], (8, 128)) for i in range(14)])
    c = [jnp.concatenate([a, a, a], axis=0)[None] for a in c]
    for plane in range(3, 22):
        press[plane] = c[0] * k0_ref[plane] + c[1] * k1_ref[plane] + c[2] * k2_ref[plane]
    for x in range(CX):
        for h in range(2):
            pressure_ref[x, :, 128 * h : 128 * h + 128] = press[x + 4, h, 8:16]
    for x in range(CX + 1):
        p = press[x + 4]
        inner = p[:, 8:24]
        slopes = (
            press[x + 5, :, 8:24] - press[x + 3, :, 8:24],
            (y_shift(p, -1) - y_shift(p, 1))[:, 8:24],
            z_ahead(inner) - z_behind(inner),
        )
        fluid = fluid_ref[x + 4, :, 8:24]
        for d in range(3):
            field = fluid * (vel_ref[d, x + 4, :, 8:24] - 0.5 * slopes[d])
            for j, rows in enumerate((field[:, 0:8], y_shift(field, -1)[:, 0:8])):
                proj[x, d, j, 0] = rows
                proj[x, d, j, 1] = z_ahead(rows)
    for x in range(CX):
        code = tag_ref[0, 2 * x : 2 * x + 2] >> 15
        fx, fy, fz = fractions(code)
        wx, wy, wz = (1.0 - fx, fx), (1.0 - fy, fy), (1.0 - fz, fz)
        w = {(i, j, k): wx[i] * wy[j] * wz[k] for i in (0, 1) for j in (0, 1) for k in (0, 1)}
        for d in range(3):
            result = None
            for (i, j, k), weight in w.items():
                term = weight * proj[x + i, d, j, k]
                result = term if result is None else result + term
            out_ref[d, 2 * x : 2 * x + 2] = result
    follow_plan([(out_ref, d) for d in range(3)], lane_ref, sub_ref, swap_ref)


def project(*args):
    return kernel_call(
        project_kernel,
        "project",
        (of((CX, CY, 256)), of((3, TILES, 8, 128))),
        [(25, 2, 24, 128), (CX + 1, 3, 2, 2, 2, 8, 128)],
        args,
    )


def neighbours(up, down, axis):
    pairs = [(i, i + 1) for i in range(lax.axis_size(axis) - 1)]
    return lax.ppermute(up, axis, pairs), lax.ppermute(down, axis, [(b, a) for a, b in pairs])


def summed(sums, axis):
    count = lax.axis_size(axis)
    parts = [sums]
    for shift in range(1, count):
        parts.append(lax.ppermute(sums, axis, [(i, (i + shift) % count) for i in range(count)]))
    return functools.reduce(jnp.add, parts)


def local(cell_index, offset_code, particle_state, fluid_flags):
    places = [(axis, lax.axis_index(axis), lax.axis_size(axis)) for axis in ("gx", "gy")]
    keep = jnp.stack([(at + 1 < size).astype(F32) for _, at, size in places])
    cells, tag = to_cells(cell_index.reshape(256, 128), offset_code, particle_state)
    grid, rim, up, down = deposit(cells, tag, fluid_flags)
    low, high = neighbours(up, down, "gy")
    plan = particle_plan(tag.reshape(256, 128))
    near, edge, flags, up, down = widen(keep, grid, rim, low, high, fluid_flags, plan[1])
    low, high = neighbours(up, down, "gx")
    vel, fluid, k0, k1, k2, sums = krylov(keep, near, edge, flags, low, high)
    sums = summed(summed(sums, "gx"), "gy")[None]
    pressure, result = project(sums, vel, fluid, k0, k1, k2, tag, *plan)
    return pressure, result.reshape(1, 3, CELLS)


def solution(mesh):
    return jax.shard_map(
        local,
        mesh=mesh,
        in_specs=(
            P(("groups", "gx", "gy"), None),
            P(("groups", "gx", "gy"), None),
            P(("groups", "gx", "gy"), None, None),
            P(("groups", "gx"), "gy", None),
        ),
        out_specs=(P(("groups", "gx"), "gy", None), P(("groups", "gx", "gy"), None, None)),
        check_vma=False,
    )
```

```python
import functools
import math

import jax
import jax.numpy as jnp
from jax import lax
from jax.experimental import pallas as pl
from jax.experimental.pallas import tpu as pltpu
from jax.sharding import PartitionSpec as P

F32, I32 = jnp.float32, jnp.int32
CX, CY, CELLS = 16, 8, 32768
TILES = CELLS // 1024
LANE_RUNS, SUB_RUNS, SWAPS = 9, 3, 30 * 16


def take(x, index, axis):
    other = tuple(d for d in range(x.ndim) if d != axis)
    dims = lax.GatherDimensionNumbers(
        offset_dims=(),
        collapsed_slice_dims=(axis,),
        start_index_map=(axis,),
        operand_batching_dims=other,
        start_indices_batching_dims=other,
    )
    return lax.gather(
        x, index[..., None], dims, (1,) * x.ndim, mode=lax.GatherScatterMode.PROMISE_IN_BOUNDS
    )


def iota(shape, dim):
    return lax.broadcasted_iota(I32, shape, dim)


def sort_plan(tiles, lane_ref, sub_ref, swap_ref):
    lanes, subs = iota((64, 128), 1), iota((8, 128), 0)
    top = 0x7FFF

    def grouped(tiles):
        return [jnp.concatenate(tiles[8 * i : 8 * i + 8], axis=0) for i in range(4)]

    def partner(x, index, stride, axis):
        if 2 * stride == (128, 8)[axis == 0]:
            return pltpu.roll(x, stride, axis)
        return take(x, index ^ stride, axis)

    def ordered(low, a, b):
        return jnp.where(low, jnp.minimum(a, b), jnp.maximum(a, b))

    def lane_steps(groups, stride):
        while stride:
            low = lanes & stride == 0
            other = [partner(g, lanes, stride, 1) for g in groups]
            groups = [ordered(low, g, o) for g, o in zip(groups, other)]
            stride //= 2
        return groups

    def record(run, groups):
        for i, g in enumerate(groups):
            lane_ref[run, 64 * i : 64 * i + 64] = g & 127
        return [groups[i // 8][8 * (i % 8) : 8 * (i % 8) + 8] >> 7 for i in range(TILES)]

    groups = [(g << 7) | lanes for g in grouped(tiles)]
    for phase in range(1, 7):
        turn = jnp.where(lanes & (1 << phase) != 0, top << 7, 0)
        groups = [g ^ turn for g in groups]
        groups = lane_steps(groups, 1 << (phase - 1))
        groups = [g ^ turn for g in groups]
    turn = jnp.where(iota((64, 128), 0) & 8 != 0, top << 7, 0)
    groups = lane_steps([g ^ turn for g in groups], 64)
    tiles = record(0, groups)
    tiles = [t ^ top if i & 1 else t for i, t in enumerate(tiles)]

    swap = 0
    for phase in range(8, 16):
        if phase < 12:
            turns = [top if i >> (phase - 7) & 1 else 0 for i in range(TILES)]
        elif phase < 15:
            turns = [jnp.where(subs & (1 << (phase - 12)) != 0, top, 0)] * TILES
        else:
            turns = [0] * TILES
        tiles = [t ^ f for t, f in zip(tiles, turns)]
        if phase > 12:
            tiles = [(t << 3) | subs for t in tiles]
            stride = 1 << (phase - 13)
            while stride:
                low = subs & stride == 0
                other = [partner(t, subs, stride, 0) for t in tiles]
                tiles = [ordered(low, t, o) for t, o in zip(tiles, other)]
                stride //= 2
            for i, t in enumerate(tiles):
                sub_ref[phase - 13, 8 * i : 8 * i + 8] = t & 7
            tiles = [t >> 3 for t in tiles]
        hop = 1 << (min(phase, 12) - 8)
        while hop:
            for i in range(TILES):
                if i & hop == 0:
                    a, b = tiles[i], tiles[i + hop]
                    swap_ref[8 * swap : 8 * swap + 8] = jnp.where(a > b, 1, 0)
                    swap += 1
                    tiles[i], tiles[i + hop] = jnp.minimum(a, b), jnp.maximum(a, b)
            hop //= 2
        groups = [(g << 7) | lanes for g in grouped(tiles)]
        tiles = record(phase - 7, lane_steps(groups, 64))
        tiles = [t ^ f for t, f in zip(tiles, turns)]
    return tiles


def follow_plan(stages, lane_ref, sub_ref, swap_ref, sources=None):
    def crossings(hops, before):
        out = {}
        for hop in hops:
            for i in range(TILES):
                if i & hop == 0:
                    out[hop, i] = before
                    before += 1
        return out, before

    def pass_over(sets, work, sources=stages):
        for members in sets:
            moved = [{i: ref[c, i] for i in members} for ref, c in sources]
            work(members, moved)
            for (ref, c), tiles in zip(stages, moved):
                for i, t in tiles.items():
                    ref[c, i] = t

    def gathered(ref, run, axis, members, moved):
        for i in members:
            index = ref[run, 8 * i : 8 * i + 8]
            for tiles in moved:
                tiles[i] = take(tiles[i], index, axis)

    def exchanged(hops, number, members, moved):
        for hop in hops:
            for i in members:
                if i & hop == 0:
                    at = 8 * number[hop, i]
                    crossed = swap_ref[at : at + 8] != 0
                    for tiles in moved:
                        a, b = tiles[i], tiles[i + hop]
                        tiles[i], tiles[i + hop] = jnp.where(crossed, b, a), jnp.where(crossed, a, b)

    eights = [range(8 * g, 8 * g + 8) for g in range(4)]
    numbers, before = {}, 0
    for phase in range(8, 16):
        hops = [1 << k for k in reversed(range(min(phase, 12) - 7))]
        numbers[phase], before = crossings(hops, before)

    def first(members, moved):
        gathered(lane_ref, 0, 1, members, moved)
        for phase in (8, 9, 10):
            exchanged([4, 2, 1][10 - phase :], numbers[phase], members, moved)
            gathered(lane_ref, phase - 7, 1, members, moved)

    pass_over(eights, first, sources or stages)
    for phase in range(11, 16):
        wide = [16, 8] if phase > 11 else [8]
        reach = 32 if phase > 11 else 16
        sets = [range(low + k, low + reach, 8) for low in range(0, 32, reach) for k in range(8)]

        def across(members, moved):
            if phase > 12:
                gathered(sub_ref, phase - 13, 0, members, moved)
            exchanged(wide, numbers[phase], members, moved)

        def within(members, moved):
            exchanged([4, 2, 1], numbers[phase], members, moved)
            gathered(lane_ref, phase - 7, 1, members, moved)

        pass_over(sets, across)
        pass_over(eights, within)


def plan_shapes():
    return [(LANE_RUNS, 256, 128), (SUB_RUNS, 256, 128), (8 * SWAPS, 128)]


def plan_scratch():
    return [pltpu.VMEM(shape, I32) for shape in plan_shapes()]


def split_tiles(array):
    return [array[8 * i : 8 * i + 8] for i in range(TILES)]


def z_behind(a):
    r = pltpu.roll(a, 1, 2)
    fill = jnp.concatenate([jnp.zeros_like(r[:1]), r[:1]], axis=0)
    return jnp.where(iota(a.shape, 2) == 0, fill, r)


def z_ahead(a):
    r = pltpu.roll(a, 127, 2)
    fill = jnp.concatenate([r[1:], jnp.zeros_like(r[:1])], axis=0)
    return jnp.where(iota(a.shape, 2) == 127, fill, r)


def y_shift(a, steps):
    return jnp.stack([pltpu.roll(a[h], steps % a.shape[1], 0) for h in range(2)])


def fractions(code):
    return [((code >> shift & 3).astype(F32) + 0.5) * 0.25 for shift in (0, 2, 4)]


PLANES = {1: range(12, 17), 0: range(17), -1: range(5)}
ROWS = {1: range(4, 9), -1: range(5)}


def reach(place, last):
    return max(0, -place, place - last)


def pieces(dx, dy):
    at, out = 0, []
    for plane in PLANES[dx]:
        far_x = reach(plane - dx * CX, CX)
        for field in range(8):
            rows = []
            for row in ROWS[dy] if dy else range(-4, 13):
                far_y = reach(row - dy * CY, CY)
                read = [
                    max(far_x - 1, 0) + far_y <= 3,
                    far_x + max(far_y - 1, 0) <= 3,
                    far_x + far_y <= 3,
                ]
                shared = plane in (0, CX) or (dy != 0 and row in (0, CY))
                if field == 7:
                    wanted = read[2] and plane < CX and (row < CY or not dy)
                elif field == 0:
                    wanted = shared and any(read)
                else:
                    wanted = read[(field - 1) % 3] and shared == (field < 4)
                if wanted:
                    rows.append(row)
            while rows:
                count = 1
                while count < len(rows) and rows[count] == rows[0] + count:
                    count += 1
                for half in range(2):
                    out.append((field, plane, half, rows[0], count, at))
                    at += count
                rows = rows[count:]
    return out, -(-at // 8) * 8


def slab_shape(dx, dy):
    return of((pieces(dx, dy)[1], 128))


def clear_end(ref, listed):
    used = listed[-1][4] + listed[-1][5]
    if used < ref.shape[0]:
        ref[used:] = jnp.zeros((ref.shape[0] - used, 128), F32)


def particle_plan_kernel(tag_ref, lane_ref, sub_ref, swap_ref):
    k = tag_ref[...] & 0x7FFF
    key = ((k & 0x380) << 5) | ((k & 0x7C00) >> 3) | (k & 0x7F)
    sort_plan(split_tiles(key), lane_ref, sub_ref, swap_ref)


def particle_plan(tag):
    outs = [of(shape, I32) for shape in plan_shapes()]
    return kernel_call(particle_plan_kernel, "particle_plan", outs, [], (tag,), flops=10**7)


def cell_plan_kernel(cell_ref, lane_ref, sub_ref, swap_ref):
    k = cell_ref[...]
    key = ((k & 0x700) << 4) | ((k & 0x7800) >> 3) | (k & 0xFF)
    sort_plan(split_tiles(key), lane_ref, sub_ref, swap_ref)


def cell_plan(cell):
    outs = [of(shape, I32) for shape in plan_shapes()]
    return kernel_call(cell_plan_kernel, "cell_plan", outs, [], (cell,), flops=7 * 10**9)


def to_cells_kernel(code_ref, state_ref, lane_ref, sub_ref, swap_ref, cells_ref, tag_ref):
    shape = (TILES, 8, 128)
    tag_ref[0] = (code_ref[...] << 15) | (iota(shape, 0) * 8 + iota(shape, 1)) * 128 + iota(shape, 2)
    for quad in range(3):
        channels = range(4 * quad, 4 * quad + 4)
        stages = [(cells_ref, c) for c in channels] + [(tag_ref, 0)] * (quad == 0)
        sources = [(state_ref, c) for c in channels] + [(tag_ref, 0)] * (quad == 0)
        follow_plan(stages, lane_ref, sub_ref, swap_ref, sources)


def to_cells(code, state, plan):
    return kernel_call(
        to_cells_kernel,
        "to_cells",
        (of((12, TILES, 8, 128)), of((1, TILES, 8, 128), I32)),
        [],
        (code.reshape(TILES, 8, 128), state.reshape(12, TILES, 8, 128), *plan),
        flops=10**7,
    )


def deposit_kernel(cells_ref, tag_ref, flag_ref, grid_ref, rim_ref, up_ref, down_ref):
    wanted = {}
    for dy, ref in ((1, up_ref), (-1, down_ref)):
        listed = pieces(0, dy)[0]
        clear_end(ref, listed)
        for field, plane, half, first, count, at in listed:
            wanted.setdefault((field, plane), []).append((ref, half, first, count, at))

    def hand_out(field, plane, main, rim):
        for ref, half, first, count, at in wanted.get((field, plane), ()):
            inside = min(count, CY - first)
            if inside > 0:
                ref[at : at + inside] = main[half, first : first + inside]
            if inside < count:
                ref[at + count - 1 : at + count] = rim[half, 0:1]

    first_row = iota((2, 8, 128), 1) == 0
    before = None
    for x in range(CX + 1):
        here = []
        if x < CX:
            code = tag_ref[0, 2 * x : 2 * x + 2] >> 15
            fx, fy, fz = fractions(code)
            wx, wy, wz = (1.0 - fx, fx), (1.0 - fy, fy), (1.0 - fz, fz)
            w = {(i, j, k): wx[i] * wy[j] * wz[k] for i in (0, 1) for j in (0, 1) for k in (0, 1)}
            here.append(w)
            for comp in range(3):
                v, c0, c1, c2 = [
                    cells_ref[c, 2 * x : 2 * x + 2]
                    for c in (comp, 3 + 3 * comp, 4 + 3 * comp, 5 + 3 * comp)
                ]
                base = v - c0 * fx - c1 * fy - c2 * fz
                terms = {}
                for i in (0, 1):
                    a = base + c0 if i else base
                    for j in (0, 1):
                        b = a + c1 if j else a
                        for k in (0, 1):
                            terms[i, j, k] = w[i, j, k] * (b + c2 if k else b)
                here.append(terms)
        for f in range(4):
            s = {}
            for j in (0, 1):
                for k in (0, 1):
                    parts = []
                    if x < CX:
                        parts.append(here[f][0, j, k])
                    if x > 0:
                        parts.append(before[f][1, j, k])
                    s[j, k] = sum(parts[1:], parts[0])
            near, far = [s[j, 0] + z_behind(s[j, 1]) for j in (0, 1)]
            turned = y_shift(far, 1)
            main = near + jnp.where(first_row, 0.0, turned)
            rim = jnp.where(first_row, turned, 0.0)
            grid_ref[f, x], rim_ref[f, x] = main, rim
            hand_out(f, x, main, rim)
            if f == 0:
                inverse = 1.0 / jnp.maximum(main, 0.5)
            else:
                hand_out(3 + f, x, main * inverse, None)
        if x < CX:
            flags = jnp.stack([flag_ref[x, :, 128 * h : 128 * h + 128] for h in range(2)])
            hand_out(7, x, flags.astype(F32), None)
        before = here


def tiled_bytes(shape):
    *outer, rows, columns = shape
    return 4 * math.prod(outer) * (-(-rows // 8) * 8) * (-(-columns // 128) * 128)


def kernel_call(body, name, outs, scratch, args, in_specs=None, flops=0):
    scratch = [x if hasattr(x, "dtype") else pltpu.VMEM(x, F32) for x in scratch]
    size = sum(tiled_bytes(x.shape) for x in (*args, *outs, *scratch) if len(x.shape) > 1)
    return pl.pallas_call(
        body,
        out_shape=outs,
        **({} if in_specs is None else dict(in_specs=in_specs)),
        scratch_shapes=scratch,
        compiler_params=pltpu.CompilerParams(vmem_limit_bytes=size + 4 * 2**20),
        cost_estimate=pl.CostEstimate(flops=flops, bytes_accessed=size, transcendentals=0),
        name=name,
    )(*args)


def of(shape, kind=F32):
    return jax.ShapeDtypeStruct(shape, kind)


def deposit(cells, tag, flags):
    grid = of((4, CX + 1, 2, 8, 128))
    return kernel_call(
        deposit_kernel, "deposit", [grid, grid, slab_shape(0, 1), slab_shape(0, -1)], [], (cells, tag, flags)
    )


def smem():
    return pl.BlockSpec(memory_space=pltpu.SMEM)


def vmem():
    return pl.BlockSpec(memory_space=pltpu.VMEM)


def add_rows(ref, place, row, rows):
    at = (*place, slice(row, row + rows.shape[0]))
    ref[at] = ref[at] + rows


def widen_kernel(
    keep_ref, grid_ref, rim_ref, low_ref, high_ref, flag_ref, after_ref, vel_ref, edge_ref, fluid_ref, up_ref, down_ref, ext
):
    zero = jnp.zeros((2, 8, 128), F32)
    for x in range(CX + 1):
        for f in range(4):
            ext[f, x, :, 0:8] = zero
            ext[f, x, :, 8:16] = grid_ref[f, x]
            ext[f, x, :, 16:24] = rim_ref[f, x]
        if x < CX:
            fluid_ref[x, :, 0:8] = zero
            fluid_ref[x, :, 16:24] = zero
            for h in range(2):
                fluid_ref[x, h, 8:16] = flag_ref[x, :, 128 * h : 128 * h + 128].astype(F32)
    arrived = []
    for dy, ref in ((1, low_ref), (-1, high_ref)):
        for field, x, half, first, count, at in pieces(0, dy)[0]:
            arrived.append((field, x, half, first - dy * CY + 8, ref[at : at + count]))
    for field, x, half, row, rows in arrived:
        if field < 4:
            add_rows(ext, (field, x, half), row, rows)
        elif field == 7:
            fluid_ref[x, half, row : row + rows.shape[0]] = rows
    for f in range(4):
        for x in range(CX + 1):
            ext[f, x, :, 16:24] = keep_ref[1] * ext[f, x, :, 16:24]
        edge_ref[f, 0], edge_ref[f, 1] = ext[f, 0], ext[f, CX]
    for x in range(1, CX):
        inverse = 1.0 / jnp.maximum(ext[0, x], 0.5)
        for d in range(3):
            vel_ref[d, x] = ext[1 + d, x] * inverse
    for field, x, half, row, rows in arrived:
        if 4 <= field < 7:
            vel_ref[field - 4, x, half, row : row + rows.shape[0]] = rows
    for dx, ref in ((1, up_ref), (-1, down_ref)):
        listed = pieces(dx, 0)[0]
        clear_end(ref, listed)
        for field, x, half, first, count, at in listed:
            source = ext.at[field] if field < 4 else fluid_ref if field == 7 else vel_ref.at[field - 4]
            ref[at : at + count] = source[x, half, first + 8 : first + 8 + count]


def widen(keep, *args):
    wide = (CX, 2, 24, 128)
    return kernel_call(
        widen_kernel,
        "widen",
        (of((3, *wide)), of((4, 2, 2, 24, 128)), of(wide), slab_shape(1, 0), slab_shape(-1, 0)),
        [(4, CX + 1, 2, 24, 128)],
        (keep, *args),
        [smem()] + [vmem()] * 5 + [pl.BlockSpec(memory_space=pl.ANY)],
    )


def krylov_kernel(
    keep_ref, near_ref, edge_ref, flag_ref, low_ref, high_ref, vel_ref, fluid_ref, k0_ref, k1_ref, k2_ref, sums_ref, edge
):
    zero = jnp.zeros((2, 24, 128), F32)
    for plane in range(25):
        inner = 4 < plane < 20
        for d in range(3):
            vel_ref[d, plane] = near_ref[d, plane - 4] if inner else zero
        fluid_ref[plane] = flag_ref[plane - 4] if 4 <= plane < 20 else zero
    for f in range(4):
        edge[f, 0], edge[f, 1] = edge_ref[f, 0], edge_ref[f, 1]
    for dx, ref in ((1, low_ref), (-1, high_ref)):
        for field, x, half, first, count, at in pieces(dx, 0)[0]:
            rows, row, plane = ref[at : at + count], first + 8, x - dx * CX + 4
            if field < 4:
                add_rows(edge, (field, (plane - 4) // CX, half), row, rows)
            elif field == 7:
                fluid_ref[plane, half, row : row + count] = rows
            else:
                vel_ref[field - 4, plane, half, row : row + count] = rows
    for side, plane, keep in ((0, 4, 1.0), (1, 20, keep_ref[0])):
        inverse = keep / jnp.maximum(edge[0, side], 0.5)
        for d in range(3):
            vel_ref[d, plane] = edge[1 + d, side] * inverse
    for plane in range(1, 24):
        vy, vz = vel_ref[1, plane], vel_ref[2, plane]
        divergence = (
            0.5 * (vel_ref[0, plane + 1] - vel_ref[0, plane - 1])
            + 0.5 * (y_shift(vy, -1) - y_shift(vy, 1))
            + 0.5 * (z_ahead(vz) - z_behind(vz))
        )
        k0_ref[plane] = -fluid_ref[plane] * divergence

    def applied(ref, plane):
        a = ref[plane]
        beside = (
            ref[plane + 1] + ref[plane - 1] + y_shift(a, 1) + y_shift(a, -1) + z_ahead(a) + z_behind(a)
        )
        return fluid_ref[plane] * (a - beside * (1.0 / 6.0))

    for plane in range(2, 23):
        k1_ref[plane] = applied(k0_ref, plane)
    for plane in range(3, 22):
        k2_ref[plane] = applied(k1_ref, plane)
    totals = [jnp.zeros((2, 8, 128), F32)] * 14
    for plane in range(4, 20):
        k0, k1, k2 = [ref[plane, :, 8:16] for ref in (k0_ref, k1_ref, k2_ref)]
        k3 = applied(k2_ref, plane)[:, 8:16]
        u1, w1 = k0 - k1, k1 - k2
        u2 = u1 - w1
        w2 = w1 - (k2 - k3)
        pairs = (
            (k0, k0), (k0, k1), (k1, k1), (k1, k2), (k2, k2), (k2, k3),
            (k0, u1), (u1, u1), (u1, u2), (u2, u2), (k0, w1), (u1, w1), (u1, w2), (u2, w2),
        )
        totals = [t + a * b for t, (a, b) in zip(totals, pairs)]
    for i, t in enumerate(totals):
        sums_ref[i : i + 1] = jnp.sum(t[0] + t[1], axis=0, keepdims=True)
    sums_ref[14:16] = jnp.zeros((2, 128), F32)


def krylov(keep, *args):
    return kernel_call(
        krylov_kernel,
        "krylov",
        (of((3, 25, 2, 24, 128)),) + (of((25, 2, 24, 128)),) * 4 + (of((16, 128)),),
        [(4, 2, 2, 24, 128)],
        (keep, *args),
        [smem()] + [vmem()] * 5,
    )


def steps_from(gram, energy, apply_once):
    def form(a, table):
        total = None
        for i, p in enumerate(a):
            for j, q in enumerate(a):
                if p is not None and q is not None:
                    term = p * q * table[i + j]
                    total = term if total is None else total + term
        return total

    def ratio(a, b):
        return jnp.where(b > 0.0, a / jnp.where(b > 0.0, b, 1.0), 0.0)

    one, zero = jnp.ones_like(gram[0]), jnp.zeros_like(gram[0])
    residual, direction, answer = [one], [one], [zero] * 3
    norm = gram[0]
    for step in range(3):
        alpha = ratio(norm, form(direction, energy))
        for i, p in enumerate(direction):
            answer[i] = answer[i] + alpha * p
        if step == 2:
            return answer
        image = apply_once(direction, zero)
        residual = [a - alpha * b for a, b in zip(residual + [zero], image)]
        norm_next = form(residual, gram)
        direction = [a + ratio(norm_next, norm) * b for a, b in zip(residual, direction + [zero])]
        norm = norm_next


def coefficients(m):
    power = steps_from(m[0:5], m[1:6], lambda a, zero: [zero] + a)
    shifted = steps_from(
        [m[0]] + m[6:10],
        [m[1]] + m[10:14],
        lambda a, zero: [p - q for p, q in zip(a + [zero], [zero] + a)],
    )
    turned = [shifted[0] + shifted[1] + shifted[2], -shifted[1] - 2.0 * shifted[2], shifted[2]]
    smooth = m[1] < 0.3 * m[0]
    return [jnp.where(smooth, a, b) * (1.0 / 6.0) for a, b in zip(power, turned)]


def project_kernel(
    sums_ref, vel_ref, fluid_ref, k0_ref, k1_ref, k2_ref, tag_ref, lane_ref, sub_ref, swap_ref,
    pressure_ref, out_ref, press, proj,
):
    total = jnp.sum(jnp.sum(sums_ref[...], axis=0), axis=1, keepdims=True)
    c = coefficients([jnp.broadcast_to(total[i : i + 1], (8, 128)) for i in range(14)])
    c = [jnp.concatenate([a, a, a], axis=0)[None] for a in c]
    for plane in range(3, 22):
        press[plane] = c[0] * k0_ref[plane] + c[1] * k1_ref[plane] + c[2] * k2_ref[plane]
    for x in range(CX):
        for h in range(2):
            pressure_ref[x, :, 128 * h : 128 * h + 128] = press[x + 4, h, 8:16]
    for x in range(CX + 1):
        p = press[x + 4]
        inner = p[:, 8:24]
        slopes = (
            press[x + 5, :, 8:24] - press[x + 3, :, 8:24],
            (y_shift(p, -1) - y_shift(p, 1))[:, 8:24],
            z_ahead(inner) - z_behind(inner),
        )
        fluid = fluid_ref[x + 4, :, 8:24]
        for d in range(3):
            field = fluid * (vel_ref[d, x + 4, :, 8:24] - 0.5 * slopes[d])
            for j, rows in enumerate((field[:, 0:8], y_shift(field, -1)[:, 0:8])):
                proj[x, d, j, 0] = rows
                proj[x, d, j, 1] = z_ahead(rows)
    for x in range(CX):
        code = tag_ref[0, 2 * x : 2 * x + 2] >> 15
        fx, fy, fz = fractions(code)
        wx, wy, wz = (1.0 - fx, fx), (1.0 - fy, fy), (1.0 - fz, fz)
        w = {(i, j, k): wx[i] * wy[j] * wz[k] for i in (0, 1) for j in (0, 1) for k in (0, 1)}
        for d in range(3):
            result = None
            for (i, j, k), weight in w.items():
                term = weight * proj[x + i, d, j, k]
                result = term if result is None else result + term
            out_ref[d, 2 * x : 2 * x + 2] = result
    follow_plan([(out_ref, d) for d in range(3)], lane_ref, sub_ref, swap_ref)


def project(*args):
    return kernel_call(
        project_kernel,
        "project",
        (of((CX, CY, 256)), of((3, TILES, 8, 128))),
        [(25, 2, 24, 128), (CX + 1, 3, 2, 2, 2, 8, 128)],
        args,
    )


def neighbours(up, down, axis):
    count = lax.axis_size(axis)
    odd = lax.axis_index(axis) % 2 == 1
    high_rows, low_rows = down.shape[0], up.shape[0]
    up = jnp.concatenate([up, jnp.zeros((high_rows - low_rows, 128), F32)])
    arrived = []
    for first, slab in ((0, jnp.where(odd, down, up)), (1, jnp.where(odd, up, down))):
        pairs = [(i, i + 1) for i in range(first, count - 1, 2)]
        arrived.append(lax.ppermute(slab, axis, pairs + [(b, a) for a, b in pairs]))
    return jnp.where(odd, arrived[0], arrived[1]), jnp.where(odd, arrived[1], arrived[0])


def summed(sums, axis):
    count = lax.axis_size(axis)
    parts = [sums]
    for shift in range(1, count):
        swaps = [(i, i ^ shift) for i in range(count)]
        if max(b for _, b in swaps) >= count:
            swaps = [(i, (i + shift) % count) for i in range(count)]
        parts.append(lax.ppermute(sums, axis, swaps))
    return functools.reduce(jnp.add, parts)


def local(cell_index, offset_code, particle_state, fluid_flags):
    places = [(axis, lax.axis_index(axis), lax.axis_size(axis)) for axis in ("gx", "gy")]
    keep = jnp.stack([(at + 1 < size).astype(F32) for _, at, size in places])
    cells, tag = to_cells(offset_code, particle_state, cell_plan(cell_index.reshape(256, 128)))
    grid, rim, up, down = deposit(cells, tag, fluid_flags)
    low, high = neighbours(up, down, "gy")
    plan = particle_plan(tag.reshape(256, 128))
    near, edge, flags, up, down = widen(keep, grid, rim, low, high, fluid_flags, plan[1])
    low, high = neighbours(up, down, "gx")
    vel, fluid, k0, k1, k2, sums = krylov(keep, near, edge, flags, low, high)
    sums = summed(summed(sums, "gx"), "gy")[None]
    pressure, result = project(sums, vel, fluid, k0, k1, k2, tag, *plan)
    return pressure, result.reshape(1, 3, CELLS)


def solution(mesh):
    return jax.shard_map(
        local,
        mesh=mesh,
        in_specs=(
            P(("groups", "gx", "gy"), None),
            P(("groups", "gx", "gy"), None),
            P(("groups", "gx", "gy"), None, None),
            P(("groups", "gx"), "gy", None),
        ),
        out_specs=(P(("groups", "gx"), "gy", None), P(("groups", "gx", "gy"), None, None)),
        check_vma=False,
    )
```

```python
import functools
import math

import jax
import jax.numpy as jnp
from jax import lax
from jax.experimental import pallas as pl
from jax.experimental.pallas import tpu as pltpu
from jax.sharding import PartitionSpec as P

F32, I32 = jnp.float32, jnp.int32
CX, CY, CELLS = 16, 8, 32768
TILES = CELLS // 1024
LANE_RUNS, SUB_RUNS, SWAPS = 9, 3, 30 * 16


def take(x, index, axis):
    other = tuple(d for d in range(x.ndim) if d != axis)
    dims = lax.GatherDimensionNumbers(
        offset_dims=(),
        collapsed_slice_dims=(axis,),
        start_index_map=(axis,),
        operand_batching_dims=other,
        start_indices_batching_dims=other,
    )
    return lax.gather(
        x, index[..., None], dims, (1,) * x.ndim, mode=lax.GatherScatterMode.PROMISE_IN_BOUNDS
    )


def iota(shape, dim):
    return lax.broadcasted_iota(I32, shape, dim)


class Lanes:
    def __init__(self, lane_bits):
        self.tiles = [None] * TILES
        self.tile_bits = [7, 8, 9, 10, 11]
        self.lane_bits = list(lane_bits)

    def trade(self, slot, lane):
        self.tile_bits[slot], self.lane_bits[lane] = self.lane_bits[lane], self.tile_bits[slot]
        if self.tiles[0] is None:
            return
        stride, hop = 1 << lane, 1 << slot
        low = iota((8, 128), 1) & stride == 0
        for i in range(TILES):
            if i & hop == 0:
                a, b = self.tiles[i], self.tiles[i + hop]
                self.tiles[i] = jnp.where(low, a, pltpu.roll(b, stride, 1))
                self.tiles[i + hop] = jnp.where(low, pltpu.roll(a, 128 - stride, 1), b)

    def bring(self, bit, out):
        if bit not in self.tile_bits:
            self.trade(self.tile_bits.index(out), self.lane_bits.index(bit))

    def compare(self, bit):
        if self.tiles[0] is None:
            return
        hop = 1 << self.tile_bits.index(bit)
        for i in range(TILES):
            if i & hop == 0:
                a, b = self.tiles[i], self.tiles[i + hop]
                self.tiles[i], self.tiles[i + hop] = jnp.minimum(a, b), jnp.maximum(a, b)

    def turn(self, bit, mask):
        if self.tiles[0] is None:
            return
        if bit in self.tile_bits:
            hop = 1 << self.tile_bits.index(bit)
            self.tiles = [t ^ mask if i & hop else t for i, t in enumerate(self.tiles)]
        else:
            here = iota((8, 128), 1) & (1 << self.lane_bits.index(bit)) != 0
            self.tiles = [t ^ jnp.where(here, mask, 0) for t in self.tiles]

    def sort_rows(self, mask):
        for bit in range(5):
            self.bring(bit, 7 + bit)
        for phase in range(1, 8):
            self.turn(phase, mask)
            if phase == 6:
                self.bring(5, 0)
                self.compare(5)
            if phase == 7:
                self.bring(6, 0)
                self.compare(6)
                self.bring(5, 6)
                self.compare(5)
            for bit in reversed(range(min(phase, 5))):
                self.bring(bit, 5)
                self.compare(bit)
            self.turn(phase, mask)
        for bit in range(5):
            self.bring(7 + bit, bit)

    def merge_rows(self):
        out = 7
        for bit in reversed(range(7)):
            self.bring(bit, out)
            self.compare(bit)
            out = bit
        self.bring(7, 0)


def first_layout():
    dry = Lanes(range(7))
    dry.sort_rows(0)
    for _ in range(8):
        dry.merge_rows()
    return [dry.lane_bits.index(bit) for bit in range(7)]


def sort_plan(tiles, lane_ref, sub_ref, swap_ref):
    lanes, subs = iota((8, 128), 1), iota((8, 128), 0)
    top = 0x7FFF

    def record(run, tiles):
        for i, t in enumerate(tiles):
            lane_ref[run, 8 * i : 8 * i + 8] = t & 127
        return [t >> 7 for t in tiles]

    state = Lanes(first_layout())
    state.tiles = [(t << 7) | lanes for t in tiles]
    state.sort_rows(top << 7)
    tiles = record(0, state.tiles)

    swap = 0
    for phase in range(8, 16):
        if phase < 12:
            turns = [top if i >> (phase - 7) & 1 else 0 for i in range(TILES)]
        elif phase < 15:
            turns = [jnp.where(subs & (1 << (phase - 12)) != 0, top, 0)] * TILES
        else:
            turns = [0] * TILES
        tiles = [t ^ f for t, f in zip(tiles, turns)]
        if phase > 12:
            tiles = [(t << 3) | subs for t in tiles]
            stride = 1 << (phase - 13)
            while stride:
                low = subs & stride == 0
                other = [
                    pltpu.roll(t, 4, 0) if stride == 4 else take(t, subs ^ stride, 0) for t in tiles
                ]
                tiles = [
                    jnp.where(low, jnp.minimum(t, o), jnp.maximum(t, o)) for t, o in zip(tiles, other)
                ]
                stride //= 2
            for i, t in enumerate(tiles):
                sub_ref[phase - 13, 8 * i : 8 * i + 8] = t & 7
            tiles = [t >> 3 for t in tiles]
        hop = 1 << (min(phase, 12) - 8)
        while hop:
            for i in range(TILES):
                if i & hop == 0:
                    a, b = tiles[i], tiles[i + hop]
                    swap_ref[8 * swap : 8 * swap + 8] = jnp.where(a > b, 1, 0)
                    swap += 1
                    tiles[i], tiles[i + hop] = jnp.minimum(a, b), jnp.maximum(a, b)
            hop //= 2
        state.tiles = [(t << 7) | lanes for t in tiles]
        state.merge_rows()
        tiles = [t ^ f for t, f in zip(record(phase - 7, state.tiles), turns)]


def follow_plan(stages, lane_ref, sub_ref, swap_ref, sources=None):
    def crossings(hops, before):
        out = {}
        for hop in hops:
            for i in range(TILES):
                if i & hop == 0:
                    out[hop, i] = before
                    before += 1
        return out, before

    def pass_over(sets, work, sources=stages):
        for members in sets:
            moved = [{i: ref[c, i] for i in members} for ref, c in sources]
            work(members, moved)
            for (ref, c), tiles in zip(stages, moved):
                for i, t in tiles.items():
                    ref[c, i] = t

    def gathered(ref, run, axis, members, moved):
        for i in members:
            index = ref[run, 8 * i : 8 * i + 8]
            for tiles in moved:
                tiles[i] = take(tiles[i], index, axis)

    def exchanged(hops, number, members, moved):
        for hop in hops:
            for i in members:
                if i & hop == 0:
                    at = 8 * number[hop, i]
                    crossed = swap_ref[at : at + 8] != 0
                    for tiles in moved:
                        a, b = tiles[i], tiles[i + hop]
                        tiles[i], tiles[i + hop] = jnp.where(crossed, b, a), jnp.where(crossed, a, b)

    eights = [range(8 * g, 8 * g + 8) for g in range(4)]
    numbers, before = {}, 0
    for phase in range(8, 16):
        hops = [1 << k for k in reversed(range(min(phase, 12) - 7))]
        numbers[phase], before = crossings(hops, before)

    def first(members, moved):
        gathered(lane_ref, 0, 1, members, moved)
        for phase in (8, 9, 10):
            exchanged([4, 2, 1][10 - phase :], numbers[phase], members, moved)
            gathered(lane_ref, phase - 7, 1, members, moved)

    pass_over(eights, first, sources or stages)
    for phase in range(11, 16):
        wide = [16, 8] if phase > 11 else [8]
        reach = 32 if phase > 11 else 16
        sets = [range(low + k, low + reach, 8) for low in range(0, 32, reach) for k in range(8)]

        def across(members, moved):
            if phase > 12:
                gathered(sub_ref, phase - 13, 0, members, moved)
            exchanged(wide, numbers[phase], members, moved)

        def within(members, moved):
            exchanged([4, 2, 1], numbers[phase], members, moved)
            gathered(lane_ref, phase - 7, 1, members, moved)

        pass_over(sets, across)
        pass_over(eights, within)


def plan_shapes():
    return [(LANE_RUNS, 256, 128), (SUB_RUNS, 256, 128), (8 * SWAPS, 128)]


def plan_scratch():
    return [pltpu.VMEM(shape, I32) for shape in plan_shapes()]


def split_tiles(array):
    return [array[8 * i : 8 * i + 8] for i in range(TILES)]


def z_behind(a):
    r = pltpu.roll(a, 1, 2)
    fill = jnp.concatenate([jnp.zeros_like(r[:1]), r[:1]], axis=0)
    return jnp.where(iota(a.shape, 2) == 0, fill, r)


def z_ahead(a):
    r = pltpu.roll(a, 127, 2)
    fill = jnp.concatenate([r[1:], jnp.zeros_like(r[:1])], axis=0)
    return jnp.where(iota(a.shape, 2) == 127, fill, r)


def y_shift(a, steps):
    return jnp.stack([pltpu.roll(a[h], steps % a.shape[1], 0) for h in range(2)])


def fractions(code):
    return [((code >> shift & 3).astype(F32) + 0.5) * 0.25 for shift in (0, 2, 4)]


PLANES = {1: range(12, 17), 0: range(17), -1: range(5)}
ROWS = {1: range(4, 9), -1: range(5)}


def reach(place, last):
    return max(0, -place, place - last)


def pieces(dx, dy):
    at, out = 0, []
    for plane in PLANES[dx]:
        far_x = reach(plane - dx * CX, CX)
        for field in range(8):
            rows = []
            for row in ROWS[dy] if dy else range(-4, 13):
                far_y = reach(row - dy * CY, CY)
                read = [
                    max(far_x - 1, 0) + far_y <= 3,
                    far_x + max(far_y - 1, 0) <= 3,
                    far_x + far_y <= 3,
                ]
                shared = plane in (0, CX) or (dy != 0 and row in (0, CY))
                if field == 7:
                    wanted = read[2] and plane < CX and (row < CY or not dy)
                elif field == 0:
                    wanted = shared and any(read)
                else:
                    wanted = read[(field - 1) % 3] and shared == (field < 4)
                if wanted:
                    rows.append(row)
            while rows:
                count = 1
                while count < len(rows) and rows[count] == rows[0] + count:
                    count += 1
                for half in range(2):
                    out.append((field, plane, half, rows[0], count, at))
                    at += count
                rows = rows[count:]
    return out, -(-at // 8) * 8


def slab_shape(dx, dy):
    return of((pieces(dx, dy)[1], 128))


def clear_end(ref, listed):
    used = listed[-1][4] + listed[-1][5]
    if used < ref.shape[0]:
        ref[used:] = jnp.zeros((ref.shape[0] - used, 128), F32)


def particle_plan_kernel(tag_ref, lane_ref, sub_ref, swap_ref):
    k = tag_ref[...] & 0x7FFF
    key = ((k & 0x380) << 5) | ((k & 0x7C00) >> 3) | (k & 0x7F)
    sort_plan(split_tiles(key), lane_ref, sub_ref, swap_ref)


def particle_plan(tag):
    outs = [of(shape, I32) for shape in plan_shapes()]
    return kernel_call(particle_plan_kernel, "particle_plan", outs, [], (tag,), flops=10**7)


def cell_plan_kernel(cell_ref, lane_ref, sub_ref, swap_ref):
    k = cell_ref[...]
    key = ((k & 0x700) << 4) | ((k & 0x7800) >> 3) | (k & 0xFF)
    sort_plan(split_tiles(key), lane_ref, sub_ref, swap_ref)


def cell_plan(cell):
    outs = [of(shape, I32) for shape in plan_shapes()]
    return kernel_call(cell_plan_kernel, "cell_plan", outs, [], (cell,), flops=7 * 10**9)


def to_cells_kernel(code_ref, state_ref, lane_ref, sub_ref, swap_ref, cells_ref, tag_ref):
    shape = (TILES, 8, 128)
    tag_ref[0] = (code_ref[...] << 15) | (iota(shape, 0) * 8 + iota(shape, 1)) * 128 + iota(shape, 2)
    for quad in range(3):
        channels = range(4 * quad, 4 * quad + 4)
        stages = [(cells_ref, c) for c in channels] + [(tag_ref, 0)] * (quad == 0)
        sources = [(state_ref, c) for c in channels] + [(tag_ref, 0)] * (quad == 0)
        follow_plan(stages, lane_ref, sub_ref, swap_ref, sources)


def to_cells(code, state, plan):
    return kernel_call(
        to_cells_kernel,
        "to_cells",
        (of((12, TILES, 8, 128)), of((1, TILES, 8, 128), I32)),
        [],
        (code.reshape(TILES, 8, 128), state.reshape(12, TILES, 8, 128), *plan),
        flops=10**7,
    )


def deposit_kernel(cells_ref, tag_ref, flag_ref, grid_ref, rim_ref, up_ref, down_ref):
    wanted = {}
    for dy, ref in ((1, up_ref), (-1, down_ref)):
        listed = pieces(0, dy)[0]
        clear_end(ref, listed)
        for field, plane, half, first, count, at in listed:
            wanted.setdefault((field, plane), []).append((ref, half, first, count, at))

    def hand_out(field, plane, main, rim):
        for ref, half, first, count, at in wanted.get((field, plane), ()):
            inside = min(count, CY - first)
            if inside > 0:
                ref[at : at + inside] = main[half, first : first + inside]
            if inside < count:
                ref[at + count - 1 : at + count] = rim[half, 0:1]

    first_row = iota((2, 8, 128), 1) == 0
    before = None
    for x in range(CX + 1):
        here = []
        if x < CX:
            code = tag_ref[0, 2 * x : 2 * x + 2] >> 15
            fx, fy, fz = fractions(code)
            wx, wy, wz = (1.0 - fx, fx), (1.0 - fy, fy), (1.0 - fz, fz)
            w = {(i, j, k): wx[i] * wy[j] * wz[k] for i in (0, 1) for j in (0, 1) for k in (0, 1)}
            here.append(w)
            for comp in range(3):
                v, c0, c1, c2 = [
                    cells_ref[c, 2 * x : 2 * x + 2]
                    for c in (comp, 3 + 3 * comp, 4 + 3 * comp, 5 + 3 * comp)
                ]
                base = v - c0 * fx - c1 * fy - c2 * fz
                terms = {}
                for i in (0, 1):
                    a = base + c0 if i else base
                    for j in (0, 1):
                        b = a + c1 if j else a
                        for k in (0, 1):
                            terms[i, j, k] = w[i, j, k] * (b + c2 if k else b)
                here.append(terms)
        for f in range(4):
            s = {}
            for j in (0, 1):
                for k in (0, 1):
                    parts = []
                    if x < CX:
                        parts.append(here[f][0, j, k])
                    if x > 0:
                        parts.append(before[f][1, j, k])
                    s[j, k] = sum(parts[1:], parts[0])
            near, far = [s[j, 0] + z_behind(s[j, 1]) for j in (0, 1)]
            turned = y_shift(far, 1)
            main = near + jnp.where(first_row, 0.0, turned)
            rim = jnp.where(first_row, turned, 0.0)
            grid_ref[f, x], rim_ref[f, x] = main, rim
            hand_out(f, x, main, rim)
            if f == 0:
                inverse = 1.0 / jnp.maximum(main, 0.5)
            else:
                hand_out(3 + f, x, main * inverse, None)
        if x < CX:
            flags = jnp.stack([flag_ref[x, :, 128 * h : 128 * h + 128] for h in range(2)])
            hand_out(7, x, flags.astype(F32), None)
        before = here


def tiled_bytes(shape):
    *outer, rows, columns = shape
    return 4 * math.prod(outer) * (-(-rows // 8) * 8) * (-(-columns // 128) * 128)


def kernel_call(body, name, outs, scratch, args, in_specs=None, flops=0):
    scratch = [x if hasattr(x, "dtype") else pltpu.VMEM(x, F32) for x in scratch]
    size = sum(tiled_bytes(x.shape) for x in (*args, *outs, *scratch) if len(x.shape) > 1)
    return pl.pallas_call(
        body,
        out_shape=outs,
        **({} if in_specs is None else dict(in_specs=in_specs)),
        scratch_shapes=scratch,
        compiler_params=pltpu.CompilerParams(vmem_limit_bytes=size + 4 * 2**20),
        cost_estimate=pl.CostEstimate(flops=flops, bytes_accessed=size, transcendentals=0),
        name=name,
    )(*args)


def of(shape, kind=F32):
    return jax.ShapeDtypeStruct(shape, kind)


def deposit(cells, tag, flags):
    grid = of((4, CX + 1, 2, 8, 128))
    return kernel_call(
        deposit_kernel, "deposit", [grid, grid, slab_shape(0, 1), slab_shape(0, -1)], [], (cells, tag, flags)
    )


def smem():
    return pl.BlockSpec(memory_space=pltpu.SMEM)


def vmem():
    return pl.BlockSpec(memory_space=pltpu.VMEM)


def add_rows(ref, place, row, rows):
    at = (*place, slice(row, row + rows.shape[0]))
    ref[at] = ref[at] + rows


def widen_kernel(
    keep_ref, grid_ref, rim_ref, low_ref, high_ref, flag_ref, after_ref, vel_ref, edge_ref, fluid_ref, up_ref, down_ref, ext
):
    zero = jnp.zeros((2, 8, 128), F32)
    for x in range(CX + 1):
        for f in range(4):
            ext[f, x, :, 0:8] = zero
            ext[f, x, :, 8:16] = grid_ref[f, x]
            ext[f, x, :, 16:24] = rim_ref[f, x]
        if x < CX:
            fluid_ref[x, :, 0:8] = zero
            fluid_ref[x, :, 16:24] = zero
            for h in range(2):
                fluid_ref[x, h, 8:16] = flag_ref[x, :, 128 * h : 128 * h + 128].astype(F32)
    arrived = []
    for dy, ref in ((1, low_ref), (-1, high_ref)):
        for field, x, half, first, count, at in pieces(0, dy)[0]:
            arrived.append((field, x, half, first - dy * CY + 8, ref[at : at + count]))
    for field, x, half, row, rows in arrived:
        if field < 4:
            add_rows(ext, (field, x, half), row, rows)
        elif field == 7:
            fluid_ref[x, half, row : row + rows.shape[0]] = rows
    for f in range(4):
        for x in range(CX + 1):
            ext[f, x, :, 16:24] = keep_ref[1] * ext[f, x, :, 16:24]
        edge_ref[f, 0], edge_ref[f, 1] = ext[f, 0], ext[f, CX]
    for x in range(1, CX):
        inverse = 1.0 / jnp.maximum(ext[0, x], 0.5)
        for d in range(3):
            vel_ref[d, x] = ext[1 + d, x] * inverse
    for field, x, half, row, rows in arrived:
        if 4 <= field < 7:
            vel_ref[field - 4, x, half, row : row + rows.shape[0]] = rows
    for dx, ref in ((1, up_ref), (-1, down_ref)):
        listed = pieces(dx, 0)[0]
        clear_end(ref, listed)
        for field, x, half, first, count, at in listed:
            source = ext.at[field] if field < 4 else fluid_ref if field == 7 else vel_ref.at[field - 4]
            ref[at : at + count] = source[x, half, first + 8 : first + 8 + count]


def widen(keep, *args):
    wide = (CX, 2, 24, 128)
    return kernel_call(
        widen_kernel,
        "widen",
        (of((3, *wide)), of((4, 2, 2, 24, 128)), of(wide), slab_shape(1, 0), slab_shape(-1, 0)),
        [(4, CX + 1, 2, 24, 128)],
        (keep, *args),
        [smem()] + [vmem()] * 5 + [pl.BlockSpec(memory_space=pl.ANY)],
    )


def krylov_kernel(
    keep_ref, near_ref, edge_ref, flag_ref, low_ref, high_ref, vel_ref, fluid_ref, k0_ref, k1_ref, k2_ref, sums_ref, edge
):
    zero = jnp.zeros((2, 24, 128), F32)
    for plane in range(25):
        inner = 4 < plane < 20
        for d in range(3):
            vel_ref[d, plane] = near_ref[d, plane - 4] if inner else zero
        fluid_ref[plane] = flag_ref[plane - 4] if 4 <= plane < 20 else zero
    for f in range(4):
        edge[f, 0], edge[f, 1] = edge_ref[f, 0], edge_ref[f, 1]
    for dx, ref in ((1, low_ref), (-1, high_ref)):
        for field, x, half, first, count, at in pieces(dx, 0)[0]:
            rows, row, plane = ref[at : at + count], first + 8, x - dx * CX + 4
            if field < 4:
                add_rows(edge, (field, (plane - 4) // CX, half), row, rows)
            elif field == 7:
                fluid_ref[plane, half, row : row + count] = rows
            else:
                vel_ref[field - 4, plane, half, row : row + count] = rows
    for side, plane, keep in ((0, 4, 1.0), (1, 20, keep_ref[0])):
        inverse = keep / jnp.maximum(edge[0, side], 0.5)
        for d in range(3):
            vel_ref[d, plane] = edge[1 + d, side] * inverse
    for plane in range(1, 24):
        vy, vz = vel_ref[1, plane], vel_ref[2, plane]
        divergence = (
            0.5 * (vel_ref[0, plane + 1] - vel_ref[0, plane - 1])
            + 0.5 * (y_shift(vy, -1) - y_shift(vy, 1))
            + 0.5 * (z_ahead(vz) - z_behind(vz))
        )
        k0_ref[plane] = -fluid_ref[plane] * divergence

    def applied(ref, plane):
        a = ref[plane]
        beside = (
            ref[plane + 1] + ref[plane - 1] + y_shift(a, 1) + y_shift(a, -1) + z_ahead(a) + z_behind(a)
        )
        return fluid_ref[plane] * (a - beside * (1.0 / 6.0))

    for plane in range(2, 23):
        k1_ref[plane] = applied(k0_ref, plane)
    for plane in range(3, 22):
        k2_ref[plane] = applied(k1_ref, plane)
    totals = [jnp.zeros((2, 8, 128), F32)] * 14
    for plane in range(4, 20):
        k0, k1, k2 = [ref[plane, :, 8:16] for ref in (k0_ref, k1_ref, k2_ref)]
        k3 = applied(k2_ref, plane)[:, 8:16]
        u1, w1 = k0 - k1, k1 - k2
        u2 = u1 - w1
        w2 = w1 - (k2 - k3)
        pairs = (
            (k0, k0), (k0, k1), (k1, k1), (k1, k2), (k2, k2), (k2, k3),
            (k0, u1), (u1, u1), (u1, u2), (u2, u2), (k0, w1), (u1, w1), (u1, w2), (u2, w2),
        )
        totals = [t + a * b for t, (a, b) in zip(totals, pairs)]
    for i, t in enumerate(totals):
        sums_ref[i : i + 1] = jnp.sum(t[0] + t[1], axis=0, keepdims=True)
    sums_ref[14:16] = jnp.zeros((2, 128), F32)


def krylov(keep, *args):
    return kernel_call(
        krylov_kernel,
        "krylov",
        (of((3, 25, 2, 24, 128)),) + (of((25, 2, 24, 128)),) * 4 + (of((16, 128)),),
        [(4, 2, 2, 24, 128)],
        (keep, *args),
        [smem()] + [vmem()] * 5,
    )


def steps_from(gram, energy, apply_once):
    def form(a, table):
        total = None
        for i, p in enumerate(a):
            for j, q in enumerate(a):
                if p is not None and q is not None:
                    term = p * q * table[i + j]
                    total = term if total is None else total + term
        return total

    def ratio(a, b):
        return jnp.where(b > 0.0, a / jnp.where(b > 0.0, b, 1.0), 0.0)

    one, zero = jnp.ones_like(gram[0]), jnp.zeros_like(gram[0])
    residual, direction, answer = [one], [one], [zero] * 3
    norm = gram[0]
    for step in range(3):
        alpha = ratio(norm, form(direction, energy))
        for i, p in enumerate(direction):
            answer[i] = answer[i] + alpha * p
        if step == 2:
            return answer
        image = apply_once(direction, zero)
        residual = [a - alpha * b for a, b in zip(residual + [zero], image)]
        norm_next = form(residual, gram)
        direction = [a + ratio(norm_next, norm) * b for a, b in zip(residual, direction + [zero])]
        norm = norm_next


def coefficients(m):
    power = steps_from(m[0:5], m[1:6], lambda a, zero: [zero] + a)
    shifted = steps_from(
        [m[0]] + m[6:10],
        [m[1]] + m[10:14],
        lambda a, zero: [p - q for p, q in zip(a + [zero], [zero] + a)],
    )
    turned = [shifted[0] + shifted[1] + shifted[2], -shifted[1] - 2.0 * shifted[2], shifted[2]]
    smooth = m[1] < 0.3 * m[0]
    return [jnp.where(smooth, a, b) * (1.0 / 6.0) for a, b in zip(power, turned)]


def project_kernel(
    sums_ref, vel_ref, fluid_ref, k0_ref, k1_ref, k2_ref, tag_ref, lane_ref, sub_ref, swap_ref,
    pressure_ref, out_ref, press, proj,
):
    total = jnp.sum(jnp.sum(sums_ref[...], axis=0), axis=1, keepdims=True)
    c = coefficients([jnp.broadcast_to(total[i : i + 1], (8, 128)) for i in range(14)])
    c = [jnp.concatenate([a, a, a], axis=0)[None] for a in c]
    for plane in range(3, 22):
        press[plane] = c[0] * k0_ref[plane] + c[1] * k1_ref[plane] + c[2] * k2_ref[plane]
    for x in range(CX):
        for h in range(2):
            pressure_ref[x, :, 128 * h : 128 * h + 128] = press[x + 4, h, 8:16]
    for x in range(CX + 1):
        p = press[x + 4]
        inner = p[:, 8:24]
        slopes = (
            press[x + 5, :, 8:24] - press[x + 3, :, 8:24],
            (y_shift(p, -1) - y_shift(p, 1))[:, 8:24],
            z_ahead(inner) - z_behind(inner),
        )
        fluid = fluid_ref[x + 4, :, 8:24]
        for d in range(3):
            field = fluid * (vel_ref[d, x + 4, :, 8:24] - 0.5 * slopes[d])
            for j, rows in enumerate((field[:, 0:8], y_shift(field, -1)[:, 0:8])):
                proj[x, d, j, 0] = rows
                proj[x, d, j, 1] = z_ahead(rows)
    for x in range(CX):
        code = tag_ref[0, 2 * x : 2 * x + 2] >> 15
        fx, fy, fz = fractions(code)
        wx, wy, wz = (1.0 - fx, fx), (1.0 - fy, fy), (1.0 - fz, fz)
        w = {(i, j, k): wx[i] * wy[j] * wz[k] for i in (0, 1) for j in (0, 1) for k in (0, 1)}
        for d in range(3):
            result = None
            for (i, j, k), weight in w.items():
                term = weight * proj[x + i, d, j, k]
                result = term if result is None else result + term
            out_ref[d, 2 * x : 2 * x + 2] = result
    follow_plan([(out_ref, d) for d in range(3)], lane_ref, sub_ref, swap_ref)


def project(*args):
    return kernel_call(
        project_kernel,
        "project",
        (of((CX, CY, 256)), of((3, TILES, 8, 128))),
        [(25, 2, 24, 128), (CX + 1, 3, 2, 2, 2, 8, 128)],
        args,
    )


def neighbours(up, down, axis):
    count = lax.axis_size(axis)
    odd = lax.axis_index(axis) % 2 == 1
    high_rows, low_rows = down.shape[0], up.shape[0]
    up = jnp.concatenate([up, jnp.zeros((high_rows - low_rows, 128), F32)])
    arrived = []
    for first, slab in ((0, jnp.where(odd, down, up)), (1, jnp.where(odd, up, down))):
        pairs = [(i, i + 1) for i in range(first, count - 1, 2)]
        arrived.append(lax.ppermute(slab, axis, pairs + [(b, a) for a, b in pairs]))
    return jnp.where(odd, arrived[0], arrived[1]), jnp.where(odd, arrived[1], arrived[0])


def summed(sums, axis):
    count = lax.axis_size(axis)
    parts = [sums]
    for shift in range(1, count):
        swaps = [(i, i ^ shift) for i in range(count)]
        if max(b for _, b in swaps) >= count:
            swaps = [(i, (i + shift) % count) for i in range(count)]
        parts.append(lax.ppermute(sums, axis, swaps))
    return functools.reduce(jnp.add, parts)


def local(cell_index, offset_code, particle_state, fluid_flags):
    places = [(axis, lax.axis_index(axis), lax.axis_size(axis)) for axis in ("gx", "gy")]
    keep = jnp.stack([(at + 1 < size).astype(F32) for _, at, size in places])
    cells, tag = to_cells(offset_code, particle_state, cell_plan(cell_index.reshape(256, 128)))
    grid, rim, up, down = deposit(cells, tag, fluid_flags)
    low, high = neighbours(up, down, "gy")
    plan = particle_plan(tag.reshape(256, 128))
    near, edge, flags, up, down = widen(keep, grid, rim, low, high, fluid_flags, plan[1])
    low, high = neighbours(up, down, "gx")
    vel, fluid, k0, k1, k2, sums = krylov(keep, near, edge, flags, low, high)
    sums = summed(summed(sums, "gx"), "gy")[None]
    pressure, result = project(sums, vel, fluid, k0, k1, k2, tag, *plan)
    return pressure, result.reshape(1, 3, CELLS)


def solution(mesh):
    return jax.shard_map(
        local,
        mesh=mesh,
        in_specs=(
            P(("groups", "gx", "gy"), None),
            P(("groups", "gx", "gy"), None),
            P(("groups", "gx", "gy"), None, None),
            P(("groups", "gx"), "gy", None),
        ),
        out_specs=(P(("groups", "gx"), "gy", None), P(("groups", "gx", "gy"), None, None)),
        check_vma=False,
    )
```

```python
import functools
import math

import jax
import jax.numpy as jnp
from jax import lax
from jax.experimental import pallas as pl
from jax.experimental.pallas import tpu as pltpu
from jax.sharding import PartitionSpec as P

F32, I32 = jnp.float32, jnp.int32
CX, CY, CELLS = 16, 8, 32768
TILES = CELLS // 1024
LANE_RUNS, SUB_RUNS, SWAPS = 9, 3, 30 * 16
GROUP = 2


def take(x, index, axis):
    other = tuple(d for d in range(x.ndim) if d != axis)
    dims = lax.GatherDimensionNumbers(
        offset_dims=(),
        collapsed_slice_dims=(axis,),
        start_index_map=(axis,),
        operand_batching_dims=other,
        start_indices_batching_dims=other,
    )
    return lax.gather(
        x, index[..., None], dims, (1,) * x.ndim, mode=lax.GatherScatterMode.PROMISE_IN_BOUNDS
    )


def iota(shape, dim):
    return lax.broadcasted_iota(I32, shape, dim)


class Lanes:
    def __init__(self, lane_bits):
        self.tiles = [None] * TILES
        self.tile_bits = [7, 8, 9, 10, 11]
        self.lane_bits = list(lane_bits)

    def trade(self, slot, lane):
        self.tile_bits[slot], self.lane_bits[lane] = self.lane_bits[lane], self.tile_bits[slot]
        if self.tiles[0] is None:
            return
        stride, hop = 1 << lane, 1 << slot
        low = iota((8, 128), 1) & stride == 0
        for i in range(TILES):
            if i & hop == 0:
                a, b = self.tiles[i], self.tiles[i + hop]
                self.tiles[i] = jnp.where(low, a, pltpu.roll(b, stride, 1))
                self.tiles[i + hop] = jnp.where(low, pltpu.roll(a, 128 - stride, 1), b)

    def bring(self, bit, out):
        if bit not in self.tile_bits:
            self.trade(self.tile_bits.index(out), self.lane_bits.index(bit))

    def compare(self, bit):
        if self.tiles[0] is None:
            return
        hop = 1 << self.tile_bits.index(bit)
        for i in range(TILES):
            if i & hop == 0:
                a, b = self.tiles[i], self.tiles[i + hop]
                self.tiles[i], self.tiles[i + hop] = jnp.minimum(a, b), jnp.maximum(a, b)

    def turn(self, bit, mask):
        if self.tiles[0] is None:
            return
        if bit in self.tile_bits:
            hop = 1 << self.tile_bits.index(bit)
            self.tiles = [t ^ mask if i & hop else t for i, t in enumerate(self.tiles)]
        else:
            here = iota((8, 128), 1) & (1 << self.lane_bits.index(bit)) != 0
            self.tiles = [t ^ jnp.where(here, mask, 0) for t in self.tiles]

    def sort_rows(self, mask):
        for bit in range(5):
            self.bring(bit, 7 + bit)
        for phase in range(1, 8):
            self.turn(phase, mask)
            if phase == 6:
                self.bring(5, 0)
                self.compare(5)
            if phase == 7:
                self.bring(6, 0)
                self.compare(6)
                self.bring(5, 6)
                self.compare(5)
            for bit in reversed(range(min(phase, 5))):
                self.bring(bit, 5)
                self.compare(bit)
            self.turn(phase, mask)
        for bit in range(5):
            self.bring(7 + bit, bit)

    def merge_rows(self, tick=lambda: None):
        out = 7
        for bit in reversed(range(7)):
            self.bring(bit, out)
            self.compare(bit)
            out = bit
            tick()
        self.bring(7, 0)
        tick()


def first_layout():
    dry = Lanes(range(7))
    dry.sort_rows(0)
    for _ in range(8):
        dry.merge_rows()
    return [dry.lane_bits.index(bit) for bit in range(7)]


def record_run(run, tiles, lane_ref):
    for i, t in enumerate(tiles):
        lane_ref[run, 8 * i : 8 * i + 8] = t & 127
    return [t >> 7 for t in tiles]


def plan_rows(tiles, lane_ref):
    state = Lanes(first_layout())
    state.tiles = [(t << 7) | iota((8, 128), 1) for t in tiles]
    state.sort_rows(0x7FFF << 7)
    return record_run(0, state.tiles, lane_ref)


def sort_plan(tiles, lane_ref, sub_ref, swap_ref):
    plan_rest(plan_rows(tiles, lane_ref), lane_ref, sub_ref, swap_ref)


def plan_rest(tiles, lane_ref, sub_ref, swap_ref, begin=lambda phase: None, tick=lambda: None):
    lanes, subs = iota((8, 128), 1), iota((8, 128), 0)
    top = 0x7FFF

    state = Lanes(first_layout())
    state.sort_rows(0)
    swap = 0
    for phase in range(8, 16):
        begin(phase)
        if phase < 12:
            turns = [top if i >> (phase - 7) & 1 else 0 for i in range(TILES)]
        elif phase < 15:
            turns = [jnp.where(subs & (1 << (phase - 12)) != 0, top, 0)] * TILES
        else:
            turns = [0] * TILES
        tiles = [t ^ f for t, f in zip(tiles, turns)]
        if phase > 12:
            tiles = [(t << 3) | subs for t in tiles]
            stride = 1 << (phase - 13)
            while stride:
                low = subs & stride == 0
                other = [
                    pltpu.roll(t, 4, 0) if stride == 4 else take(t, subs ^ stride, 0) for t in tiles
                ]
                tiles = [
                    jnp.where(low, jnp.minimum(t, o), jnp.maximum(t, o)) for t, o in zip(tiles, other)
                ]
                stride //= 2
            for i, t in enumerate(tiles):
                sub_ref[phase - 13, 8 * i : 8 * i + 8] = t & 7
            tiles = [t >> 3 for t in tiles]
        hop = 1 << (min(phase, 12) - 8)
        while hop:
            for i in range(TILES):
                if i & hop == 0:
                    a, b = tiles[i], tiles[i + hop]
                    swap_ref[8 * swap : 8 * swap + 8] = jnp.where(a > b, 1, 0)
                    swap += 1
                    tiles[i], tiles[i + hop] = jnp.minimum(a, b), jnp.maximum(a, b)
            hop //= 2
        state.tiles = [(t << 7) | lanes for t in tiles]
        state.merge_rows(tick)
        tiles = [t ^ f for t, f in zip(record_run(phase - 7, state.tiles, lane_ref), turns)]


def follow_plan(stages, lane_ref, sub_ref, swap_ref, sources=None):
    def crossings(hops, before):
        out = {}
        for hop in hops:
            for i in range(TILES):
                if i & hop == 0:
                    out[hop, i] = before
                    before += 1
        return out, before

    def pass_over(sets, work, sources=stages):
        for members in sets:
            moved = [{i: ref[c, i] for i in members} for ref, c in sources]
            work(members, moved)
            for (ref, c), tiles in zip(stages, moved):
                for i, t in tiles.items():
                    ref[c, i] = t

    def gathered(ref, run, axis, members, moved):
        for i in members:
            index = ref[run, 8 * i : 8 * i + 8]
            for tiles in moved:
                tiles[i] = take(tiles[i], index, axis)

    def exchanged(hops, number, members, moved):
        for hop in hops:
            for i in members:
                if i & hop == 0:
                    at = 8 * number[hop, i]
                    crossed = swap_ref[at : at + 8] != 0
                    for tiles in moved:
                        a, b = tiles[i], tiles[i + hop]
                        tiles[i], tiles[i + hop] = jnp.where(crossed, b, a), jnp.where(crossed, a, b)

    eights = [range(8 * g, 8 * g + 8) for g in range(4)]
    numbers, before = {}, 0
    for phase in range(8, 16):
        hops = [1 << k for k in reversed(range(min(phase, 12) - 7))]
        numbers[phase], before = crossings(hops, before)

    def first(members, moved):
        gathered(lane_ref, 0, 1, members, moved)
        for phase in (8, 9, 10):
            exchanged([4, 2, 1][10 - phase :], numbers[phase], members, moved)
            gathered(lane_ref, phase - 7, 1, members, moved)

    pass_over(eights, first, sources or stages)
    for phase in range(11, 16):
        wide = [16, 8] if phase > 11 else [8]
        reach = 32 if phase > 11 else 16
        sets = [range(low + k, low + reach, 8) for low in range(0, 32, reach) for k in range(8)]

        def across(members, moved):
            if phase > 12:
                gathered(sub_ref, phase - 13, 0, members, moved)
            exchanged(wide, numbers[phase], members, moved)

        def within(members, moved):
            exchanged([4, 2, 1], numbers[phase], members, moved)
            gathered(lane_ref, phase - 7, 1, members, moved)

        pass_over(sets, across)
        pass_over(eights, within)


def crossings(phase):
    before, numbers = 0, {}
    for p in range(8, phase + 1):
        for k in reversed(range(min(p, 12) - 7)):
            for i in range(TILES):
                if i & (1 << k) == 0:
                    if p == phase:
                        numbers[1 << k, i] = before
                    before += 1
    return numbers


def move_items(phase, stages, sources, lane_ref, sub_ref, swap_ref):
    numbers = crossings(phase)

    def item(members, sources, steps):
        def work():
            moved = [{i: ref[c, i] for i in members} for ref, c in sources]
            for step in steps:
                step(members, moved)
            for (ref, c), tiles in zip(stages, moved):
                for i, t in tiles.items():
                    ref[c, i] = t

        return work

    def gathered(ref, run, axis):
        def step(members, moved):
            for i in members:
                index = ref[run, 8 * i : 8 * i + 8]
                for tiles in moved:
                    tiles[i] = take(tiles[i], index, axis)

        return step

    def exchanged(*hops):
        def step(members, moved):
            for hop in hops:
                for i in members:
                    if i & hop == 0:
                        at = 8 * numbers[hop, i]
                        crossed = swap_ref[at : at + 8] != 0
                        for tiles in moved:
                            a, b = tiles[i], tiles[i + hop]
                            tiles[i], tiles[i + hop] = jnp.where(crossed, b, a), jnp.where(crossed, a, b)

        return step

    items = []
    if phase > 10:
        spread = 32 if phase > 11 else 16
        steps = [gathered(sub_ref, phase - 13, 0)] if phase > 12 else []
        steps.append(exchanged(16, 8) if phase > 11 else exchanged(8))
        for low in range(0, 32, spread):
            items += [item(range(low + k, low + spread, 8), stages, steps) for k in range(8)]
    steps = [gathered(lane_ref, 0, 1)] if phase == 8 else []
    steps.append(exchanged(*[4, 2, 1][max(0, 10 - phase) :]))
    steps.append(gathered(lane_ref, phase - 7, 1))
    return items + [
        item(range(8 * g, 8 * g + 8), sources if phase == 8 else stages, steps) for g in range(4)
    ]


def plan_shapes():
    return [(LANE_RUNS, 256, 128), (SUB_RUNS, 256, 128), (8 * SWAPS, 128)]


def plan_scratch():
    return [pltpu.VMEM(shape, I32) for shape in plan_shapes()]


def split_tiles(array):
    return [array[8 * i : 8 * i + 8] for i in range(TILES)]


def z_behind(a):
    r = pltpu.roll(a, 1, 2)
    fill = jnp.concatenate([jnp.zeros_like(r[:1]), r[:1]], axis=0)
    return jnp.where(iota(a.shape, 2) == 0, fill, r)


def z_ahead(a):
    r = pltpu.roll(a, 127, 2)
    fill = jnp.concatenate([r[1:], jnp.zeros_like(r[:1])], axis=0)
    return jnp.where(iota(a.shape, 2) == 127, fill, r)


def y_shift(a, steps):
    return jnp.stack([pltpu.roll(a[h], steps % a.shape[1], 0) for h in range(2)])


def fractions(code):
    return [((code >> shift & 3).astype(F32) + 0.5) * 0.25 for shift in (0, 2, 4)]


PLANES = {1: range(12, 17), 0: range(17), -1: range(5)}
ROWS = {1: range(4, 9), -1: range(5)}


def reach(place, last):
    return max(0, -place, place - last)


def pieces(dx, dy):
    at, out = 0, []
    for plane in PLANES[dx]:
        far_x = reach(plane - dx * CX, CX)
        for field in range(8):
            rows = []
            for row in ROWS[dy] if dy else range(-4, 13):
                far_y = reach(row - dy * CY, CY)
                read = [
                    max(far_x - 1, 0) + far_y <= 3,
                    far_x + max(far_y - 1, 0) <= 3,
                    far_x + far_y <= 3,
                ]
                shared = plane in (0, CX) or (dy != 0 and row in (0, CY))
                if field == 7:
                    wanted = read[2] and plane < CX and (row < CY or not dy)
                elif field == 0:
                    wanted = shared and any(read)
                else:
                    wanted = read[(field - 1) % 3] and shared == (field < 4)
                if wanted:
                    rows.append(row)
            while rows:
                count = 1
                while count < len(rows) and rows[count] == rows[0] + count:
                    count += 1
                for half in range(2):
                    out.append((field, plane, half, rows[0], count, at))
                    at += count
                rows = rows[count:]
    return out, -(-at // 8) * 8


def slab_shape(dx, dy):
    return of((pieces(dx, dy)[1], 128))


def clear_end(ref, listed):
    used = listed[-1][4] + listed[-1][5]
    if used < ref.shape[0]:
        ref[used:] = jnp.zeros((ref.shape[0] - used, 128), F32)


def particle_plan_kernel(tag_ref, lane_ref, sub_ref, swap_ref):
    k = tag_ref[...] & 0x7FFF
    key = ((k & 0x380) << 5) | ((k & 0x7C00) >> 3) | (k & 0x7F)
    sort_plan(split_tiles(key), lane_ref, sub_ref, swap_ref)


def particle_plan(tag):
    outs = [of(shape, I32) for shape in plan_shapes()]
    return kernel_call(particle_plan_kernel, "particle_plan", outs, [], (tag,), flops=10**7)


def cell_rows_kernel(cell_ref, key_ref, lane_ref):
    k = cell_ref[...]
    key = ((k & 0x700) << 4) | ((k & 0x7800) >> 3) | (k & 0xFF)
    for i, t in enumerate(plan_rows(split_tiles(key), lane_ref)):
        key_ref[8 * i : 8 * i + 8] = t


def cell_rows(cell):
    outs = [of((256, 128), I32), of((1, 256, 128), I32)]
    return kernel_call(cell_rows_kernel, "cell_rows", outs, [], (cell,), flops=3 * 10**9)


def to_cells_kernel(code_ref, state_ref, key_ref, rows_ref, cells_ref, tag_ref, lane_ref, sub_ref, swap_ref):
    shape = (TILES, 8, 128)
    tag_ref[0] = (code_ref[...] << 15) | (iota(shape, 0) * 8 + iota(shape, 1)) * 128 + iota(shape, 2)
    lane_ref[0] = rows_ref[0]
    stages = [(tag_ref, 0)] + [(cells_ref, c) for c in range(12)]
    sources = [(tag_ref, 0)] + [(state_ref, c) for c in range(12)]
    waiting, pace = [], [0]

    def begin(phase):
        while waiting:
            waiting.pop(0)()
        if phase > 8:
            for low in range(0, 13, GROUP):
                chosen = slice(low, low + GROUP)
                waiting.extend(
                    move_items(phase - 1, stages[chosen], sources[chosen], lane_ref, sub_ref, swap_ref)
                )
        pace[0] = -(-len(waiting) // 8)

    def tick():
        for _ in range(min(pace[0], len(waiting))):
            waiting.pop(0)()

    plan_rest(split_tiles(key_ref[...]), lane_ref, sub_ref, swap_ref, begin, tick)
    begin(16)
    while waiting:
        waiting.pop(0)()


def to_cells(code, state, key, rows):
    return kernel_call(
        to_cells_kernel,
        "to_cells",
        (of((12, TILES, 8, 128)), of((1, TILES, 8, 128), I32)),
        plan_scratch(),
        (code.reshape(TILES, 8, 128), state.reshape(12, TILES, 8, 128), key, rows),
        flops=10**7,
    )


def deposit_kernel(cells_ref, tag_ref, flag_ref, grid_ref, rim_ref, up_ref, down_ref):
    wanted = {}
    for dy, ref in ((1, up_ref), (-1, down_ref)):
        listed = pieces(0, dy)[0]
        clear_end(ref, listed)
        for field, plane, half, first, count, at in listed:
            wanted.setdefault((field, plane), []).append((ref, half, first, count, at))

    def hand_out(field, plane, main, rim):
        for ref, half, first, count, at in wanted.get((field, plane), ()):
            inside = min(count, CY - first)
            if inside > 0:
                ref[at : at + inside] = main[half, first : first + inside]
            if inside < count:
                ref[at + count - 1 : at + count] = rim[half, 0:1]

    first_row = iota((2, 8, 128), 1) == 0
    before = None
    for x in range(CX + 1):
        here = []
        if x < CX:
            code = tag_ref[0, 2 * x : 2 * x + 2] >> 15
            fx, fy, fz = fractions(code)
            wx, wy, wz = (1.0 - fx, fx), (1.0 - fy, fy), (1.0 - fz, fz)
            w = {(i, j, k): wx[i] * wy[j] * wz[k] for i in (0, 1) for j in (0, 1) for k in (0, 1)}
            here.append(w)
            for comp in range(3):
                v, c0, c1, c2 = [
                    cells_ref[c, 2 * x : 2 * x + 2]
                    for c in (comp, 3 + 3 * comp, 4 + 3 * comp, 5 + 3 * comp)
                ]
                base = v - c0 * fx - c1 * fy - c2 * fz
                terms = {}
                for i in (0, 1):
                    a = base + c0 if i else base
                    for j in (0, 1):
                        b = a + c1 if j else a
                        for k in (0, 1):
                            terms[i, j, k] = w[i, j, k] * (b + c2 if k else b)
                here.append(terms)
        for f in range(4):
            s = {}
            for j in (0, 1):
                for k in (0, 1):
                    parts = []
                    if x < CX:
                        parts.append(here[f][0, j, k])
                    if x > 0:
                        parts.append(before[f][1, j, k])
                    s[j, k] = sum(parts[1:], parts[0])
            near, far = [s[j, 0] + z_behind(s[j, 1]) for j in (0, 1)]
            turned = y_shift(far, 1)
            main = near + jnp.where(first_row, 0.0, turned)
            rim = jnp.where(first_row, turned, 0.0)
            grid_ref[f, x], rim_ref[f, x] = main, rim
            hand_out(f, x, main, rim)
            if f == 0:
                inverse = 1.0 / jnp.maximum(main, 0.5)
            else:
                hand_out(3 + f, x, main * inverse, None)
        if x < CX:
            flags = jnp.stack([flag_ref[x, :, 128 * h : 128 * h + 128] for h in range(2)])
            hand_out(7, x, flags.astype(F32), None)
        before = here


def tiled_bytes(shape):
    *outer, rows, columns = shape
    return 4 * math.prod(outer) * (-(-rows // 8) * 8) * (-(-columns // 128) * 128)


def kernel_call(body, name, outs, scratch, args, in_specs=None, flops=0):
    scratch = [x if hasattr(x, "dtype") else pltpu.VMEM(x, F32) for x in scratch]
    size = sum(tiled_bytes(x.shape) for x in (*args, *outs, *scratch) if len(x.shape) > 1)
    return pl.pallas_call(
        body,
        out_shape=outs,
        **({} if in_specs is None else dict(in_specs=in_specs)),
        scratch_shapes=scratch,
        compiler_params=pltpu.CompilerParams(vmem_limit_bytes=size + 4 * 2**20),
        cost_estimate=pl.CostEstimate(flops=flops, bytes_accessed=size, transcendentals=0),
        name=name,
    )(*args)


def of(shape, kind=F32):
    return jax.ShapeDtypeStruct(shape, kind)


def deposit(cells, tag, flags):
    grid = of((4, CX + 1, 2, 8, 128))
    return kernel_call(
        deposit_kernel, "deposit", [grid, grid, slab_shape(0, 1), slab_shape(0, -1)], [], (cells, tag, flags)
    )


def smem():
    return pl.BlockSpec(memory_space=pltpu.SMEM)


def vmem():
    return pl.BlockSpec(memory_space=pltpu.VMEM)


def add_rows(ref, place, row, rows):
    at = (*place, slice(row, row + rows.shape[0]))
    ref[at] = ref[at] + rows


def widen_kernel(
    keep_ref, grid_ref, rim_ref, low_ref, high_ref, flag_ref, after_ref, vel_ref, edge_ref, fluid_ref, up_ref, down_ref, ext
):
    zero = jnp.zeros((2, 8, 128), F32)
    for x in range(CX + 1):
        for f in range(4):
            ext[f, x, :, 0:8] = zero
            ext[f, x, :, 8:16] = grid_ref[f, x]
            ext[f, x, :, 16:24] = rim_ref[f, x]
        if x < CX:
            fluid_ref[x, :, 0:8] = zero
            fluid_ref[x, :, 16:24] = zero
            for h in range(2):
                fluid_ref[x, h, 8:16] = flag_ref[x, :, 128 * h : 128 * h + 128].astype(F32)
    arrived = []
    for dy, ref in ((1, low_ref), (-1, high_ref)):
        for field, x, half, first, count, at in pieces(0, dy)[0]:
            arrived.append((field, x, half, first - dy * CY + 8, ref[at : at + count]))
    for field, x, half, row, rows in arrived:
        if field < 4:
            add_rows(ext, (field, x, half), row, rows)
        elif field == 7:
            fluid_ref[x, half, row : row + rows.shape[0]] = rows
    for f in range(4):
        for x in range(CX + 1):
            ext[f, x, :, 16:24] = keep_ref[1] * ext[f, x, :, 16:24]
        edge_ref[f, 0], edge_ref[f, 1] = ext[f, 0], ext[f, CX]
    for x in range(1, CX):
        inverse = 1.0 / jnp.maximum(ext[0, x], 0.5)
        for d in range(3):
            vel_ref[d, x] = ext[1 + d, x] * inverse
    for field, x, half, row, rows in arrived:
        if 4 <= field < 7:
            vel_ref[field - 4, x, half, row : row + rows.shape[0]] = rows
    for dx, ref in ((1, up_ref), (-1, down_ref)):
        listed = pieces(dx, 0)[0]
        clear_end(ref, listed)
        for field, x, half, first, count, at in listed:
            source = ext.at[field] if field < 4 else fluid_ref if field == 7 else vel_ref.at[field - 4]
            ref[at : at + count] = source[x, half, first + 8 : first + 8 + count]


def widen(keep, *args):
    wide = (CX, 2, 24, 128)
    return kernel_call(
        widen_kernel,
        "widen",
        (of((3, *wide)), of((4, 2, 2, 24, 128)), of(wide), slab_shape(1, 0), slab_shape(-1, 0)),
        [(4, CX + 1, 2, 24, 128)],
        (keep, *args),
        [smem()] + [vmem()] * 5 + [pl.BlockSpec(memory_space=pl.ANY)],
    )


def krylov_kernel(
    keep_ref, near_ref, edge_ref, flag_ref, low_ref, high_ref, vel_ref, fluid_ref, k0_ref, k1_ref, k2_ref, sums_ref, edge
):
    zero = jnp.zeros((2, 24, 128), F32)
    for plane in range(25):
        inner = 4 < plane < 20
        for d in range(3):
            vel_ref[d, plane] = near_ref[d, plane - 4] if inner else zero
        fluid_ref[plane] = flag_ref[plane - 4] if 4 <= plane < 20 else zero
    for f in range(4):
        edge[f, 0], edge[f, 1] = edge_ref[f, 0], edge_ref[f, 1]
    for dx, ref in ((1, low_ref), (-1, high_ref)):
        for field, x, half, first, count, at in pieces(dx, 0)[0]:
            rows, row, plane = ref[at : at + count], first + 8, x - dx * CX + 4
            if field < 4:
                add_rows(edge, (field, (plane - 4) // CX, half), row, rows)
            elif field == 7:
                fluid_ref[plane, half, row : row + count] = rows
            else:
                vel_ref[field - 4, plane, half, row : row + count] = rows
    for side, plane, keep in ((0, 4, 1.0), (1, 20, keep_ref[0])):
        inverse = keep / jnp.maximum(edge[0, side], 0.5)
        for d in range(3):
            vel_ref[d, plane] = edge[1 + d, side] * inverse
    for plane in range(1, 24):
        vy, vz = vel_ref[1, plane], vel_ref[2, plane]
        divergence = (
            0.5 * (vel_ref[0, plane + 1] - vel_ref[0, plane - 1])
            + 0.5 * (y_shift(vy, -1) - y_shift(vy, 1))
            + 0.5 * (z_ahead(vz) - z_behind(vz))
        )
        k0_ref[plane] = -fluid_ref[plane] * divergence

    def applied(ref, plane):
        a = ref[plane]
        beside = (
            ref[plane + 1] + ref[plane - 1] + y_shift(a, 1) + y_shift(a, -1) + z_ahead(a) + z_behind(a)
        )
        return fluid_ref[plane] * (a - beside * (1.0 / 6.0))

    for plane in range(2, 23):
        k1_ref[plane] = applied(k0_ref, plane)
    for plane in range(3, 22):
        k2_ref[plane] = applied(k1_ref, plane)
    totals = [jnp.zeros((2, 8, 128), F32)] * 14
    for plane in range(4, 20):
        k0, k1, k2 = [ref[plane, :, 8:16] for ref in (k0_ref, k1_ref, k2_ref)]
        k3 = applied(k2_ref, plane)[:, 8:16]
        u1, w1 = k0 - k1, k1 - k2
        u2 = u1 - w1
        w2 = w1 - (k2 - k3)
        pairs = (
            (k0, k0), (k0, k1), (k1, k1), (k1, k2), (k2, k2), (k2, k3),
            (k0, u1), (u1, u1), (u1, u2), (u2, u2), (k0, w1), (u1, w1), (u1, w2), (u2, w2),
        )
        totals = [t + a * b for t, (a, b) in zip(totals, pairs)]
    for i, t in enumerate(totals):
        sums_ref[i : i + 1] = jnp.sum(t[0] + t[1], axis=0, keepdims=True)
    sums_ref[14:16] = jnp.zeros((2, 128), F32)


def krylov(keep, *args):
    return kernel_call(
        krylov_kernel,
        "krylov",
        (of((3, 25, 2, 24, 128)),) + (of((25, 2, 24, 128)),) * 4 + (of((16, 128)),),
        [(4, 2, 2, 24, 128)],
        (keep, *args),
        [smem()] + [vmem()] * 5,
    )


def steps_from(gram, energy, apply_once):
    def form(a, table):
        total = None
        for i, p in enumerate(a):
            for j, q in enumerate(a):
                if p is not None and q is not None:
                    term = p * q * table[i + j]
                    total = term if total is None else total + term
        return total

    def ratio(a, b):
        return jnp.where(b > 0.0, a / jnp.where(b > 0.0, b, 1.0), 0.0)

    one, zero = jnp.ones_like(gram[0]), jnp.zeros_like(gram[0])
    residual, direction, answer = [one], [one], [zero] * 3
    norm = gram[0]
    for step in range(3):
        alpha = ratio(norm, form(direction, energy))
        for i, p in enumerate(direction):
            answer[i] = answer[i] + alpha * p
        if step == 2:
            return answer
        image = apply_once(direction, zero)
        residual = [a - alpha * b for a, b in zip(residual + [zero], image)]
        norm_next = form(residual, gram)
        direction = [a + ratio(norm_next, norm) * b for a, b in zip(residual, direction + [zero])]
        norm = norm_next


def coefficients(m):
    power = steps_from(m[0:5], m[1:6], lambda a, zero: [zero] + a)
    shifted = steps_from(
        [m[0]] + m[6:10],
        [m[1]] + m[10:14],
        lambda a, zero: [p - q for p, q in zip(a + [zero], [zero] + a)],
    )
    turned = [shifted[0] + shifted[1] + shifted[2], -shifted[1] - 2.0 * shifted[2], shifted[2]]
    smooth = m[1] < 0.3 * m[0]
    return [jnp.where(smooth, a, b) * (1.0 / 6.0) for a, b in zip(power, turned)]


def project_kernel(
    sums_ref, vel_ref, fluid_ref, k0_ref, k1_ref, k2_ref, tag_ref, lane_ref, sub_ref, swap_ref,
    pressure_ref, out_ref, press, proj,
):
    total = jnp.sum(jnp.sum(sums_ref[...], axis=0), axis=1, keepdims=True)
    c = coefficients([jnp.broadcast_to(total[i : i + 1], (8, 128)) for i in range(14)])
    c = [jnp.concatenate([a, a, a], axis=0)[None] for a in c]
    for plane in range(3, 22):
        press[plane] = c[0] * k0_ref[plane] + c[1] * k1_ref[plane] + c[2] * k2_ref[plane]
    for x in range(CX):
        for h in range(2):
            pressure_ref[x, :, 128 * h : 128 * h + 128] = press[x + 4, h, 8:16]
    for x in range(CX + 1):
        p = press[x + 4]
        inner = p[:, 8:24]
        slopes = (
            press[x + 5, :, 8:24] - press[x + 3, :, 8:24],
            (y_shift(p, -1) - y_shift(p, 1))[:, 8:24],
            z_ahead(inner) - z_behind(inner),
        )
        fluid = fluid_ref[x + 4, :, 8:24]
        for d in range(3):
            field = fluid * (vel_ref[d, x + 4, :, 8:24] - 0.5 * slopes[d])
            for j, rows in enumerate((field[:, 0:8], y_shift(field, -1)[:, 0:8])):
                proj[x, d, j, 0] = rows
                proj[x, d, j, 1] = z_ahead(rows)
    for x in range(CX):
        code = tag_ref[0, 2 * x : 2 * x + 2] >> 15
        fx, fy, fz = fractions(code)
        wx, wy, wz = (1.0 - fx, fx), (1.0 - fy, fy), (1.0 - fz, fz)
        w = {(i, j, k): wx[i] * wy[j] * wz[k] for i in (0, 1) for j in (0, 1) for k in (0, 1)}
        for d in range(3):
            result = None
            for (i, j, k), weight in w.items():
                term = weight * proj[x + i, d, j, k]
                result = term if result is None else result + term
            out_ref[d, 2 * x : 2 * x + 2] = result
    follow_plan([(out_ref, d) for d in range(3)], lane_ref, sub_ref, swap_ref)


def project(*args):
    return kernel_call(
        project_kernel,
        "project",
        (of((CX, CY, 256)), of((3, TILES, 8, 128))),
        [(25, 2, 24, 128), (CX + 1, 3, 2, 2, 2, 8, 128)],
        args,
    )


def neighbours(up, down, axis):
    count = lax.axis_size(axis)
    odd = lax.axis_index(axis) % 2 == 1
    high_rows, low_rows = down.shape[0], up.shape[0]
    up = jnp.concatenate([up, jnp.zeros((high_rows - low_rows, 128), F32)])
    arrived = []
    for first, slab in ((0, jnp.where(odd, down, up)), (1, jnp.where(odd, up, down))):
        pairs = [(i, i + 1) for i in range(first, count - 1, 2)]
        arrived.append(lax.ppermute(slab, axis, pairs + [(b, a) for a, b in pairs]))
    return jnp.where(odd, arrived[0], arrived[1]), jnp.where(odd, arrived[1], arrived[0])


def summed(sums, axis):
    count = lax.axis_size(axis)
    parts = [sums]
    for shift in range(1, count):
        swaps = [(i, i ^ shift) for i in range(count)]
        if max(b for _, b in swaps) >= count:
            swaps = [(i, (i + shift) % count) for i in range(count)]
        parts.append(lax.ppermute(sums, axis, swaps))
    return functools.reduce(jnp.add, parts)


def local(cell_index, offset_code, particle_state, fluid_flags):
    places = [(axis, lax.axis_index(axis), lax.axis_size(axis)) for axis in ("gx", "gy")]
    keep = jnp.stack([(at + 1 < size).astype(F32) for _, at, size in places])
    cells, tag = to_cells(offset_code, particle_state, *cell_rows(cell_index.reshape(256, 128)))
    grid, rim, up, down = deposit(cells, tag, fluid_flags)
    low, high = neighbours(up, down, "gy")
    plan = particle_plan(tag.reshape(256, 128))
    near, edge, flags, up, down = widen(keep, grid, rim, low, high, fluid_flags, plan[1])
    low, high = neighbours(up, down, "gx")
    vel, fluid, k0, k1, k2, sums = krylov(keep, near, edge, flags, low, high)
    sums = summed(summed(sums, "gx"), "gy")[None]
    pressure, result = project(sums, vel, fluid, k0, k1, k2, tag, *plan)
    return pressure, result.reshape(1, 3, CELLS)


def solution(mesh):
    return jax.shard_map(
        local,
        mesh=mesh,
        in_specs=(
            P(("groups", "gx", "gy"), None),
            P(("groups", "gx", "gy"), None),
            P(("groups", "gx", "gy"), None, None),
            P(("groups", "gx"), "gy", None),
        ),
        out_specs=(P(("groups", "gx"), "gy", None), P(("groups", "gx", "gy"), None, None)),
        check_vma=False,
    )
```

```python
import functools
import math

import jax
import jax.numpy as jnp
from jax import lax
from jax.experimental import pallas as pl
from jax.experimental.pallas import tpu as pltpu
from jax.sharding import PartitionSpec as P

F32, I32 = jnp.float32, jnp.int32
CX, CY, CELLS = 16, 8, 32768
TILES = CELLS // 1024
LANE_RUNS, SUB_RUNS, SWAPS = 9, 3, 30 * 16
GROUP = 3


def take(x, index, axis):
    other = tuple(d for d in range(x.ndim) if d != axis)
    dims = lax.GatherDimensionNumbers(
        offset_dims=(),
        collapsed_slice_dims=(axis,),
        start_index_map=(axis,),
        operand_batching_dims=other,
        start_indices_batching_dims=other,
    )
    return lax.gather(
        x, index[..., None], dims, (1,) * x.ndim, mode=lax.GatherScatterMode.PROMISE_IN_BOUNDS
    )


def iota(shape, dim):
    return lax.broadcasted_iota(I32, shape, dim)


class Lanes:
    def __init__(self, lane_bits):
        self.tiles = [None] * TILES
        self.tile_bits = [7, 8, 9, 10, 11]
        self.lane_bits = list(lane_bits)

    def trade(self, slot, lane):
        self.tile_bits[slot], self.lane_bits[lane] = self.lane_bits[lane], self.tile_bits[slot]
        if self.tiles[0] is None:
            return
        stride, hop = 1 << lane, 1 << slot
        low = iota((8, 128), 1) & stride == 0
        for i in range(TILES):
            if i & hop == 0:
                a, b = self.tiles[i], self.tiles[i + hop]
                self.tiles[i] = jnp.where(low, a, pltpu.roll(b, stride, 1))
                self.tiles[i + hop] = jnp.where(low, pltpu.roll(a, 128 - stride, 1), b)

    def bring(self, bit, out):
        if bit not in self.tile_bits:
            self.trade(self.tile_bits.index(out), self.lane_bits.index(bit))

    def compare(self, bit):
        if self.tiles[0] is None:
            return
        hop = 1 << self.tile_bits.index(bit)
        for i in range(TILES):
            if i & hop == 0:
                a, b = self.tiles[i], self.tiles[i + hop]
                self.tiles[i], self.tiles[i + hop] = jnp.minimum(a, b), jnp.maximum(a, b)

    def turn(self, bit, mask):
        if self.tiles[0] is None:
            return
        if bit in self.tile_bits:
            hop = 1 << self.tile_bits.index(bit)
            self.tiles = [t ^ mask if i & hop else t for i, t in enumerate(self.tiles)]
        else:
            here = iota((8, 128), 1) & (1 << self.lane_bits.index(bit)) != 0
            self.tiles = [t ^ jnp.where(here, mask, 0) for t in self.tiles]

    def sort_rows(self, mask):
        for bit in range(5):
            self.bring(bit, 7 + bit)
        for phase in range(1, 8):
            self.turn(phase, mask)
            if phase == 6:
                self.bring(5, 0)
                self.compare(5)
            if phase == 7:
                self.bring(6, 0)
                self.compare(6)
                self.bring(5, 6)
                self.compare(5)
            for bit in reversed(range(min(phase, 5))):
                self.bring(bit, 5)
                self.compare(bit)
            self.turn(phase, mask)
        for bit in range(5):
            self.bring(7 + bit, bit)

    def merge_rows(self, tick=lambda: None):
        out = 7
        for bit in reversed(range(7)):
            self.bring(bit, out)
            self.compare(bit)
            out = bit
            tick()
        self.bring(7, 0)
        tick()


def first_layout():
    dry = Lanes(range(7))
    dry.sort_rows(0)
    for _ in range(8):
        dry.merge_rows()
    return [dry.lane_bits.index(bit) for bit in range(7)]


def record_run(run, tiles, lane_ref):
    for i, t in enumerate(tiles):
        lane_ref[run, 8 * i : 8 * i + 8] = t & 127
    return [t >> 7 for t in tiles]


def plan_rows(tiles, lane_ref):
    state = Lanes(first_layout())
    state.tiles = [(t << 7) | iota((8, 128), 1) for t in tiles]
    state.sort_rows(0x7FFF << 7)
    return record_run(0, state.tiles, lane_ref)


def sort_plan(tiles, lane_ref, sub_ref, swap_ref):
    plan_rest(plan_rows(tiles, lane_ref), lane_ref, sub_ref, swap_ref)


def plan_rest(tiles, lane_ref, sub_ref, swap_ref, begin=lambda phase: None, tick=lambda: None):
    lanes, subs = iota((8, 128), 1), iota((8, 128), 0)
    top = 0x7FFF

    state = Lanes(first_layout())
    state.sort_rows(0)
    swap = 0
    for phase in range(8, 16):
        begin(phase)
        if phase < 12:
            turns = [top if i >> (phase - 7) & 1 else 0 for i in range(TILES)]
        elif phase < 15:
            turns = [jnp.where(subs & (1 << (phase - 12)) != 0, top, 0)] * TILES
        else:
            turns = [0] * TILES
        tiles = [t ^ f for t, f in zip(tiles, turns)]
        if phase > 12:
            tiles = [(t << 3) | subs for t in tiles]
            stride = 1 << (phase - 13)
            while stride:
                low = subs & stride == 0
                other = [
                    pltpu.roll(t, 4, 0) if stride == 4 else take(t, subs ^ stride, 0) for t in tiles
                ]
                tiles = [
                    jnp.where(low, jnp.minimum(t, o), jnp.maximum(t, o)) for t, o in zip(tiles, other)
                ]
                stride //= 2
            for i, t in enumerate(tiles):
                sub_ref[phase - 13, 8 * i : 8 * i + 8] = t & 7
            tiles = [t >> 3 for t in tiles]
        hop = 1 << (min(phase, 12) - 8)
        while hop:
            for i in range(TILES):
                if i & hop == 0:
                    a, b = tiles[i], tiles[i + hop]
                    swap_ref[8 * swap : 8 * swap + 8] = jnp.where(a > b, 1, 0)
                    swap += 1
                    tiles[i], tiles[i + hop] = jnp.minimum(a, b), jnp.maximum(a, b)
            hop //= 2
        state.tiles = [(t << 7) | lanes for t in tiles]
        state.merge_rows(tick)
        tiles = [t ^ f for t, f in zip(record_run(phase - 7, state.tiles, lane_ref), turns)]


def follow_plan(stages, lane_ref, sub_ref, swap_ref, sources=None):
    def crossings(hops, before):
        out = {}
        for hop in hops:
            for i in range(TILES):
                if i & hop == 0:
                    out[hop, i] = before
                    before += 1
        return out, before

    def pass_over(sets, work, sources=stages):
        for members in sets:
            moved = [{i: ref[c, i] for i in members} for ref, c in sources]
            work(members, moved)
            for (ref, c), tiles in zip(stages, moved):
                for i, t in tiles.items():
                    ref[c, i] = t

    def gathered(ref, run, axis, members, moved):
        for i in members:
            index = ref[run, 8 * i : 8 * i + 8]
            for tiles in moved:
                tiles[i] = take(tiles[i], index, axis)

    def exchanged(hops, number, members, moved):
        for hop in hops:
            for i in members:
                if i & hop == 0:
                    at = 8 * number[hop, i]
                    crossed = swap_ref[at : at + 8] != 0
                    for tiles in moved:
                        a, b = tiles[i], tiles[i + hop]
                        tiles[i], tiles[i + hop] = jnp.where(crossed, b, a), jnp.where(crossed, a, b)

    eights = [range(8 * g, 8 * g + 8) for g in range(4)]
    numbers, before = {}, 0
    for phase in range(8, 16):
        hops = [1 << k for k in reversed(range(min(phase, 12) - 7))]
        numbers[phase], before = crossings(hops, before)

    def first(members, moved):
        gathered(lane_ref, 0, 1, members, moved)
        for phase in (8, 9, 10):
            exchanged([4, 2, 1][10 - phase :], numbers[phase], members, moved)
            gathered(lane_ref, phase - 7, 1, members, moved)

    pass_over(eights, first, sources or stages)
    for phase in range(11, 16):
        wide = [16, 8] if phase > 11 else [8]
        reach = 32 if phase > 11 else 16
        sets = [range(low + k, low + reach, 8) for low in range(0, 32, reach) for k in range(8)]

        def across(members, moved):
            if phase > 12:
                gathered(sub_ref, phase - 13, 0, members, moved)
            exchanged(wide, numbers[phase], members, moved)

        def within(members, moved):
            exchanged([4, 2, 1], numbers[phase], members, moved)
            gathered(lane_ref, phase - 7, 1, members, moved)

        pass_over(sets, across)
        pass_over(eights, within)


def crossings(phase):
    before, numbers = 0, {}
    for p in range(8, phase + 1):
        for k in reversed(range(min(p, 12) - 7)):
            for i in range(TILES):
                if i & (1 << k) == 0:
                    if p == phase:
                        numbers[1 << k, i] = before
                    before += 1
    return numbers


def move_items(phase, stages, sources, lane_ref, sub_ref, swap_ref):
    numbers = crossings(phase)

    def item(members, sources, steps):
        def work():
            moved = [{i: ref[c, i] for i in members} for ref, c in sources]
            for step in steps:
                step(members, moved)
            for (ref, c), tiles in zip(stages, moved):
                for i, t in tiles.items():
                    ref[c, i] = t

        return work

    def gathered(ref, run, axis):
        def step(members, moved):
            for i in members:
                index = ref[run, 8 * i : 8 * i + 8]
                for tiles in moved:
                    tiles[i] = take(tiles[i], index, axis)

        return step

    def exchanged(*hops):
        def step(members, moved):
            for hop in hops:
                for i in members:
                    if i & hop == 0:
                        at = 8 * numbers[hop, i]
                        crossed = swap_ref[at : at + 8] != 0
                        for tiles in moved:
                            a, b = tiles[i], tiles[i + hop]
                            tiles[i], tiles[i + hop] = jnp.where(crossed, b, a), jnp.where(crossed, a, b)

        return step

    items = []
    if phase > 10:
        spread = 32 if phase > 11 else 16
        steps = [gathered(sub_ref, phase - 13, 0)] if phase > 12 else []
        steps.append(exchanged(16, 8) if phase > 11 else exchanged(8))
        for low in range(0, 32, spread):
            items += [item(range(low + k, low + spread, 8), stages, steps) for k in range(8)]
    steps = [gathered(lane_ref, 0, 1)] if phase == 8 else []
    steps.append(exchanged(*[4, 2, 1][max(0, 10 - phase) :]))
    steps.append(gathered(lane_ref, phase - 7, 1))
    return items + [
        item(range(8 * g, 8 * g + 8), sources if phase == 8 else stages, steps) for g in range(4)
    ]


def plan_shapes():
    return [(LANE_RUNS, 256, 128), (SUB_RUNS, 256, 128), (8 * SWAPS, 128)]


def plan_scratch():
    return [pltpu.VMEM(shape, I32) for shape in plan_shapes()]


def split_tiles(array):
    return [array[8 * i : 8 * i + 8] for i in range(TILES)]


def z_behind(a):
    r = pltpu.roll(a, 1, 2)
    fill = jnp.concatenate([jnp.zeros_like(r[:1]), r[:1]], axis=0)
    return jnp.where(iota(a.shape, 2) == 0, fill, r)


def z_ahead(a):
    r = pltpu.roll(a, 127, 2)
    fill = jnp.concatenate([r[1:], jnp.zeros_like(r[:1])], axis=0)
    return jnp.where(iota(a.shape, 2) == 127, fill, r)


def y_shift(a, steps):
    return jnp.stack([pltpu.roll(a[h], steps % a.shape[1], 0) for h in range(2)])


def fractions(code):
    return [((code >> shift & 3).astype(F32) + 0.5) * 0.25 for shift in (0, 2, 4)]


PLANES = {1: range(12, 17), 0: range(17), -1: range(5)}
ROWS = {1: range(4, 9), -1: range(5)}


def reach(place, last):
    return max(0, -place, place - last)


def pieces(dx, dy):
    at, out = 0, []
    for plane in PLANES[dx]:
        far_x = reach(plane - dx * CX, CX)
        for field in range(8):
            rows = []
            for row in ROWS[dy] if dy else range(-4, 13):
                far_y = reach(row - dy * CY, CY)
                read = [
                    max(far_x - 1, 0) + far_y <= 3,
                    far_x + max(far_y - 1, 0) <= 3,
                    far_x + far_y <= 3,
                ]
                shared = plane in (0, CX) or (dy != 0 and row in (0, CY))
                if field == 7:
                    wanted = read[2] and plane < CX and (row < CY or not dy)
                elif field == 0:
                    wanted = shared and any(read)
                else:
                    wanted = read[(field - 1) % 3] and shared == (field < 4)
                if wanted:
                    rows.append(row)
            while rows:
                count = 1
                while count < len(rows) and rows[count] == rows[0] + count:
                    count += 1
                for half in range(2):
                    out.append((field, plane, half, rows[0], count, at))
                    at += count
                rows = rows[count:]
    return out, -(-at // 8) * 8


def slab_shape(dx, dy):
    return of((pieces(dx, dy)[1], 128))


def clear_end(ref, listed):
    used = listed[-1][4] + listed[-1][5]
    if used < ref.shape[0]:
        ref[used:] = jnp.zeros((ref.shape[0] - used, 128), F32)


def particle_plan_kernel(tag_ref, lane_ref, sub_ref, swap_ref):
    k = tag_ref[...] & 0x7FFF
    key = ((k & 0x380) << 5) | ((k & 0x7C00) >> 3) | (k & 0x7F)
    sort_plan(split_tiles(key), lane_ref, sub_ref, swap_ref)


def particle_plan(tag):
    outs = [of(shape, I32) for shape in plan_shapes()]
    return kernel_call(particle_plan_kernel, "particle_plan", outs, [], (tag,), flops=10**7)


def cell_rows_kernel(cell_ref, key_ref, lane_ref):
    k = cell_ref[...]
    key = ((k & 0x700) << 4) | ((k & 0x7800) >> 3) | (k & 0xFF)
    for i, t in enumerate(plan_rows(split_tiles(key), lane_ref)):
        key_ref[8 * i : 8 * i + 8] = t


def cell_rows(cell):
    outs = [of((256, 128), I32), of((1, 256, 128), I32)]
    return kernel_call(cell_rows_kernel, "cell_rows", outs, [], (cell,), flops=3 * 10**9)


def to_cells_kernel(code_ref, state_ref, key_ref, rows_ref, cells_ref, tag_ref, lane_ref, sub_ref, swap_ref):
    shape = (TILES, 8, 128)
    tag_ref[0] = (code_ref[...] << 15) | (iota(shape, 0) * 8 + iota(shape, 1)) * 128 + iota(shape, 2)
    lane_ref[0] = rows_ref[0]
    stages = [(tag_ref, 0)] + [(cells_ref, c) for c in range(12)]
    sources = [(tag_ref, 0)] + [(state_ref, c) for c in range(12)]
    waiting, pace = [], [0]

    def begin(phase):
        while waiting:
            waiting.pop(0)()
        if phase > 8:
            for low in range(0, 13, GROUP):
                chosen = slice(low, low + GROUP)
                waiting.extend(
                    move_items(phase - 1, stages[chosen], sources[chosen], lane_ref, sub_ref, swap_ref)
                )
        pace[0] = -(-len(waiting) // 8)

    def tick():
        for _ in range(min(pace[0], len(waiting))):
            waiting.pop(0)()

    plan_rest(split_tiles(key_ref[...]), lane_ref, sub_ref, swap_ref, begin, tick)
    begin(16)
    while waiting:
        waiting.pop(0)()


def to_cells(code, state, key, rows):
    return kernel_call(
        to_cells_kernel,
        "to_cells",
        (of((12, TILES, 8, 128)), of((1, TILES, 8, 128), I32)),
        plan_scratch(),
        (code.reshape(TILES, 8, 128), state.reshape(12, TILES, 8, 128), key, rows),
        flops=10**7,
    )


def deposit_kernel(cells_ref, tag_ref, flag_ref, grid_ref, rim_ref, up_ref, down_ref):
    wanted = {}
    for dy, ref in ((1, up_ref), (-1, down_ref)):
        listed = pieces(0, dy)[0]
        clear_end(ref, listed)
        for field, plane, half, first, count, at in listed:
            wanted.setdefault((field, plane), []).append((ref, half, first, count, at))

    def hand_out(field, plane, main, rim):
        for ref, half, first, count, at in wanted.get((field, plane), ()):
            inside = min(count, CY - first)
            if inside > 0:
                ref[at : at + inside] = main[half, first : first + inside]
            if inside < count:
                ref[at + count - 1 : at + count] = rim[half, 0:1]

    first_row = iota((2, 8, 128), 1) == 0
    before = None
    for x in range(CX + 1):
        here = []
        if x < CX:
            code = tag_ref[0, 2 * x : 2 * x + 2] >> 15
            fx, fy, fz = fractions(code)
            wx, wy, wz = (1.0 - fx, fx), (1.0 - fy, fy), (1.0 - fz, fz)
            w = {(i, j, k): wx[i] * wy[j] * wz[k] for i in (0, 1) for j in (0, 1) for k in (0, 1)}
            here.append(w)
            for comp in range(3):
                v, c0, c1, c2 = [
                    cells_ref[c, 2 * x : 2 * x + 2]
                    for c in (comp, 3 + 3 * comp, 4 + 3 * comp, 5 + 3 * comp)
                ]
                base = v - c0 * fx - c1 * fy - c2 * fz
                terms = {}
                for i in (0, 1):
                    a = base + c0 if i else base
                    for j in (0, 1):
                        b = a + c1 if j else a
                        for k in (0, 1):
                            terms[i, j, k] = w[i, j, k] * (b + c2 if k else b)
                here.append(terms)
        for f in range(4):
            s = {}
            for j in (0, 1):
                for k in (0, 1):
                    parts = []
                    if x < CX:
                        parts.append(here[f][0, j, k])
                    if x > 0:
                        parts.append(before[f][1, j, k])
                    s[j, k] = sum(parts[1:], parts[0])
            near, far = [s[j, 0] + z_behind(s[j, 1]) for j in (0, 1)]
            turned = y_shift(far, 1)
            main = near + jnp.where(first_row, 0.0, turned)
            rim = jnp.where(first_row, turned, 0.0)
            grid_ref[f, x], rim_ref[f, x] = main, rim
            hand_out(f, x, main, rim)
            if f == 0:
                inverse = 1.0 / jnp.maximum(main, 0.5)
            else:
                hand_out(3 + f, x, main * inverse, None)
        if x < CX:
            flags = jnp.stack([flag_ref[x, :, 128 * h : 128 * h + 128] for h in range(2)])
            hand_out(7, x, flags.astype(F32), None)
        before = here


def tiled_bytes(shape):
    *outer, rows, columns = shape
    return 4 * math.prod(outer) * (-(-rows // 8) * 8) * (-(-columns // 128) * 128)


def kernel_call(body, name, outs, scratch, args, in_specs=None, flops=0):
    scratch = [x if hasattr(x, "dtype") else pltpu.VMEM(x, F32) for x in scratch]
    size = sum(tiled_bytes(x.shape) for x in (*args, *outs, *scratch) if len(x.shape) > 1)
    return pl.pallas_call(
        body,
        out_shape=outs,
        **({} if in_specs is None else dict(in_specs=in_specs)),
        scratch_shapes=scratch,
        compiler_params=pltpu.CompilerParams(vmem_limit_bytes=size + 4 * 2**20),
        cost_estimate=pl.CostEstimate(flops=flops, bytes_accessed=size, transcendentals=0),
        name=name,
    )(*args)


def of(shape, kind=F32):
    return jax.ShapeDtypeStruct(shape, kind)


def deposit(cells, tag, flags):
    grid = of((4, CX + 1, 2, 8, 128))
    return kernel_call(
        deposit_kernel, "deposit", [grid, grid, slab_shape(0, 1), slab_shape(0, -1)], [], (cells, tag, flags)
    )


def smem():
    return pl.BlockSpec(memory_space=pltpu.SMEM)


def vmem():
    return pl.BlockSpec(memory_space=pltpu.VMEM)


def add_rows(ref, place, row, rows):
    at = (*place, slice(row, row + rows.shape[0]))
    ref[at] = ref[at] + rows


def widen_kernel(
    keep_ref, grid_ref, rim_ref, low_ref, high_ref, flag_ref, after_ref, vel_ref, edge_ref, fluid_ref, up_ref, down_ref, ext
):
    zero = jnp.zeros((2, 8, 128), F32)
    for x in range(CX + 1):
        for f in range(4):
            ext[f, x, :, 0:8] = zero
            ext[f, x, :, 8:16] = grid_ref[f, x]
            ext[f, x, :, 16:24] = rim_ref[f, x]
        if x < CX:
            fluid_ref[x, :, 0:8] = zero
            fluid_ref[x, :, 16:24] = zero
            for h in range(2):
                fluid_ref[x, h, 8:16] = flag_ref[x, :, 128 * h : 128 * h + 128].astype(F32)
    arrived = []
    for dy, ref in ((1, low_ref), (-1, high_ref)):
        for field, x, half, first, count, at in pieces(0, dy)[0]:
            arrived.append((field, x, half, first - dy * CY + 8, ref[at : at + count]))
    for field, x, half, row, rows in arrived:
        if field < 4:
            add_rows(ext, (field, x, half), row, rows)
        elif field == 7:
            fluid_ref[x, half, row : row + rows.shape[0]] = rows
    for f in range(4):
        for x in range(CX + 1):
            ext[f, x, :, 16:24] = keep_ref[1] * ext[f, x, :, 16:24]
        edge_ref[f, 0], edge_ref[f, 1] = ext[f, 0], ext[f, CX]
    for x in range(1, CX):
        inverse = 1.0 / jnp.maximum(ext[0, x], 0.5)
        for d in range(3):
            vel_ref[d, x] = ext[1 + d, x] * inverse
    for field, x, half, row, rows in arrived:
        if 4 <= field < 7:
            vel_ref[field - 4, x, half, row : row + rows.shape[0]] = rows
    for dx, ref in ((1, up_ref), (-1, down_ref)):
        listed = pieces(dx, 0)[0]
        clear_end(ref, listed)
        for field, x, half, first, count, at in listed:
            source = ext.at[field] if field < 4 else fluid_ref if field == 7 else vel_ref.at[field - 4]
            ref[at : at + count] = source[x, half, first + 8 : first + 8 + count]


def widen(keep, *args):
    wide = (CX, 2, 24, 128)
    return kernel_call(
        widen_kernel,
        "widen",
        (of((3, *wide)), of((4, 2, 2, 24, 128)), of(wide), slab_shape(1, 0), slab_shape(-1, 0)),
        [(4, CX + 1, 2, 24, 128)],
        (keep, *args),
        [smem()] + [vmem()] * 5 + [pl.BlockSpec(memory_space=pl.ANY)],
    )


def krylov_kernel(
    keep_ref, near_ref, edge_ref, flag_ref, low_ref, high_ref, vel_ref, fluid_ref, k0_ref, k1_ref, k2_ref, sums_ref, edge
):
    zero = jnp.zeros((2, 24, 128), F32)
    for plane in range(25):
        inner = 4 < plane < 20
        for d in range(3):
            vel_ref[d, plane] = near_ref[d, plane - 4] if inner else zero
        fluid_ref[plane] = flag_ref[plane - 4] if 4 <= plane < 20 else zero
    for f in range(4):
        edge[f, 0], edge[f, 1] = edge_ref[f, 0], edge_ref[f, 1]
    for dx, ref in ((1, low_ref), (-1, high_ref)):
        for field, x, half, first, count, at in pieces(dx, 0)[0]:
            rows, row, plane = ref[at : at + count], first + 8, x - dx * CX + 4
            if field < 4:
                add_rows(edge, (field, (plane - 4) // CX, half), row, rows)
            elif field == 7:
                fluid_ref[plane, half, row : row + count] = rows
            else:
                vel_ref[field - 4, plane, half, row : row + count] = rows
    for side, plane, keep in ((0, 4, 1.0), (1, 20, keep_ref[0])):
        inverse = keep / jnp.maximum(edge[0, side], 0.5)
        for d in range(3):
            vel_ref[d, plane] = edge[1 + d, side] * inverse
    for plane in range(1, 24):
        vy, vz = vel_ref[1, plane], vel_ref[2, plane]
        divergence = (
            0.5 * (vel_ref[0, plane + 1] - vel_ref[0, plane - 1])
            + 0.5 * (y_shift(vy, -1) - y_shift(vy, 1))
            + 0.5 * (z_ahead(vz) - z_behind(vz))
        )
        k0_ref[plane] = -fluid_ref[plane] * divergence

    def applied(ref, plane):
        a = ref[plane]
        beside = (
            ref[plane + 1] + ref[plane - 1] + y_shift(a, 1) + y_shift(a, -1) + z_ahead(a) + z_behind(a)
        )
        return fluid_ref[plane] * (a - beside * (1.0 / 6.0))

    for plane in range(2, 23):
        k1_ref[plane] = applied(k0_ref, plane)
    for plane in range(3, 22):
        k2_ref[plane] = applied(k1_ref, plane)
    totals = [jnp.zeros((2, 8, 128), F32)] * 14
    for plane in range(4, 20):
        k0, k1, k2 = [ref[plane, :, 8:16] for ref in (k0_ref, k1_ref, k2_ref)]
        k3 = applied(k2_ref, plane)[:, 8:16]
        u1, w1 = k0 - k1, k1 - k2
        u2 = u1 - w1
        w2 = w1 - (k2 - k3)
        pairs = (
            (k0, k0), (k0, k1), (k1, k1), (k1, k2), (k2, k2), (k2, k3),
            (k0, u1), (u1, u1), (u1, u2), (u2, u2), (k0, w1), (u1, w1), (u1, w2), (u2, w2),
        )
        totals = [t + a * b for t, (a, b) in zip(totals, pairs)]
    for i, t in enumerate(totals):
        sums_ref[i : i + 1] = jnp.sum(t[0] + t[1], axis=0, keepdims=True)
    sums_ref[14:16] = jnp.zeros((2, 128), F32)


def krylov(keep, *args):
    return kernel_call(
        krylov_kernel,
        "krylov",
        (of((3, 25, 2, 24, 128)),) + (of((25, 2, 24, 128)),) * 4 + (of((16, 128)),),
        [(4, 2, 2, 24, 128)],
        (keep, *args),
        [smem()] + [vmem()] * 5,
    )


def steps_from(gram, energy, apply_once):
    def form(a, table):
        total = None
        for i, p in enumerate(a):
            for j, q in enumerate(a):
                if p is not None and q is not None:
                    term = p * q * table[i + j]
                    total = term if total is None else total + term
        return total

    def ratio(a, b):
        return jnp.where(b > 0.0, a / jnp.where(b > 0.0, b, 1.0), 0.0)

    one, zero = jnp.ones_like(gram[0]), jnp.zeros_like(gram[0])
    residual, direction, answer = [one], [one], [zero] * 3
    norm = gram[0]
    for step in range(3):
        alpha = ratio(norm, form(direction, energy))
        for i, p in enumerate(direction):
            answer[i] = answer[i] + alpha * p
        if step == 2:
            return answer
        image = apply_once(direction, zero)
        residual = [a - alpha * b for a, b in zip(residual + [zero], image)]
        norm_next = form(residual, gram)
        direction = [a + ratio(norm_next, norm) * b for a, b in zip(residual, direction + [zero])]
        norm = norm_next


def coefficients(m):
    power = steps_from(m[0:5], m[1:6], lambda a, zero: [zero] + a)
    shifted = steps_from(
        [m[0]] + m[6:10],
        [m[1]] + m[10:14],
        lambda a, zero: [p - q for p, q in zip(a + [zero], [zero] + a)],
    )
    turned = [shifted[0] + shifted[1] + shifted[2], -shifted[1] - 2.0 * shifted[2], shifted[2]]
    smooth = m[1] < 0.3 * m[0]
    return [jnp.where(smooth, a, b) * (1.0 / 6.0) for a, b in zip(power, turned)]


def interpolate_kernel(tag_ref, fluid_ref, *refs):
    *fields, out_ref, proj = refs
    for x in range(CX + 1):
        fluid = fluid_ref[x + 4, :, 8:24]
        channel = 0
        for ref in fields:
            if len(ref.shape) == 5:
                parts = [fluid * ref[d, x + 4, :, 8:24] for d in range(3)]
            else:
                p, scale = ref[x + 4], -0.5 * fluid
                inner = p[:, 8:24]
                parts = [
                    scale * (ref[x + 5, :, 8:24] - ref[x + 3, :, 8:24]),
                    scale * (y_shift(p, -1) - y_shift(p, 1))[:, 8:24],
                    scale * (z_ahead(inner) - z_behind(inner)),
                ]
            for part in parts:
                for j, rows in enumerate((part[:, 0:8], y_shift(part, -1)[:, 0:8])):
                    proj[x, channel, j, 0] = rows
                    proj[x, channel, j, 1] = z_ahead(rows)
                channel += 1
    for x in range(CX):
        code = tag_ref[0, 2 * x : 2 * x + 2] >> 15
        fx, fy, fz = fractions(code)
        wx, wy, wz = (1.0 - fx, fx), (1.0 - fy, fy), (1.0 - fz, fz)
        w = {(i, j, k): wx[i] * wy[j] * wz[k] for i in (0, 1) for j in (0, 1) for k in (0, 1)}
        for c in range(6):
            result = None
            for (i, j, k), weight in w.items():
                term = weight * proj[x + i, c, j, k]
                result = term if result is None else result + term
            out_ref[c, 2 * x : 2 * x + 2] = result


def interpolate(*args):
    return kernel_call(
        interpolate_kernel,
        "interpolate",
        (of((6, TILES, 8, 128)),),
        [(CX + 1, 6, 2, 2, 2, 8, 128)],
        args,
        flops=10**7,
    )[0]


def finish_kernel(
    sums_ref, k0_ref, k1_ref, k2_ref, first_ref, second_ref, lane_ref, sub_ref, swap_ref, pressure_ref, out_ref
):
    total = jnp.sum(sums_ref[...], axis=1, keepdims=True)
    c = coefficients([jnp.broadcast_to(total[i : i + 1], (8, 128)) for i in range(14)])
    for i in range(TILES):
        for d in range(3):
            out_ref[d, i] = (
                first_ref[d, i]
                + c[0] * first_ref[3 + d, i]
                + c[1] * second_ref[d, i]
                + c[2] * second_ref[3 + d, i]
            )
    follow_plan([(out_ref, d) for d in range(3)], lane_ref, sub_ref, swap_ref)
    for x in range(CX):
        for h in range(2):
            k0, k1, k2 = [ref[x + 4, h, 8:16] for ref in (k0_ref, k1_ref, k2_ref)]
            pressure_ref[x, :, 128 * h : 128 * h + 128] = c[0] * k0 + c[1] * k1 + c[2] * k2


def finish(*args):
    return kernel_call(finish_kernel, "finish", (of((CX, CY, 256)), of((3, TILES, 8, 128))), [], args)


def neighbours(up, down, axis):
    count = lax.axis_size(axis)
    odd = lax.axis_index(axis) % 2 == 1
    high_rows, low_rows = down.shape[0], up.shape[0]
    up = jnp.concatenate([up, jnp.zeros((high_rows - low_rows, 128), F32)])
    arrived = []
    for first, slab in ((0, jnp.where(odd, down, up)), (1, jnp.where(odd, up, down))):
        pairs = [(i, i + 1) for i in range(first, count - 1, 2)]
        arrived.append(lax.ppermute(slab, axis, pairs + [(b, a) for a, b in pairs]))
    return jnp.where(odd, arrived[0], arrived[1]), jnp.where(odd, arrived[1], arrived[0])


def summed(sums, axis):
    count = lax.axis_size(axis)
    parts = [sums]
    for shift in range(1, count):
        swaps = [(i, i ^ shift) for i in range(count)]
        if max(b for _, b in swaps) >= count:
            swaps = [(i, (i + shift) % count) for i in range(count)]
        parts.append(lax.ppermute(sums, axis, swaps))
    return functools.reduce(jnp.add, parts)


def local(cell_index, offset_code, particle_state, fluid_flags):
    places = [(axis, lax.axis_index(axis), lax.axis_size(axis)) for axis in ("gx", "gy")]
    keep = jnp.stack([(at + 1 < size).astype(F32) for _, at, size in places])
    cells, tag = to_cells(offset_code, particle_state, *cell_rows(cell_index.reshape(256, 128)))
    grid, rim, up, down = deposit(cells, tag, fluid_flags)
    low, high = neighbours(up, down, "gy")
    plan = particle_plan(tag.reshape(256, 128))
    near, edge, flags, up, down = widen(keep, grid, rim, low, high, fluid_flags, plan[1])
    low, high = neighbours(up, down, "gx")
    vel, fluid, k0, k1, k2, sums = krylov(keep, near, edge, flags, low, high)
    first = interpolate(tag, fluid, vel, k0)
    sums, first, tag = lax.optimization_barrier((summed(sums, "gx"), first, tag))
    second = interpolate(tag, fluid, k1, k2)
    pressure, result = finish(summed(sums, "gy"), k0, k1, k2, first, second, *plan)
    return pressure, result.reshape(1, 3, CELLS)


def solution(mesh):
    return jax.shard_map(
        local,
        mesh=mesh,
        in_specs=(
            P(("groups", "gx", "gy"), None),
            P(("groups", "gx", "gy"), None),
            P(("groups", "gx", "gy"), None, None),
            P(("groups", "gx"), "gy", None),
        ),
        out_specs=(P(("groups", "gx"), "gy", None), P(("groups", "gx", "gy"), None, None)),
        check_vma=False,
    )
```

```python
import functools
import math

import jax
import jax.numpy as jnp
from jax import lax
from jax.experimental import pallas as pl
from jax.experimental.pallas import tpu as pltpu
from jax.sharding import PartitionSpec as P

F32, I32 = jnp.float32, jnp.int32
CX, CY, CELLS = 16, 8, 32768
TILES = CELLS // 1024
LANE_RUNS, SUB_RUNS, SWAPS = 9, 3, 30 * 16
GROUP = 4


def take(x, index, axis):
    other = tuple(d for d in range(x.ndim) if d != axis)
    dims = lax.GatherDimensionNumbers(
        offset_dims=(),
        collapsed_slice_dims=(axis,),
        start_index_map=(axis,),
        operand_batching_dims=other,
        start_indices_batching_dims=other,
    )
    return lax.gather(
        x, index[..., None], dims, (1,) * x.ndim, mode=lax.GatherScatterMode.PROMISE_IN_BOUNDS
    )


def iota(shape, dim):
    return lax.broadcasted_iota(I32, shape, dim)


class Lanes:
    def __init__(self, lane_bits):
        self.tiles = [None] * TILES
        self.tile_bits = [7, 8, 9, 10, 11]
        self.lane_bits = list(lane_bits)

    def trade(self, slot, lane):
        self.tile_bits[slot], self.lane_bits[lane] = self.lane_bits[lane], self.tile_bits[slot]
        if self.tiles[0] is None:
            return
        stride, hop = 1 << lane, 1 << slot
        low = iota((8, 128), 1) & stride == 0
        for i in range(TILES):
            if i & hop == 0:
                a, b = self.tiles[i], self.tiles[i + hop]
                self.tiles[i] = jnp.where(low, a, pltpu.roll(b, stride, 1))
                self.tiles[i + hop] = jnp.where(low, pltpu.roll(a, 128 - stride, 1), b)

    def bring(self, bit, out):
        if bit not in self.tile_bits:
            self.trade(self.tile_bits.index(out), self.lane_bits.index(bit))

    def compare(self, bit):
        if self.tiles[0] is None:
            return
        hop = 1 << self.tile_bits.index(bit)
        for i in range(TILES):
            if i & hop == 0:
                a, b = self.tiles[i], self.tiles[i + hop]
                self.tiles[i], self.tiles[i + hop] = jnp.minimum(a, b), jnp.maximum(a, b)

    def turn(self, bit, mask):
        if self.tiles[0] is None:
            return
        if bit in self.tile_bits:
            hop = 1 << self.tile_bits.index(bit)
            self.tiles = [t ^ mask if i & hop else t for i, t in enumerate(self.tiles)]
        else:
            here = iota((8, 128), 1) & (1 << self.lane_bits.index(bit)) != 0
            self.tiles = [t ^ jnp.where(here, mask, 0) for t in self.tiles]

    def sort_rows(self, mask):
        for bit in range(5):
            self.bring(bit, 7 + bit)
        for phase in range(1, 8):
            self.turn(phase, mask)
            if phase == 6:
                self.bring(5, 0)
                self.compare(5)
            if phase == 7:
                self.bring(6, 0)
                self.compare(6)
                self.bring(5, 6)
                self.compare(5)
            for bit in reversed(range(min(phase, 5))):
                self.bring(bit, 5)
                self.compare(bit)
            self.turn(phase, mask)
        for bit in range(5):
            self.bring(7 + bit, bit)

    def merge_rows(self, tick=lambda: None):
        out = 7
        for bit in reversed(range(7)):
            self.bring(bit, out)
            self.compare(bit)
            out = bit
            tick()
        self.bring(7, 0)
        tick()


def first_layout():
    dry = Lanes(range(7))
    dry.sort_rows(0)
    for _ in range(8):
        dry.merge_rows()
    return [dry.lane_bits.index(bit) for bit in range(7)]


def record_run(run, tiles, lane_ref):
    for i, t in enumerate(tiles):
        lane_ref[run, 8 * i : 8 * i + 8] = t & 127
    return [t >> 7 for t in tiles]


def plan_rows(tiles, lane_ref):
    state = Lanes(first_layout())
    state.tiles = [(t << 7) | iota((8, 128), 1) for t in tiles]
    state.sort_rows(0x7FFF << 7)
    return record_run(0, state.tiles, lane_ref)


def sort_plan(tiles, lane_ref, sub_ref, swap_ref):
    plan_rest(plan_rows(tiles, lane_ref), lane_ref, sub_ref, swap_ref)


def plan_rest(tiles, lane_ref, sub_ref, swap_ref, begin=lambda phase: None, tick=lambda: None):
    lanes, subs = iota((8, 128), 1), iota((8, 128), 0)
    top = 0x7FFF

    state = Lanes(first_layout())
    state.sort_rows(0)
    swap = 0
    for phase in range(8, 16):
        begin(phase)
        if phase < 12:
            turns = [top if i >> (phase - 7) & 1 else 0 for i in range(TILES)]
        elif phase < 15:
            turns = [jnp.where(subs & (1 << (phase - 12)) != 0, top, 0)] * TILES
        else:
            turns = [0] * TILES
        tiles = [t ^ f for t, f in zip(tiles, turns)]
        if phase > 12:
            tiles = [(t << 3) | subs for t in tiles]
            stride = 1 << (phase - 13)
            while stride:
                low = subs & stride == 0
                other = [
                    pltpu.roll(t, 4, 0) if stride == 4 else take(t, subs ^ stride, 0) for t in tiles
                ]
                tiles = [
                    jnp.where(low, jnp.minimum(t, o), jnp.maximum(t, o)) for t, o in zip(tiles, other)
                ]
                stride //= 2
            for i, t in enumerate(tiles):
                sub_ref[phase - 13, 8 * i : 8 * i + 8] = t & 7
            tiles = [t >> 3 for t in tiles]
        hop = 1 << (min(phase, 12) - 8)
        while hop:
            for i in range(TILES):
                if i & hop == 0:
                    a, b = tiles[i], tiles[i + hop]
                    swap_ref[8 * swap : 8 * swap + 8] = jnp.where(a > b, 1, 0)
                    swap += 1
                    tiles[i], tiles[i + hop] = jnp.minimum(a, b), jnp.maximum(a, b)
            hop //= 2
        state.tiles = [(t << 7) | lanes for t in tiles]
        state.merge_rows(tick)
        tiles = [t ^ f for t, f in zip(record_run(phase - 7, state.tiles, lane_ref), turns)]


def follow_plan(stages, lane_ref, sub_ref, swap_ref, sources=None):
    def crossings(hops, before):
        out = {}
        for hop in hops:
            for i in range(TILES):
                if i & hop == 0:
                    out[hop, i] = before
                    before += 1
        return out, before

    def pass_over(sets, work, sources=stages):
        for members in sets:
            moved = [{i: ref[c, i] for i in members} for ref, c in sources]
            work(members, moved)
            for (ref, c), tiles in zip(stages, moved):
                for i, t in tiles.items():
                    ref[c, i] = t

    def gathered(ref, run, axis, members, moved):
        for i in members:
            index = ref[run, 8 * i : 8 * i + 8]
            for tiles in moved:
                tiles[i] = take(tiles[i], index, axis)

    def exchanged(hops, number, members, moved):
        for hop in hops:
            for i in members:
                if i & hop == 0:
                    at = 8 * number[hop, i]
                    crossed = swap_ref[at : at + 8] != 0
                    for tiles in moved:
                        a, b = tiles[i], tiles[i + hop]
                        tiles[i], tiles[i + hop] = jnp.where(crossed, b, a), jnp.where(crossed, a, b)

    eights = [range(8 * g, 8 * g + 8) for g in range(4)]
    numbers, before = {}, 0
    for phase in range(8, 16):
        hops = [1 << k for k in reversed(range(min(phase, 12) - 7))]
        numbers[phase], before = crossings(hops, before)

    def first(members, moved):
        gathered(lane_ref, 0, 1, members, moved)
        for phase in (8, 9, 10):
            exchanged([4, 2, 1][10 - phase :], numbers[phase], members, moved)
            gathered(lane_ref, phase - 7, 1, members, moved)

    pass_over(eights, first, sources or stages)
    for phase in range(11, 16):
        wide = [16, 8] if phase > 11 else [8]
        reach = 32 if phase > 11 else 16
        sets = [range(low + k, low + reach, 8) for low in range(0, 32, reach) for k in range(8)]

        def across(members, moved):
            if phase > 12:
                gathered(sub_ref, phase - 13, 0, members, moved)
            exchanged(wide, numbers[phase], members, moved)

        def within(members, moved):
            exchanged([4, 2, 1], numbers[phase], members, moved)
            gathered(lane_ref, phase - 7, 1, members, moved)

        pass_over(sets, across)
        pass_over(eights, within)


def crossings(phase):
    before, numbers = 0, {}
    for p in range(8, phase + 1):
        for k in reversed(range(min(p, 12) - 7)):
            for i in range(TILES):
                if i & (1 << k) == 0:
                    if p == phase:
                        numbers[1 << k, i] = before
                    before += 1
    return numbers


def move_items(phase, stages, sources, lane_ref, sub_ref, swap_ref):
    numbers = crossings(phase)

    def item(members, sources, steps):
        def work():
            moved = [{i: ref[c, i] for i in members} for ref, c in sources]
            for step in steps:
                step(members, moved)
            for (ref, c), tiles in zip(stages, moved):
                for i, t in tiles.items():
                    ref[c, i] = t

        return work

    def gathered(ref, run, axis):
        def step(members, moved):
            for i in members:
                index = ref[run, 8 * i : 8 * i + 8]
                for tiles in moved:
                    tiles[i] = take(tiles[i], index, axis)

        return step

    def exchanged(*hops):
        def step(members, moved):
            for hop in hops:
                for i in members:
                    if i & hop == 0:
                        at = 8 * numbers[hop, i]
                        crossed = swap_ref[at : at + 8] != 0
                        for tiles in moved:
                            a, b = tiles[i], tiles[i + hop]
                            tiles[i], tiles[i + hop] = jnp.where(crossed, b, a), jnp.where(crossed, a, b)

        return step

    items = []
    if phase > 10:
        spread = 32 if phase > 11 else 16
        steps = [gathered(sub_ref, phase - 13, 0)] if phase > 12 else []
        steps.append(exchanged(16, 8) if phase > 11 else exchanged(8))
        for low in range(0, 32, spread):
            items += [item(range(low + k, low + spread, 8), stages, steps) for k in range(8)]
    steps = [gathered(lane_ref, 0, 1)] if phase == 8 else []
    steps.append(exchanged(*[4, 2, 1][max(0, 10 - phase) :]))
    steps.append(gathered(lane_ref, phase - 7, 1))
    return items + [
        item(range(8 * g, 8 * g + 8), sources if phase == 8 else stages, steps) for g in range(4)
    ]


def plan_shapes():
    return [(LANE_RUNS, 256, 128), (SUB_RUNS, 256, 128), (8 * SWAPS, 128)]


def plan_scratch():
    return [pltpu.VMEM(shape, I32) for shape in plan_shapes()]


def split_tiles(array):
    return [array[8 * i : 8 * i + 8] for i in range(TILES)]


def z_behind(a):
    r = pltpu.roll(a, 1, 2)
    fill = jnp.concatenate([jnp.zeros_like(r[:1]), r[:1]], axis=0)
    return jnp.where(iota(a.shape, 2) == 0, fill, r)


def z_ahead(a):
    r = pltpu.roll(a, 127, 2)
    fill = jnp.concatenate([r[1:], jnp.zeros_like(r[:1])], axis=0)
    return jnp.where(iota(a.shape, 2) == 127, fill, r)


def y_shift(a, steps):
    return jnp.stack([pltpu.roll(a[h], steps % a.shape[1], 0) for h in range(2)])


def fractions(code):
    return [((code >> shift & 3).astype(F32) + 0.5) * 0.25 for shift in (0, 2, 4)]


PLANES = {1: range(12, 17), 0: range(17), -1: range(5)}
ROWS = {1: range(4, 9), -1: range(5)}


def reach(place, last):
    return max(0, -place, place - last)


def pieces(dx, dy):
    at, out = 0, []
    for plane in PLANES[dx]:
        far_x = reach(plane - dx * CX, CX)
        for field in range(8):
            rows = []
            for row in ROWS[dy] if dy else range(-4, 13):
                far_y = reach(row - dy * CY, CY)
                read = [
                    max(far_x - 1, 0) + far_y <= 3,
                    far_x + max(far_y - 1, 0) <= 3,
                    far_x + far_y <= 3,
                ]
                shared = plane in (0, CX) or (dy != 0 and row in (0, CY))
                if field == 7:
                    wanted = read[2] and plane < CX and (row < CY or not dy)
                elif field == 0:
                    wanted = shared and any(read)
                else:
                    wanted = read[(field - 1) % 3] and shared == (field < 4)
                if wanted:
                    rows.append(row)
            while rows:
                count = 1
                while count < len(rows) and rows[count] == rows[0] + count:
                    count += 1
                for half in range(2):
                    out.append((field, plane, half, rows[0], count, at))
                    at += count
                rows = rows[count:]
    return out, -(-at // 8) * 8


def slab_shape(dx, dy):
    return of((pieces(dx, dy)[1], 128))


def clear_end(ref, listed):
    used = listed[-1][4] + listed[-1][5]
    if used < ref.shape[0]:
        ref[used:] = jnp.zeros((ref.shape[0] - used, 128), F32)


def particle_plan_kernel(tag_ref, lane_ref, sub_ref, swap_ref):
    k = tag_ref[...] & 0x7FFF
    key = ((k & 0x380) << 5) | ((k & 0x7C00) >> 3) | (k & 0x7F)
    sort_plan(split_tiles(key), lane_ref, sub_ref, swap_ref)


def particle_plan(tag):
    outs = [of(shape, I32) for shape in plan_shapes()]
    return kernel_call(particle_plan_kernel, "particle_plan", outs, [], (tag,), flops=10**7)


def cell_rows_kernel(cell_ref, key_ref, lane_ref):
    k = cell_ref[...]
    key = ((k & 0x700) << 4) | ((k & 0x7800) >> 3) | (k & 0xFF)
    for i, t in enumerate(plan_rows(split_tiles(key), lane_ref)):
        key_ref[8 * i : 8 * i + 8] = t


def cell_rows(cell):
    outs = [of((256, 128), I32), of((1, 256, 128), I32)]
    return kernel_call(cell_rows_kernel, "cell_rows", outs, [], (cell,), flops=3 * 10**9)


def to_cells_kernel(code_ref, state_ref, key_ref, rows_ref, cells_ref, tag_ref, lane_ref, sub_ref, swap_ref):
    shape = (TILES, 8, 128)
    tag_ref[0] = (code_ref[...] << 15) | (iota(shape, 0) * 8 + iota(shape, 1)) * 128 + iota(shape, 2)
    lane_ref[0] = rows_ref[0]
    stages = [(tag_ref, 0)] + [(cells_ref, c) for c in range(12)]
    sources = [(tag_ref, 0)] + [(state_ref, c) for c in range(12)]
    waiting, pace = [], [0]

    def begin(phase):
        while waiting:
            waiting.pop(0)()
        if phase > 8:
            for low in range(0, 13, GROUP):
                chosen = slice(low, low + GROUP)
                waiting.extend(
                    move_items(phase - 1, stages[chosen], sources[chosen], lane_ref, sub_ref, swap_ref)
                )
        pace[0] = -(-len(waiting) // 8)

    def tick():
        for _ in range(min(pace[0], len(waiting))):
            waiting.pop(0)()

    plan_rest(split_tiles(key_ref[...]), lane_ref, sub_ref, swap_ref, begin, tick)
    begin(16)
    while waiting:
        waiting.pop(0)()


def to_cells(code, state, key, rows):
    return kernel_call(
        to_cells_kernel,
        "to_cells",
        (of((12, TILES, 8, 128)), of((1, TILES, 8, 128), I32)),
        plan_scratch(),
        (code.reshape(TILES, 8, 128), state.reshape(12, TILES, 8, 128), key, rows),
        flops=10**7,
    )


def deposit_kernel(cells_ref, tag_ref, flag_ref, grid_ref, rim_ref, up_ref, down_ref):
    wanted = {}
    for dy, ref in ((1, up_ref), (-1, down_ref)):
        listed = pieces(0, dy)[0]
        clear_end(ref, listed)
        for field, plane, half, first, count, at in listed:
            wanted.setdefault((field, plane), []).append((ref, half, first, count, at))

    def hand_out(field, plane, main, rim):
        for ref, half, first, count, at in wanted.get((field, plane), ()):
            inside = min(count, CY - first)
            if inside > 0:
                ref[at : at + inside] = main[half, first : first + inside]
            if inside < count:
                ref[at + count - 1 : at + count] = rim[half, 0:1]

    first_row = iota((2, 8, 128), 1) == 0
    before = None
    for x in range(CX + 1):
        here = []
        if x < CX:
            code = tag_ref[0, 2 * x : 2 * x + 2] >> 15
            fx, fy, fz = fractions(code)
            wx, wy, wz = (1.0 - fx, fx), (1.0 - fy, fy), (1.0 - fz, fz)
            w = {(i, j, k): wx[i] * wy[j] * wz[k] for i in (0, 1) for j in (0, 1) for k in (0, 1)}
            here.append(w)
            for comp in range(3):
                v, c0, c1, c2 = [
                    cells_ref[c, 2 * x : 2 * x + 2]
                    for c in (comp, 3 + 3 * comp, 4 + 3 * comp, 5 + 3 * comp)
                ]
                base = v - c0 * fx - c1 * fy - c2 * fz
                terms = {}
                for i in (0, 1):
                    a = base + c0 if i else base
                    for j in (0, 1):
                        b = a + c1 if j else a
                        for k in (0, 1):
                            terms[i, j, k] = w[i, j, k] * (b + c2 if k else b)
                here.append(terms)
        for f in range(4):
            s = {}
            for j in (0, 1):
                for k in (0, 1):
                    parts = []
                    if x < CX:
                        parts.append(here[f][0, j, k])
                    if x > 0:
                        parts.append(before[f][1, j, k])
                    s[j, k] = sum(parts[1:], parts[0])
            near, far = [s[j, 0] + z_behind(s[j, 1]) for j in (0, 1)]
            turned = y_shift(far, 1)
            main = near + jnp.where(first_row, 0.0, turned)
            rim = jnp.where(first_row, turned, 0.0)
            grid_ref[f, x], rim_ref[f, x] = main, rim
            hand_out(f, x, main, rim)
            if f == 0:
                inverse = 1.0 / jnp.maximum(main, 0.5)
            else:
                hand_out(3 + f, x, main * inverse, None)
        if x < CX:
            flags = jnp.stack([flag_ref[x, :, 128 * h : 128 * h + 128] for h in range(2)])
            hand_out(7, x, flags.astype(F32), None)
        before = here


def tiled_bytes(shape):
    *outer, rows, columns = shape
    return 4 * math.prod(outer) * (-(-rows // 8) * 8) * (-(-columns // 128) * 128)


def kernel_call(body, name, outs, scratch, args, in_specs=None, flops=0):
    scratch = [x if hasattr(x, "dtype") else pltpu.VMEM(x, F32) for x in scratch]
    size = sum(tiled_bytes(x.shape) for x in (*args, *outs, *scratch) if len(x.shape) > 1)
    return pl.pallas_call(
        body,
        out_shape=outs,
        **({} if in_specs is None else dict(in_specs=in_specs)),
        scratch_shapes=scratch,
        compiler_params=pltpu.CompilerParams(vmem_limit_bytes=size + 4 * 2**20),
        cost_estimate=pl.CostEstimate(flops=flops, bytes_accessed=size, transcendentals=0),
        name=name,
    )(*args)


def of(shape, kind=F32):
    return jax.ShapeDtypeStruct(shape, kind)


def deposit(cells, tag, flags):
    grid = of((4, CX + 1, 2, 8, 128))
    return kernel_call(
        deposit_kernel, "deposit", [grid, grid, slab_shape(0, 1), slab_shape(0, -1)], [], (cells, tag, flags)
    )


def smem():
    return pl.BlockSpec(memory_space=pltpu.SMEM)


def vmem():
    return pl.BlockSpec(memory_space=pltpu.VMEM)


def add_rows(ref, place, row, rows):
    at = (*place, slice(row, row + rows.shape[0]))
    ref[at] = ref[at] + rows


def widen_kernel(
    keep_ref, grid_ref, rim_ref, low_ref, high_ref, flag_ref, after_ref, vel_ref, edge_ref, fluid_ref, up_ref, down_ref, ext
):
    zero = jnp.zeros((2, 8, 128), F32)
    for x in range(CX + 1):
        for f in range(4):
            ext[f, x, :, 0:8] = zero
            ext[f, x, :, 8:16] = grid_ref[f, x]
            ext[f, x, :, 16:24] = rim_ref[f, x]
        if x < CX:
            fluid_ref[x, :, 0:8] = zero
            fluid_ref[x, :, 16:24] = zero
            for h in range(2):
                fluid_ref[x, h, 8:16] = flag_ref[x, :, 128 * h : 128 * h + 128].astype(F32)
    arrived = []
    for dy, ref in ((1, low_ref), (-1, high_ref)):
        for field, x, half, first, count, at in pieces(0, dy)[0]:
            arrived.append((field, x, half, first - dy * CY + 8, ref[at : at + count]))
    for field, x, half, row, rows in arrived:
        if field < 4:
            add_rows(ext, (field, x, half), row, rows)
        elif field == 7:
            fluid_ref[x, half, row : row + rows.shape[0]] = rows
    for f in range(4):
        for x in range(CX + 1):
            ext[f, x, :, 16:24] = keep_ref[1] * ext[f, x, :, 16:24]
        edge_ref[f, 0], edge_ref[f, 1] = ext[f, 0], ext[f, CX]
    for x in range(1, CX):
        inverse = 1.0 / jnp.maximum(ext[0, x], 0.5)
        for d in range(3):
            vel_ref[d, x] = ext[1 + d, x] * inverse
    for field, x, half, row, rows in arrived:
        if 4 <= field < 7:
            vel_ref[field - 4, x, half, row : row + rows.shape[0]] = rows
    for dx, ref in ((1, up_ref), (-1, down_ref)):
        listed = pieces(dx, 0)[0]
        clear_end(ref, listed)
        for field, x, half, first, count, at in listed:
            source = ext.at[field] if field < 4 else fluid_ref if field == 7 else vel_ref.at[field - 4]
            ref[at : at + count] = source[x, half, first + 8 : first + 8 + count]


def widen(keep, *args):
    wide = (CX, 2, 24, 128)
    return kernel_call(
        widen_kernel,
        "widen",
        (of((3, *wide)), of((4, 2, 2, 24, 128)), of(wide), slab_shape(1, 0), slab_shape(-1, 0)),
        [(4, CX + 1, 2, 24, 128)],
        (keep, *args),
        [smem()] + [vmem()] * 5 + [pl.BlockSpec(memory_space=pl.ANY)],
    )


def krylov_kernel(
    keep_ref, near_ref, edge_ref, flag_ref, low_ref, high_ref, vel_ref, fluid_ref, k0_ref, k1_ref, k2_ref, sums_ref, edge
):
    zero = jnp.zeros((2, 24, 128), F32)
    for plane in range(25):
        inner = 4 < plane < 20
        for d in range(3):
            vel_ref[d, plane] = near_ref[d, plane - 4] if inner else zero
        fluid_ref[plane] = flag_ref[plane - 4] if 4 <= plane < 20 else zero
    for f in range(4):
        edge[f, 0], edge[f, 1] = edge_ref[f, 0], edge_ref[f, 1]
    for dx, ref in ((1, low_ref), (-1, high_ref)):
        for field, x, half, first, count, at in pieces(dx, 0)[0]:
            rows, row, plane = ref[at : at + count], first + 8, x - dx * CX + 4
            if field < 4:
                add_rows(edge, (field, (plane - 4) // CX, half), row, rows)
            elif field == 7:
                fluid_ref[plane, half, row : row + count] = rows
            else:
                vel_ref[field - 4, plane, half, row : row + count] = rows
    for side, plane, keep in ((0, 4, 1.0), (1, 20, keep_ref[0])):
        inverse = keep / jnp.maximum(edge[0, side], 0.5)
        for d in range(3):
            vel_ref[d, plane] = edge[1 + d, side] * inverse
    for plane in range(1, 24):
        vy, vz = vel_ref[1, plane], vel_ref[2, plane]
        divergence = (
            0.5 * (vel_ref[0, plane + 1] - vel_ref[0, plane - 1])
            + 0.5 * (y_shift(vy, -1) - y_shift(vy, 1))
            + 0.5 * (z_ahead(vz) - z_behind(vz))
        )
        k0_ref[plane] = -fluid_ref[plane] * divergence

    def applied(ref, plane):
        a = ref[plane]
        beside = (
            ref[plane + 1] + ref[plane - 1] + y_shift(a, 1) + y_shift(a, -1) + z_ahead(a) + z_behind(a)
        )
        return fluid_ref[plane] * (a - beside * (1.0 / 6.0))

    for plane in range(2, 23):
        k1_ref[plane] = applied(k0_ref, plane)
    for plane in range(3, 22):
        k2_ref[plane] = applied(k1_ref, plane)
    totals = [jnp.zeros((2, 8, 128), F32)] * 14
    for plane in range(4, 20):
        k0, k1, k2 = [ref[plane, :, 8:16] for ref in (k0_ref, k1_ref, k2_ref)]
        k3 = applied(k2_ref, plane)[:, 8:16]
        u1, w1 = k0 - k1, k1 - k2
        u2 = u1 - w1
        w2 = w1 - (k2 - k3)
        pairs = (
            (k0, k0), (k0, k1), (k1, k1), (k1, k2), (k2, k2), (k2, k3),
            (k0, u1), (u1, u1), (u1, u2), (u2, u2), (k0, w1), (u1, w1), (u1, w2), (u2, w2),
        )
        totals = [t + a * b for t, (a, b) in zip(totals, pairs)]
    for i, t in enumerate(totals):
        sums_ref[i : i + 1] = jnp.sum(t[0] + t[1], axis=0, keepdims=True)
    sums_ref[14:16] = jnp.zeros((2, 128), F32)


def krylov(keep, *args):
    return kernel_call(
        krylov_kernel,
        "krylov",
        (of((3, 25, 2, 24, 128)),) + (of((25, 2, 24, 128)),) * 4 + (of((16, 128)),),
        [(4, 2, 2, 24, 128)],
        (keep, *args),
        [smem()] + [vmem()] * 5,
    )


def steps_from(gram, energy, apply_once):
    def form(a, table):
        total = None
        for i, p in enumerate(a):
            for j, q in enumerate(a):
                if p is not None and q is not None:
                    term = p * q * table[i + j]
                    total = term if total is None else total + term
        return total

    def ratio(a, b):
        return jnp.where(b > 0.0, a / jnp.where(b > 0.0, b, 1.0), 0.0)

    one, zero = jnp.ones_like(gram[0]), jnp.zeros_like(gram[0])
    residual, direction, answer = [one], [one], [zero] * 3
    norm = gram[0]
    for step in range(3):
        alpha = ratio(norm, form(direction, energy))
        for i, p in enumerate(direction):
            answer[i] = answer[i] + alpha * p
        if step == 2:
            return answer
        image = apply_once(direction, zero)
        residual = [a - alpha * b for a, b in zip(residual + [zero], image)]
        norm_next = form(residual, gram)
        direction = [a + ratio(norm_next, norm) * b for a, b in zip(residual, direction + [zero])]
        norm = norm_next


def coefficients(m):
    power = steps_from(m[0:5], m[1:6], lambda a, zero: [zero] + a)
    shifted = steps_from(
        [m[0]] + m[6:10],
        [m[1]] + m[10:14],
        lambda a, zero: [p - q for p, q in zip(a + [zero], [zero] + a)],
    )
    turned = [shifted[0] + shifted[1] + shifted[2], -shifted[1] - 2.0 * shifted[2], shifted[2]]
    smooth = m[1] < 0.3 * m[0]
    return [jnp.where(smooth, a, b) * (1.0 / 6.0) for a, b in zip(power, turned)]


def interpolate_kernel(tag_ref, fluid_ref, *refs):
    *fields, out_ref, proj = refs
    for x in range(CX + 1):
        fluid = fluid_ref[x + 4, :, 8:24]
        channel = 0
        for ref in fields:
            if len(ref.shape) == 5:
                parts = [fluid * ref[d, x + 4, :, 8:24] for d in range(3)]
            else:
                p, scale = ref[x + 4], -0.5 * fluid
                inner = p[:, 8:24]
                parts = [
                    scale * (ref[x + 5, :, 8:24] - ref[x + 3, :, 8:24]),
                    scale * (y_shift(p, -1) - y_shift(p, 1))[:, 8:24],
                    scale * (z_ahead(inner) - z_behind(inner)),
                ]
            for part in parts:
                for j, rows in enumerate((part[:, 0:8], y_shift(part, -1)[:, 0:8])):
                    proj[x, channel, j, 0] = rows
                    proj[x, channel, j, 1] = z_ahead(rows)
                channel += 1
    for x in range(CX):
        code = tag_ref[0, 2 * x : 2 * x + 2] >> 15
        fx, fy, fz = fractions(code)
        wx, wy, wz = (1.0 - fx, fx), (1.0 - fy, fy), (1.0 - fz, fz)
        w = {(i, j, k): wx[i] * wy[j] * wz[k] for i in (0, 1) for j in (0, 1) for k in (0, 1)}
        for c in range(6):
            result = None
            for (i, j, k), weight in w.items():
                term = weight * proj[x + i, c, j, k]
                result = term if result is None else result + term
            out_ref[c, 2 * x : 2 * x + 2] = result


def interpolate(*args):
    return kernel_call(
        interpolate_kernel,
        "interpolate",
        (of((6, TILES, 8, 128)),),
        [(CX + 1, 6, 2, 2, 2, 8, 128)],
        args,
        flops=10**7,
    )[0]


def finish_kernel(
    sums_ref, k0_ref, k1_ref, k2_ref, first_ref, second_ref, lane_ref, sub_ref, swap_ref, pressure_ref, out_ref
):
    total = jnp.sum(sums_ref[...], axis=1, keepdims=True)
    c = coefficients([jnp.broadcast_to(total[i : i + 1], (8, 128)) for i in range(14)])
    for i in range(TILES):
        for d in range(3):
            out_ref[d, i] = (
                first_ref[d, i]
                + c[0] * first_ref[3 + d, i]
                + c[1] * second_ref[d, i]
                + c[2] * second_ref[3 + d, i]
            )
    follow_plan([(out_ref, d) for d in range(3)], lane_ref, sub_ref, swap_ref)
    for x in range(CX):
        for h in range(2):
            k0, k1, k2 = [ref[x + 4, h, 8:16] for ref in (k0_ref, k1_ref, k2_ref)]
            pressure_ref[x, :, 128 * h : 128 * h + 128] = c[0] * k0 + c[1] * k1 + c[2] * k2


def finish(*args):
    return kernel_call(finish_kernel, "finish", (of((CX, CY, 256)), of((3, TILES, 8, 128))), [], args)


def neighbours(up, down, axis):
    count = lax.axis_size(axis)
    odd = lax.axis_index(axis) % 2 == 1
    high_rows, low_rows = down.shape[0], up.shape[0]
    up = jnp.concatenate([up, jnp.zeros((high_rows - low_rows, 128), F32)])
    arrived = []
    for first, slab in ((0, jnp.where(odd, down, up)), (1, jnp.where(odd, up, down))):
        pairs = [(i, i + 1) for i in range(first, count - 1, 2)]
        arrived.append(lax.ppermute(slab, axis, pairs + [(b, a) for a, b in pairs]))
    return jnp.where(odd, arrived[0], arrived[1]), jnp.where(odd, arrived[1], arrived[0])


def summed(sums, axis):
    count = lax.axis_size(axis)
    parts = [sums]
    for shift in range(1, count):
        swaps = [(i, i ^ shift) for i in range(count)]
        if max(b for _, b in swaps) >= count:
            swaps = [(i, (i + shift) % count) for i in range(count)]
        parts.append(lax.ppermute(sums, axis, swaps))
    return functools.reduce(jnp.add, parts)


def local(cell_index, offset_code, particle_state, fluid_flags):
    places = [(axis, lax.axis_index(axis), lax.axis_size(axis)) for axis in ("gx", "gy")]
    keep = jnp.stack([(at + 1 < size).astype(F32) for _, at, size in places])
    cells, tag = to_cells(offset_code, particle_state, *cell_rows(cell_index.reshape(256, 128)))
    grid, rim, up, down = deposit(cells, tag, fluid_flags)
    low, high = neighbours(up, down, "gy")
    plan = particle_plan(tag.reshape(256, 128))
    near, edge, flags, up, down = widen(keep, grid, rim, low, high, fluid_flags, plan[1])
    low, high = neighbours(up, down, "gx")
    vel, fluid, k0, k1, k2, sums = krylov(keep, near, edge, flags, low, high)
    first = interpolate(tag, fluid, vel, k0)
    sums, first, tag = lax.optimization_barrier((summed(sums, "gx"), first, tag))
    second = interpolate(tag, fluid, k1, k2)
    pressure, result = finish(summed(sums, "gy"), k0, k1, k2, first, second, *plan)
    return pressure, result.reshape(1, 3, CELLS)


def solution(mesh):
    return jax.shard_map(
        local,
        mesh=mesh,
        in_specs=(
            P(("groups", "gx", "gy"), None),
            P(("groups", "gx", "gy"), None),
            P(("groups", "gx", "gy"), None, None),
            P(("groups", "gx"), "gy", None),
        ),
        out_specs=(P(("groups", "gx"), "gy", None), P(("groups", "gx", "gy"), None, None)),
        check_vma=False,
    )
```
